32 devices in a mesh: dp: 16 (over z, y, x), tensor: 2 (over core).
Axes of the slice: x: 2, y: 2, z: 4, core: 2. Of those that a mesh axis runs over, the one named last changes fastest.
Arguments:
- hidden_in: bfloat16 [4096, 2560], P(('dp', 'tensor')), may hold values from -6 to 6
- prefix_len: int32 [16], P('dp'), may hold values from 25 to 128
- attn_gain: bfloat16 [2560], P(('dp', 'tensor')), may hold values from 0.25 to 1.75
- q_down: bfloat16 [2560, 768], P(('dp', 'tensor')), may hold values from -0.125 to 0.125
- q_gain: bfloat16 [768], P(('dp', 'tensor')), may hold values from 0.25 to 1.75
- kv_down: bfloat16 [2560, 288], P(('dp', 'tensor')), may hold values from -0.125 to 0.125
- kv_gain: bfloat16 [256], P(('dp', 'tensor')), may hold values from 0.25 to 1.75
- q_up: bfloat16 [768, 3840], P('dp', 'tensor'), may hold values from -0.21875 to 0.21875
- kv_up: bfloat16 [256, 5120], P('dp', 'tensor'), may hold values from -0.375 to 0.375
- o_proj: bfloat16 [2560, 2560], P('tensor', 'dp'), may hold values from -1.25 to 1.25
- mlp_gain: bfloat16 [2560], P(('dp', 'tensor')), may hold values from 0.25 to 1.75
- w_gate: bfloat16 [2560, 6400], P('dp', 'tensor'), may hold values from -0.125 to 0.125
- w_up: bfloat16 [2560, 6400], P('dp', 'tensor'), may hold values from -0.125 to 0.125
- w_down: bfloat16 [6400, 2560], P('tensor', 'dp'), may hold values from -0.4375 to 0.4375
- cotangent: bfloat16 [4096, 2560], P(('dp', 'tensor')), may hold values from -6 to 6
Outputs:
- layer_out: bfloat16 [4096, 2560], P(('dp', 'tensor'))
- grad_input: float32 [4096, 2560], P(('dp', 'tensor'))
- grad_attn_gain: float32 [2560], P(('dp', 'tensor'))
- grad_q_down: float32 [2560, 768], P(('dp', 'tensor'))
- grad_q_gain: float32 [768], P(('dp', 'tensor'))
- grad_kv_down: float32 [2560, 288], P(('dp', 'tensor'))
- grad_kv_gain: float32 [256], P(('dp', 'tensor'))
- grad_q_up: float32 [768, 3840], P('dp', 'tensor')
- grad_kv_up: float32 [256, 5120], P('dp', 'tensor')
- grad_o_proj: float32 [2560, 2560], P('tensor', 'dp')
- grad_mlp_gain: float32 [2560], P(('dp', 'tensor'))
- grad_w_gate: float32 [2560, 6400], P('dp', 'tensor')
- grad_w_up: float32 [2560, 6400], P('dp', 'tensor')
- grad_w_down: float32 [6400, 2560], P('tensor', 'dp')
The draws below stay inside these ranges and needn't reach their ends.
Inputs may be any that keep to these rules, and one draw needn't show every extreme that they name: prefix_len of a sequence is the number of its leading tokens that see one another in both directions.
All inputs are finite; a program needn't handle non-finite values.
Results may differ from the reference program's by a relative error of at most 0.022.
Values may be sent and summed in bfloat16 or wider, within the bound.
No kernel may reach another device: no remote copies, remote signals or barrier semaphores. Data moves between devices by JAX's collectives and lax.ppermute only.
A program may use at most 320 MiB of HBM per device.

```python
import math
import jax
import jax.numpy as jnp
from jax import lax

D = 2560
H = 40
NOPE = 64
ROPE = 32
VD = 64
QR = 768
KR = 256
FF = 6400
LENGTH = 256
TOKENS = 4096
N_DP = 16


def with_ends(drawn, rng, low, top_value):
    shape = drawn.shape
    place = [jax.random.randint(jax.random.fold_in(rng, axis), (), 0, shape[axis]) for axis in range(len(shape))]
    drawn = drawn.at[tuple(place)].set(low)
    longest = shape.index(max(shape))
    place[longest] = (place[longest] + 1) % shape[longest]
    return drawn.at[tuple(place)].set(top_value)


def with_spikes(entries, key, source, target, blocks, factor):
    def block_of(dim):
        return (jnp.arange(entries.shape[dim]) // (entries.shape[dim] // blocks)).reshape((-1,) + (1,) * (entries.ndim - 1 - dim))

    one_side = jax.random.permutation(key, blocks)[block_of(target)]
    other_side = (block_of(target) + blocks // 2) % blocks
    return jnp.where((block_of(source) == one_side) | (block_of(source) == other_side), factor * entries, entries)


def block_scale(rng, shape, split, low, high):
    def one(axis_at, blocks):
        steps = jax.random.uniform(jax.random.fold_in(jax.random.fold_in(rng, 6), axis_at), (blocks,), jnp.float32, low / len(split), high / len(split))
        return jnp.repeat(jnp.exp(steps), shape[axis_at] // blocks).reshape((-1,) + (1,) * (len(shape) - axis_at - 1))

    loudness = one(*split[0])
    for cut in split[1:]:
        loudness = loudness * one(*cut)
    return loudness


def bell_draw(rng, extent, deviation, limit, cuts=(), held_as=jnp.bfloat16):
    level = block_scale(rng, extent, cuts, -0.22, 0.18) if cuts else 1.0
    drawn = jax.random.normal(rng, extent, jnp.float32) * deviation * level
    return jnp.minimum(jnp.maximum(drawn, -limit), limit).astype(held_as)


def bell_draw_with(key, extent, scale, reach, split, heavy, held_as=jnp.bfloat16):
    result = scale * jax.random.normal(key, extent, jnp.float32)
    if split:
        result = result * block_scale(key, extent, split, -0.22, 0.18)
    return jnp.clip(with_spikes(result, jax.random.fold_in(key, 3), *heavy), -reach, reach).astype(held_as)


def setup_inputs(seed: int = 0) -> dict:
    arg_keys = jax.random.split(jax.random.key(seed), 16)
    return {
        "hidden_in": bell_draw_with(arg_keys[0], (TOKENS, D), 1.0, 6.0, ((0, 32),), (0, 1, 32, 2.75)),
        "prefix_len": with_ends(jax.random.randint(arg_keys[1], (N_DP,), LENGTH // 10, LENGTH // 2 + 1), jax.random.fold_in(arg_keys[1], 1), LENGTH // 10, (LENGTH // 2 + 1) - 1).astype(jnp.int32),
        "attn_gain": jnp.clip(1.0 + 0.15 * jax.random.normal(arg_keys[2], (D,), jnp.float32), 0.25, 1.75).astype(jnp.bfloat16),
        "q_down": bell_draw(arg_keys[3], (D, QR), D ** -0.5, 0.125, ((0, 32),)),
        "q_gain": jnp.clip(1.0 + 0.15 * jax.random.normal(arg_keys[4], (QR,), jnp.float32), 0.25, 1.75).astype(jnp.bfloat16),
        "kv_down": bell_draw(arg_keys[5], (D, KR + ROPE), D ** -0.5, 0.125, ((0, 32),)),
        "kv_gain": jnp.clip(1.0 + 0.15 * jax.random.normal(arg_keys[6], (KR,), jnp.float32), 0.25, 1.75).astype(jnp.bfloat16),
        "q_up": bell_draw(arg_keys[7], (QR, H * (NOPE + ROPE)), QR ** -0.5, 0.21875, ((0, 16), (1, 2))),
        "kv_up": bell_draw(arg_keys[8], (KR, H * (NOPE + VD)), KR ** -0.5, 0.375, ((0, 16), (1, 2))),
        "o_proj": bell_draw(arg_keys[9], (H * VD, D), (max(H * VD // 128, 8)) ** -0.5, 1.25, ((0, 2), (1, 16))),
        "mlp_gain": jnp.clip(1.0 + 0.15 * jax.random.normal(arg_keys[10], (D,), jnp.float32), 0.25, 1.75).astype(jnp.bfloat16),
        "w_gate": bell_draw(arg_keys[11], (D, FF), D ** -0.5, 0.125, ((0, 16), (1, 2))),
        "w_up": bell_draw(arg_keys[12], (D, FF), D ** -0.5, 0.125, ((0, 16), (1, 2))),
        "w_down": bell_draw(arg_keys[13], (FF, D), (max(FF // 32, 8)) ** -0.5, 0.4375, ((0, 2), (1, 16))),
        "cotangent": bell_draw_with(arg_keys[14], (TOKENS, D), 1.0, 6.0, ((0, 32),), (0, 1, 32, 2.75)),
    }


EPS = 1e-05
RESID = 1.4 / math.sqrt(62.0)
THETA = 10000.0
NEG_FILL = -1e+30
HIGH = lax.Precision.HIGHEST

@jax.custom_vjp
def low(v):
    return lax.optimization_barrier(v.astype(jnp.bfloat16)).astype(jnp.float32)

@jax.custom_vjp
def low_back(v):
    return v

def low_keep(v):
    return (low(v), None)

def low_pass(kept, grad):
    return (grad,)

def back_keep(v):
    return (v, None)

def back_low(kept, grad):
    return (low(grad),)
low.defvjp(low_keep, low_pass)
low_back.defvjp(back_keep, back_low)

def norm_apply(values, gain):
    inverse = lax.rsqrt(lax.optimization_barrier(jnp.mean(values * values, axis=-1, keepdims=True)) + EPS)
    return values * inverse * gain

def rotate(values, positions):
    width_half = values.shape[-1] // 2
    frequency = THETA ** (-2.0 * jnp.arange(width_half, dtype=jnp.float32) / values.shape[-1])
    angles = positions.astype(jnp.float32)[:, None] * frequency[None, :]
    extra_dims = (1,) * (values.ndim - 2)
    cosine = jnp.cos(angles).reshape(angles.shape[:1] + extra_dims + angles.shape[1:])
    sine = jnp.sin(angles).reshape(angles.shape[:1] + extra_dims + angles.shape[1:])
    lower_part = values[..., :width_half]
    upper_part = values[..., width_half:]
    return jnp.concatenate([lower_part * cosine - upper_part * sine, upper_part * cosine + lower_part * sine], axis=-1)

def swish(values):
    return values / (1.0 + jnp.exp(-values))

def matmul_hi(left, right):
    return jnp.dot(left, right, precision=HIGH, preferred_element_type=jnp.float32)

def one_sequence(resid_in, prefix_one, weights):
    gain_attn, qdown_weight, gain_q, kvdown_weight, gain_kv, q_weight, kv_weight, out_weight, gain_mlp, gate_weight, upper_weight, down_weight = weights
    seq_length = resid_in.shape[0]
    positions = jnp.arange(seq_length, dtype=jnp.int32)
    x_normed = low(norm_apply(resid_in, gain_attn))
    q_latent = low_back(matmul_hi(x_normed, qdown_weight))
    q_normed = low(norm_apply(q_latent, gain_q))
    kv_latent = low_back(matmul_hi(x_normed, kvdown_weight))
    kv_normed = low(norm_apply(kv_latent[:, :KR], gain_kv))
    k_rotary = low(rotate(kv_latent[:, KR:], positions))
    query = low_back(matmul_hi(q_normed, q_weight)).reshape(seq_length, H, NOPE + ROPE)
    query_full = low(jnp.concatenate([query[..., :NOPE], rotate(query[..., NOPE:], positions)], axis=-1))
    key_value = low_back(matmul_hi(kv_normed, kv_weight)).reshape(seq_length, H, NOPE + VD)
    rotary_heads = jnp.broadcast_to(k_rotary[:, None, :], (seq_length, H, ROPE))
    key_full = low(jnp.concatenate([key_value[..., :NOPE], rotary_heads], axis=-1))
    values_low = low(key_value[..., NOPE:])
    raw_scores = low_back(jnp.einsum('qhd,khd->hqk', query_full, key_full, precision=HIGH))
    scaled = raw_scores * (NOPE + ROPE) ** (-0.5)
    row_pos = positions[:, None]
    col_pos = positions[None, :]
    visible = (col_pos <= row_pos) | (col_pos < prefix_one)
    masked = jnp.where(visible[None], scaled, NEG_FILL)
    row_peak = lax.optimization_barrier(jnp.max(masked, axis=-1, keepdims=True))
    exp_scores = jnp.exp(masked - row_peak)
    attn_probs = exp_scores / lax.optimization_barrier(jnp.sum(exp_scores, axis=-1, keepdims=True))
    heads_out = jnp.einsum('hqk,khd->qhd', low(attn_probs), values_low, precision=HIGH)
    heads_low = low(low_back(heads_out)).reshape(seq_length, H * VD)
    attn_out = low_back(matmul_hi(heads_low, out_weight))
    mid_resid = resid_in + RESID * attn_out
    mlp_normed = low(norm_apply(mid_resid, gain_mlp))
    gate_proj = low_back(matmul_hi(mlp_normed, gate_weight))
    up_proj = low_back(matmul_hi(mlp_normed, upper_weight))
    act_low = low(swish(gate_proj) * up_proj)
    mlp_out = low_back(matmul_hi(act_low, down_weight))
    return mid_resid + RESID * mlp_out

def reference(hidden_in, prefix_len, attn_gain, q_down, q_gain, kv_down, kv_gain, q_up, kv_up, o_proj, mlp_gain, w_gate, w_up, w_down, cotangent):
    group_size = math.gcd(N_DP, max(1, 2048 // LENGTH))
    weights = tuple((item.astype(jnp.float32) for item in (attn_gain, q_down, q_gain, kv_down, kv_gain, q_up, kv_up, o_proj, mlp_gain, w_gate, w_up, w_down)))
    inputs = hidden_in.astype(jnp.float32).reshape(N_DP // group_size, group_size, LENGTH, D)
    prefixes = prefix_len.astype(jnp.int32).reshape(N_DP // group_size, group_size)
    block_fn = jax.checkpoint(jax.vmap(one_sequence, in_axes=(0, 0, None)))

    def forward(inputs, weights):

        def scan_step(carry, pieces):
            return (carry, block_fn(pieces[0], pieces[1], weights))
        _, outputs = lax.scan(scan_step, jnp.zeros((), jnp.float32), (inputs, prefixes))
        return outputs
    outputs, pullback = jax.vjp(forward, inputs, weights)
    grad_in, grad_w = pullback(cotangent.astype(jnp.float32).reshape(inputs.shape))
    layer_out = outputs.reshape(TOKENS, D).astype(jnp.bfloat16)
    grad_input = grad_in.reshape(TOKENS, D)
    return (layer_out, grad_input, grad_w[0], grad_w[1], grad_w[2], grad_w[3], grad_w[4], grad_w[5], grad_w[6], grad_w[7], grad_w[8], grad_w[9], grad_w[10], grad_w[11])
```

```python
from functools import partial
import math

import jax
import jax.numpy as jnp
from jax import lax
from jax.sharding import PartitionSpec as P

NOPE = 64
ROPE = 32
VD = 64
KR = 256
COLUMN = 4


EPS = 1e-05
RESID = 1.4 / math.sqrt(62.0)
THETA = 10000.0
NEG_FILL = -1e30


def norm_apply(values, gain):
    inverse = lax.rsqrt(jnp.mean(values * values, axis=-1, keepdims=True) + EPS)
    return values * inverse * gain


def rotate(values, positions):
    width_half = values.shape[-1] // 2
    frequency = THETA ** (-2.0 * jnp.arange(width_half, dtype=jnp.float32) / values.shape[-1])
    angles = positions.astype(jnp.float32)[:, None] * frequency[None, :]
    extra_dims = (1,) * (values.ndim - 2)
    cosine = jnp.cos(angles).reshape(angles.shape[:1] + extra_dims + angles.shape[1:])
    sine = jnp.sin(angles).reshape(angles.shape[:1] + extra_dims + angles.shape[1:])
    lower_part = values[..., :width_half]
    upper_part = values[..., width_half:]
    return jnp.concatenate(
        [lower_part * cosine - upper_part * sine, upper_part * cosine + lower_part * sine], axis=-1
    )


def rotate_back(values, positions, grads):
    _, pullback = jax.vjp(partial(rotate, positions=positions), values)
    return pullback(grads)[0]


def swish(values):
    return values / (1.0 + jnp.exp(-values))


def gated(gate_in, upper_in):
    return swish(gate_in) * upper_in


def plain_mul(left, right):
    return jnp.dot(left, right, preferred_element_type=jnp.float32)


def mul_trans(left, right):
    return lax.dot_general(
        left, right, (((1,), (1,)), ((), ())), preferred_element_type=jnp.float32
    )


def trans_mul(left, right):
    return lax.dot_general(
        left, right, (((0,), (0,)), ((), ())), preferred_element_type=jnp.float32
    )


def split_heads(values, groups):
    seq_length, heads_local, width = values.shape
    return jnp.moveaxis(values.reshape(seq_length, groups, heads_local // groups, width), 1, 0)


def join_heads(values):
    groups, seq_length, group_heads, width = values.shape
    return jnp.moveaxis(values, 0, 1).reshape(seq_length, groups * group_heads, width)


def masked_scores(query_part, key_part, visible, scale):
    scores = (
        jnp.einsum("qhd,khd->hqk", query_part, key_part, preferred_element_type=jnp.float32) * scale
    )
    return jnp.where(visible[None], scores, NEG_FILL)


def attend_forward(pieces, visible, scale):
    query_part, key_part, value_part = pieces
    masked = masked_scores(query_part, key_part, visible, scale)
    row_peak = jnp.max(masked, axis=-1, keepdims=True)
    exp_scores = jnp.exp(masked - row_peak)
    row_total = jnp.sum(exp_scores, axis=-1, keepdims=True)
    attn_probs = exp_scores / row_total
    heads_part = jnp.einsum(
        "hqk,khd->qhd",
        attn_probs.astype(jnp.bfloat16),
        value_part,
        preferred_element_type=jnp.float32,
    )
    return (heads_part, row_peak + jnp.log(row_total))


def attend_backward(pieces, visible, scale):
    query_part, key_part, value_part, log_total, d_heads_part = pieces
    masked = masked_scores(query_part, key_part, visible, scale)
    attn_probs = jnp.exp(masked - log_total)
    probs_low = attn_probs.astype(jnp.bfloat16)
    d_probs = jnp.einsum(
        "qhd,khd->hqk", d_heads_part, value_part, preferred_element_type=jnp.float32
    )
    d_values = jnp.einsum(
        "hqk,qhd->khd", probs_low, d_heads_part, preferred_element_type=jnp.float32
    )
    row_dot = jnp.sum(attn_probs * d_probs, axis=-1, keepdims=True)
    d_scores = (attn_probs * (d_probs - row_dot) * scale).astype(jnp.bfloat16)
    d_query = jnp.einsum("hqk,khd->qhd", d_scores, key_part, preferred_element_type=jnp.float32)
    d_key = jnp.einsum("hqk,qhd->khd", d_scores, query_part, preferred_element_type=jnp.float32)
    return (d_query, d_key, d_values)


def low(values):
    return values.astype(jnp.bfloat16)


def wide(values):
    return values.astype(jnp.float32)


def core_swap(values):
    return lax.ppermute(values, "tensor", [(0, 1), (1, 0)])


def hop(values, place_of):
    count = lax.axis_size("dp")
    return lax.ppermute(values, "dp", [(place, place_of(place)) for place in range(count)])


def turn(values, steps):
    count = lax.axis_size("dp")
    rest = count // COLUMN
    return hop(values, lambda place: (place + steps * rest) % count)


def flip(values, mask):
    return hop(values, lambda place: place ^ mask)


def places():
    rest = lax.axis_size("dp") // COLUMN
    place = lax.axis_index("dp")
    return place // rest, place % rest, rest


def top_bit(mask):
    return 1 << (mask.bit_length() - 1)


def low_bit(mask):
    return mask & -mask


def by_count(rest):
    return sorted(range(1, rest), key=lambda mask: bin(mask).count("1"))


def spread_rest(values):
    _, rest_place, rest = places()
    half = COLUMN // 2
    known = {0: (values[:half], values[half:])}
    for mask in by_count(rest):
        if mask == low_bit(mask):
            got = flip(values, mask)
            known[mask] = (got[:half], got[half:])
        else:
            first, last = top_bit(mask), low_bit(mask)
            known[mask] = (
                flip(known[mask ^ first][0], first),
                flip(known[mask ^ last][1], last),
            )
    whole = jnp.zeros((COLUMN, rest) + values.shape[1:], values.dtype)
    for mask, parts in known.items():
        for start, part in zip((0, half), parts):
            whole = lax.dynamic_update_slice(
                whole,
                part[:, None],
                (start, rest_place ^ mask) + (0,) * (values.ndim - 1),
            )
    return whole


def reduce_rest(values):
    _, rest_place, rest = places()
    half = COLUMN // 2
    parts = {}
    for mask in range(rest):
        block = lax.dynamic_index_in_dim(values, rest_place ^ mask, axis=1, keepdims=False)
        parts[mask] = [block[:half], block[half:]]
    for mask in reversed(by_count(rest)):
        if mask == low_bit(mask):
            got = flip(low(jnp.concatenate(parts[mask])), mask)
            parts[0][0] += wide(got[:half])
            parts[0][1] += wide(got[half:])
        else:
            first, last = top_bit(mask), low_bit(mask)
            parts[mask ^ first][0] += wide(flip(low(parts[mask][0]), first))
            parts[mask ^ last][1] += wide(flip(low(parts[mask][1]), last))
    return jnp.concatenate(parts[0])


def place_column(blocks):
    column_place, _, _ = places()
    stacked = jnp.zeros((COLUMN,) + blocks[0].shape, blocks[0].dtype)
    for step, block in enumerate(blocks):
        stacked = lax.dynamic_update_slice(
            stacked, block[None], ((column_place - step) % COLUMN,) + (0,) * block.ndim
        )
    return stacked


def exchange_column(values):
    column_place, _, _ = places()
    blocks = []
    for step in range(COLUMN):
        block = lax.dynamic_index_in_dim(
            values, (column_place + step) % COLUMN, axis=0, keepdims=False
        )
        blocks.append(turn(block, step) if step else block)
    return blocks


def gather_dp(values):
    blocks = [values] + [turn(values, step) for step in range(1, COLUMN)]
    whole = spread_rest(place_column(blocks))
    return whole.reshape((-1,) + values.shape)


def reduce_dp(values):
    rest = lax.axis_size("dp") // COLUMN
    values = values.reshape((COLUMN, rest, -1) + values.shape[1:])
    partial_sum = reduce_rest(values)
    column_place, _, _ = places()
    total = lax.dynamic_index_in_dim(partial_sum, column_place, axis=0, keepdims=False)
    moving = low(partial_sum)
    for step in range(1, COLUMN):
        block = lax.dynamic_index_in_dim(
            moving, (column_place + step) % COLUMN, axis=0, keepdims=False
        )
        total = total + wide(turn(block, step))
    return total


def gather_units(weight):
    rows, units = weight.shape
    pieces = jnp.moveaxis(weight.reshape(rows, COLUMN, units // COLUMN), 1, 0)
    whole = spread_rest(place_column(exchange_column(pieces)))
    return whole.reshape(-1, units // COLUMN)


def reduce_units(grad):
    rest = lax.axis_size("dp") // COLUMN
    units = grad.shape[1]
    partial_sum = low(reduce_rest(grad.reshape(COLUMN, rest, -1, units)))
    pieces = place_column(exchange_column(partial_sum))
    return wide(jnp.moveaxis(pieces, 0, 1).reshape(-1, COLUMN * units))


def gather_tokens(values):
    own = jnp.stack([values] + [turn(values, step) for step in range(1, COLUMN)])
    return jnp.stack([own, core_swap(own)], axis=1).reshape(-1, values.shape[1])


def return_tokens(values, rows):
    values = values.reshape(COLUMN, 2, rows, -1)
    chip_sum = values[:, 0] + wide(core_swap(low(values[:, 1])))
    total = chip_sum[0]
    moving = low(chip_sum)
    for step in range(1, COLUMN):
        total = total + wide(turn(moving[step], -step))
    return total


def pair_tokens(values):
    return jnp.concatenate([values, core_swap(values)], axis=0)


def split_pair(values):
    rows = values.shape[0] // 2
    return values[:rows] + wide(core_swap(low(values[rows:])))


def body(
    hidden_in,
    prefix_len,
    attn_gain,
    q_down,
    q_gain,
    kv_down,
    kv_gain,
    q_up,
    kv_up,
    o_proj,
    mlp_gain,
    w_gate,
    w_up,
    w_down,
    cotangent,
):
    tensor_count = lax.axis_size("tensor")
    tensor_rank = lax.axis_index("tensor")
    dp_count = lax.axis_size("dp")
    own_rows, width = hidden_in.shape
    seq_length = own_rows * tensor_count
    q_rank = q_down.shape[1]
    down_rows = q_down.shape[0]
    q_share = q_gain.shape[0]
    kv_share = kv_gain.shape[0]
    head_qk = NOPE + ROPE
    heads_local = q_up.shape[1] // head_qk
    groups = heads_local // math.gcd(heads_local, 4)
    scale = head_qk ** (-0.5)

    def column_of(gain):
        return jnp.pad(gain, (0, down_rows - gain.shape[0]))[:, None]

    down_columns = q_rank + kv_down.shape[1]
    packed = jnp.concatenate(
        [q_down, kv_down, column_of(attn_gain), column_of(mlp_gain), column_of(q_gain), column_of(kv_gain)],
        axis=1,
    )
    core_packed = gather_dp(packed)
    other_packed = core_swap(core_packed)
    is_first = tensor_rank == 0
    all_packed = jnp.stack(
        [
            jnp.where(is_first, core_packed, other_packed),
            jnp.where(is_first, other_packed, core_packed),
        ],
        axis=1,
    )
    down_weight = all_packed.reshape(width, -1)[:, :down_columns]
    gains = wide(jnp.moveaxis(all_packed[..., down_columns:], -1, 0))
    gain_attn = gains[0].reshape(width)
    gain_mlp = gains[1].reshape(width)
    gain_q = gains[2][..., :q_share].reshape(q_rank)
    gain_kv = gains[3][..., :kv_share].reshape(KR)

    q_weight = gather_dp(q_up).reshape(q_rank, -1)
    kv_weight = gather_dp(kv_up).reshape(KR, -1)
    out_trans = gather_dp(o_proj.T).reshape(width, -1)
    gate_weight = gather_units(w_gate)
    upper_weight = gather_units(w_up)
    down_trans = gather_units(w_down.T)

    resid_in = hidden_in.astype(jnp.float32)
    x_normed = norm_apply(resid_in, gain_attn).astype(jnp.bfloat16)
    latents = plain_mul(x_normed, down_weight)
    q_latent = latents[:, :q_rank]
    kv_latent = latents[:, q_rank:]
    q_normed = norm_apply(q_latent, gain_q).astype(jnp.bfloat16)
    own_pos = tensor_rank * own_rows + jnp.arange(own_rows, dtype=jnp.int32)
    other_pos = (1 - tensor_rank) * own_rows + jnp.arange(own_rows, dtype=jnp.int32)
    kv_normed = norm_apply(kv_latent[:, :KR], gain_kv).astype(jnp.bfloat16)
    k_rotary = rotate(kv_latent[:, KR:], own_pos).astype(jnp.bfloat16)
    q_seq = pair_tokens(q_normed)
    kv_seq = pair_tokens(kv_normed)
    rot_seq = pair_tokens(k_rotary)
    positions = jnp.concatenate([own_pos, other_pos])
    query = plain_mul(q_seq, q_weight).reshape(seq_length, heads_local, head_qk)
    q_rot_in = query[..., NOPE:]
    query_full = jnp.concatenate([query[..., :NOPE], rotate(q_rot_in, positions)], axis=-1).astype(
        jnp.bfloat16
    )
    key_value = plain_mul(kv_seq, kv_weight).reshape(seq_length, heads_local, NOPE + VD)
    rotary_heads = jnp.broadcast_to(
        rot_seq.astype(jnp.float32)[:, None, :], (seq_length, heads_local, ROPE)
    )
    key_full = jnp.concatenate([key_value[..., :NOPE], rotary_heads], axis=-1).astype(jnp.bfloat16)
    values_low = key_value[..., NOPE:].astype(jnp.bfloat16)
    row_pos = positions[:, None]
    col_pos = positions[None, :]
    visible = (col_pos <= row_pos) | (col_pos < prefix_len[0])
    query_groups = split_heads(query_full, groups)
    key_groups = split_heads(key_full, groups)
    value_groups = split_heads(values_low, groups)
    heads_groups, log_totals = lax.map(
        partial(attend_forward, visible=visible, scale=scale),
        (query_groups, key_groups, value_groups),
    )
    heads_low = join_heads(heads_groups).astype(jnp.bfloat16).reshape(seq_length, heads_local * VD)
    attn_own = split_pair(mul_trans(heads_low, out_trans))
    mid_resid = resid_in + RESID * attn_own
    mlp_normed = norm_apply(mid_resid, gain_mlp).astype(jnp.bfloat16)

    grad_out = cotangent.astype(jnp.float32)
    mlp_back = gather_tokens((RESID * grad_out).astype(jnp.bfloat16))
    mlp_seq = gather_tokens(mlp_normed)
    gate_proj = plain_mul(mlp_seq, gate_weight)
    up_proj = plain_mul(mlp_seq, upper_weight)
    act_low = gated(gate_proj, up_proj).astype(jnp.bfloat16)
    d_act = plain_mul(mlp_back, down_trans)
    _, act_pullback = jax.vjp(gated, gate_proj, up_proj)
    d_gate, d_upper = act_pullback(d_act)
    d_gate_low = d_gate.astype(jnp.bfloat16)
    d_upper_low = d_upper.astype(jnp.bfloat16)
    d_mlp_terms = mul_trans(d_gate_low, gate_weight) + mul_trans(d_upper_low, upper_weight)
    d_mlp_own = return_tokens(d_mlp_terms, own_rows)
    mlp_own = return_tokens(mul_trans(act_low, down_trans), own_rows)
    layer_out = (mid_resid + RESID * mlp_own).astype(jnp.bfloat16)
    gate_shard = reduce_units(trans_mul(mlp_seq, d_gate_low))
    upper_shard = reduce_units(trans_mul(mlp_seq, d_upper_low))
    down_shard = reduce_units(trans_mul(mlp_back, act_low)).T

    _, mlp_norm_back = jax.vjp(norm_apply, mid_resid, gain_mlp)
    d_mid_norm, d_gain_mlp = mlp_norm_back(d_mlp_own)
    d_mid = grad_out + d_mid_norm
    attn_back = pair_tokens((RESID * d_mid).astype(jnp.bfloat16))
    d_heads = plain_mul(attn_back, out_trans).astype(jnp.bfloat16).reshape(
        seq_length, heads_local, VD
    )
    out_shard = reduce_dp(trans_mul(attn_back, heads_low)).T
    d_query_groups, d_key_groups, d_value_groups = lax.map(
        partial(attend_backward, visible=visible, scale=scale),
        (query_groups, key_groups, value_groups, log_totals, split_heads(d_heads, groups)),
    )
    d_query = join_heads(d_query_groups)
    d_key = join_heads(d_key_groups)
    d_values = join_heads(d_value_groups)
    d_query_rot = rotate_back(q_rot_in, positions, d_query[..., NOPE:])
    d_query_low = (
        jnp.concatenate([d_query[..., :NOPE], d_query_rot], axis=-1)
        .astype(jnp.bfloat16)
        .reshape(seq_length, heads_local * head_qk)
    )
    d_kv_low = (
        jnp.concatenate([d_key[..., :NOPE], d_values], axis=-1)
        .astype(jnp.bfloat16)
        .reshape(seq_length, heads_local * (NOPE + VD))
    )
    d_q_own = split_pair(mul_trans(d_query_low, q_weight))
    d_kv_own = split_pair(mul_trans(d_kv_low, kv_weight))
    d_rot_own = split_pair(jnp.sum(d_key[..., NOPE:], axis=1))
    qup_shard = reduce_dp(trans_mul(q_seq, d_query_low))
    kvup_shard = reduce_dp(trans_mul(kv_seq, d_kv_low))

    _, q_norm_back = jax.vjp(norm_apply, q_latent, gain_q)
    d_q_latent, d_gain_q = q_norm_back(d_q_own)
    _, kv_norm_back = jax.vjp(norm_apply, kv_latent[:, :KR], gain_kv)
    d_kv_latent, d_gain_kv = kv_norm_back(d_kv_own)
    d_rot_raw = rotate_back(kv_latent[:, KR:], own_pos, d_rot_own)
    d_latents = jnp.concatenate([d_q_latent, d_kv_latent, d_rot_raw], axis=-1).astype(jnp.bfloat16)
    d_x_normed = mul_trans(d_latents, down_weight)
    _, x_norm_back = jax.vjp(norm_apply, resid_in, gain_attn)
    d_x_norm, d_gain_attn = x_norm_back(d_x_normed)
    grad_input = d_mid + d_x_norm

    def columns_of(gain, share):
        gain = gain.reshape(-1, share)
        return jnp.pad(gain, ((0, 0), (0, down_rows - share))).reshape(width, 1)

    grad_packed = jnp.concatenate(
        [
            trans_mul(x_normed, d_latents),
            columns_of(d_gain_attn, down_rows),
            columns_of(d_gain_mlp, down_rows),
            columns_of(d_gain_q, q_share),
            columns_of(d_gain_kv, kv_share),
        ],
        axis=1,
    ).reshape(dp_count, tensor_count, down_rows, -1)
    keep = lax.dynamic_index_in_dim(grad_packed, tensor_rank, axis=1, keepdims=False)
    give = lax.dynamic_index_in_dim(grad_packed, 1 - tensor_rank, axis=1, keepdims=False)
    keep = keep + wide(core_swap(low(give)))
    packed_shard = reduce_dp(keep.reshape(dp_count * down_rows, -1))
    gain_shards = packed_shard[:, down_columns:].T

    return (
        layer_out,
        grad_input,
        gain_shards[0],
        packed_shard[:, :q_rank],
        gain_shards[2, :q_share],
        packed_shard[:, q_rank:down_columns],
        gain_shards[3, :kv_share],
        qup_shard,
        kvup_shard,
        out_shard,
        gain_shards[1],
        gate_shard,
        upper_shard,
        down_shard,
    )


def solution(mesh):
    return jax.shard_map(
        body,
        mesh=mesh,
        in_specs=(
            P(("dp", "tensor"), None),
            P("dp"),
            P(("dp", "tensor")),
            P(("dp", "tensor"), None),
            P(("dp", "tensor")),
            P(("dp", "tensor"), None),
            P(("dp", "tensor")),
            P("dp", "tensor"),
            P("dp", "tensor"),
            P("tensor", "dp"),
            P(("dp", "tensor")),
            P("dp", "tensor"),
            P("dp", "tensor"),
            P("tensor", "dp"),
            P(("dp", "tensor"), None),
        ),
        out_specs=(
            P(("dp", "tensor"), None),
            P(("dp", "tensor"), None),
            P(("dp", "tensor")),
            P(("dp", "tensor"), None),
            P(("dp", "tensor")),
            P(("dp", "tensor"), None),
            P(("dp", "tensor")),
            P("dp", "tensor"),
            P("dp", "tensor"),
            P("tensor", "dp"),
            P(("dp", "tensor")),
            P("dp", "tensor"),
            P("dp", "tensor"),
            P("tensor", "dp"),
        ),
        check_vma=False,
    )
```

```python
from functools import partial
import math

import jax
import jax.numpy as jnp
from jax import lax
from jax.experimental import pallas as pl
from jax.experimental.pallas import tpu as pltpu
from jax.sharding import PartitionSpec as P

NOPE = 64
ROPE = 32
VD = 64
KR = 256
LANES = 128
GROUP_BITS = (2, 8)
LAST_BITS = (1, 2)
NEAR, FAR = 4, 8
GROUP = 4


EPS = 1e-05
RESID = 1.4 / math.sqrt(62.0)
THETA = 10000.0
NEG_FILL = -1e30


def norm_apply(values, gain):
    inverse = lax.rsqrt(jnp.mean(values * values, axis=-1, keepdims=True) + EPS)
    return values * inverse * gain


def rotate(values, positions):
    width_half = values.shape[-1] // 2
    frequency = THETA ** (-2.0 * jnp.arange(width_half, dtype=jnp.float32) / values.shape[-1])
    angles = positions.astype(jnp.float32)[:, None] * frequency[None, :]
    extra_dims = (1,) * (values.ndim - 2)
    cosine = jnp.cos(angles).reshape(angles.shape[:1] + extra_dims + angles.shape[1:])
    sine = jnp.sin(angles).reshape(angles.shape[:1] + extra_dims + angles.shape[1:])
    lower_part = values[..., :width_half]
    upper_part = values[..., width_half:]
    return jnp.concatenate(
        [lower_part * cosine - upper_part * sine, upper_part * cosine + lower_part * sine], axis=-1
    )


def rotate_back(values, positions, grads):
    _, pullback = jax.vjp(partial(rotate, positions=positions), values)
    return pullback(grads)[0]


def plain_mul(left, right):
    return jnp.dot(left, right, preferred_element_type=jnp.float32)


def mul_trans(left, right):
    return lax.dot_general(
        left, right, (((1,), (1,)), ((), ())), preferred_element_type=jnp.float32
    )


def trans_mul(left, right):
    return lax.dot_general(
        left, right, (((0,), (0,)), ((), ())), preferred_element_type=jnp.float32
    )


def low(values):
    return values.astype(jnp.bfloat16)


def wide(values):
    return values.astype(jnp.float32)


def core_swap(values):
    return lax.ppermute(values, "tensor", [(0, 1), (1, 0)])


def all_bits():
    count = lax.axis_size("dp")
    return tuple(1 << at for at in range(count.bit_length() - 1))


def other_bits(bits):
    return tuple(bit for bit in all_bits() if bit not in bits)


def masks_of(bits):
    masks = [0]
    for bit in bits:
        masks += [mask | bit for mask in masks]
    return masks


def by_count(bits):
    return sorted(masks_of(bits)[1:], key=lambda mask: (bin(mask).count("1"), mask))


def group_place():
    place = lax.axis_index("dp")
    return sum(((place // bit) % 2) << at for at, bit in enumerate(GROUP_BITS))


class Links:
    def __init__(self):
        self.last = {}
        self.ties = {}

    def tie(self, bit, other):
        self.ties[bit] = self.last[other]

    def flip(self, values, mask):
        bits = [bit for bit in all_bits() if bit & mask]
        before = [self.last[bit] for bit in bits if bit in self.last]
        before += [self.ties.pop(bit) for bit in bits if bit in self.ties]
        if before:
            values, _ = lax.optimization_barrier((values, before))
        count = lax.axis_size("dp")
        got = lax.ppermute(values, "dp", [(place, place ^ mask) for place in range(count)])
        for bit in bits:
            self.last[bit] = got
        return got


def routes(mask, bits, split):
    ordered = [bit for bit in bits if bit & mask]
    if len(ordered) == 1 or not split:
        return [(ordered[0], slice(None))]
    return [(ordered[0], 0), (ordered[-1], 1)]


def halves(values):
    half = values.shape[0] // 2
    return values[:half], values[half:]


def gather_bits(links, values, bits, split, known=None, most=None):
    known = dict(known or {0: [values]})
    for mask in by_count(bits):
        if mask in known or (most and bin(mask).count("1") > most):
            continue
        pieces = []
        for bit, part in routes(mask, bits, split):
            source = known[mask ^ bit]
            whole = source[0] if len(source) == 1 else None
            if part == slice(None):
                moving = whole if whole is not None else jnp.concatenate(source)
            else:
                moving = halves(whole)[part] if whole is not None else source[part]
            pieces.append(links.flip(moving, bit))
        known[mask] = pieces
    return known


def reduce_bits(links, block_of, bits, split, arrive=lambda values, bit: values):
    added = {mask: [] for mask in masks_of(bits)}

    def summed(mask, part):
        values = block_of(mask)
        if part != slice(None):
            values = halves(values)[part]
        if added[mask]:
            values = wide(values)
        for held, extra in added[mask]:
            if part == slice(None) and held != slice(None):
                rest = [jnp.zeros_like(extra)] * 2
                rest[held] = extra
                values = values + jnp.concatenate([wide(item) for item in rest])
            elif part == held:
                values = values + wide(extra)
            elif held == slice(None):
                values = values + wide(halves(extra)[part])
        return values

    for mask in reversed(by_count(bits)):
        for bit, part in routes(mask, bits, split):
            if part == slice(None) and any(held != slice(None) for held, _ in added[mask]):
                moving = jnp.concatenate([low(summed(mask, 0)), low(summed(mask, 1))])
            else:
                moving = low(summed(mask, part))
            added[mask ^ bit].append((part, arrive(links.flip(moving, bit), bit)))
    if any(held != slice(None) for held, _ in added[0]):
        return jnp.concatenate([summed(0, 0), summed(0, 1)])
    return summed(0, slice(None))


def row_order():
    return [
        other | group for other in masks_of(other_bits(GROUP_BITS)) for group in masks_of(GROUP_BITS)
    ]


def first_bits():
    return other_bits(LAST_BITS)


def start_gather(links, values):
    known = gather_bits(links, values, first_bits(), False)
    return jnp.stack([known[mask][0] for mask in masks_of(first_bits())])


def end_gather(links, column, split=True):
    known = gather_bits(links, column, LAST_BITS, split)
    first = masks_of(first_bits())
    half = column.shape[0] // 2

    def block(mask):
        at = first.index(mask & ~sum(LAST_BITS))
        pieces = known[mask & sum(LAST_BITS)]
        return pieces[0][at] if len(pieces) == 1 else pieces[at // half][at % half]

    return jnp.concatenate([block(mask) for mask in row_order()], axis=0)


def reduce_dp(links, grad, split=True):
    order = row_order()
    blocks = grad.reshape(len(order), -1, grad.shape[1])
    first = masks_of(first_bits())

    def column(last):
        return jnp.stack([blocks[order.index(last | mask)] for mask in first])

    partial_sum = reduce_bits(links, column, LAST_BITS, split)
    return reduce_bits(links, lambda mask: partial_sum[first.index(mask)], first_bits(), False)


def place_kernel(place_ref, *refs):
    out_ref = refs[-1]
    for step, ref in enumerate(refs[:-1]):

        @pl.when(pl.program_id(0) == step)
        def _():
            out_ref[0] = ref[...]


def pick_kernel(place_ref, values_ref, *out_refs):
    for step, ref in enumerate(out_refs):

        @pl.when(pl.program_id(0) == step)
        def _():
            ref[...] = values_ref[0]


def place_index():
    return group_place().reshape(1).astype(jnp.int32)


def place_group(blocks):
    rows, width = blocks[0].shape
    return pl.pallas_call(
        place_kernel,
        grid_spec=pltpu.PrefetchScalarGridSpec(
            num_scalar_prefetch=1,
            grid=(GROUP,),
            in_specs=[pl.BlockSpec((rows, width), lambda step, place: (0, 0))] * GROUP,
            out_specs=pl.BlockSpec(
                (1, rows, width), lambda step, place: (lax.bitwise_xor(place[0], step), 0, 0)
            ),
        ),
        out_shape=jax.ShapeDtypeStruct((GROUP, rows, width), blocks[0].dtype),
        compiler_params=pltpu.CompilerParams(vmem_limit_bytes=32 * 2**20),
        name="place_group",
    )(place_index(), *blocks)


def pick_group(values):
    _, rows, width = values.shape
    blocks = pl.pallas_call(
        pick_kernel,
        grid_spec=pltpu.PrefetchScalarGridSpec(
            num_scalar_prefetch=1,
            grid=(GROUP,),
            in_specs=[
                pl.BlockSpec(
                    (1, rows, width), lambda step, place: (lax.bitwise_xor(place[0], step), 0, 0)
                )
            ],
            out_specs=[pl.BlockSpec((rows, width), lambda step, place: (0, 0))] * GROUP,
        ),
        out_shape=[jax.ShapeDtypeStruct((rows, width), values.dtype)] * GROUP,
        compiler_params=pltpu.CompilerParams(vmem_limit_bytes=32 * 2**20),
        name="pick_group",
    )(place_index(), values)
    return list(blocks)


def exchange_group(links, blocks):
    near, far = GROUP_BITS
    there = links.flip(jnp.stack([blocks[1], blocks[3]]), near)
    across = links.flip(blocks[2], far)
    return [blocks[0], there[0], across, links.flip(there[1], far)]


def cut_units(weight, share):
    rows, units = weight.shape
    cut = jnp.moveaxis(weight.reshape(rows, GROUP, units // GROUP), 1, 0)
    return jnp.pad(cut, ((0, 0), (0, 0), (0, share - units // GROUP)))


def join_units(pieces, units):
    rows = pieces.shape[1]
    return wide(jnp.moveaxis(pieces[..., : units // GROUP], 0, 1)).reshape(rows, units)


CHUNKS = 4


def reorder_kernel(steps, block, *refs):
    width = refs[0].shape[-1]
    chunk = width // CHUNKS
    for at, step in enumerate(steps):
        source, target = refs[at], refs[-1].at[at]
        if not step:
            target[...] = source[...]
            continue
        row = lax.broadcasted_iota(jnp.int32, (chunk, chunk), 0)
        column = lax.broadcasted_iota(jnp.int32, (chunk, chunk), 1)
        index = lax.rem(lax.div(column, block), GROUP)
        origin = column + (lax.bitwise_xor(index, step) - index) * block
        moved = jnp.where(row == origin, 1.0, 0.0).astype(jnp.bfloat16)
        for part in range(CHUNKS):
            columns = slice(part * chunk, (part + 1) * chunk)
            target[:, columns] = low(plain_mul(source[:, columns], moved))


def reorder(arrays, steps):
    rows, width = arrays[0].shape
    return pl.pallas_call(
        partial(reorder_kernel, tuple(steps), width // lax.axis_size("dp")),
        out_shape=jax.ShapeDtypeStruct((len(steps), rows, width), arrays[0].dtype),
        compiler_params=pltpu.CompilerParams(vmem_limit_bytes=32 * 2**20),
        name="reorder",
    )(*arrays)


def gather_tokens(links, values):
    known = gather_bits(links, values, GROUP_BITS, False)
    own = reorder([known[mask][0] for mask in masks_of(GROUP_BITS)], range(GROUP))
    own = own.reshape(-1, values.shape[1])
    return own, core_swap(own)


def return_tokens(links, values, rows):
    mine = values.shape[0] // 2
    chip_sum = wide(values[:mine]) + wide(core_swap(values[mine:]))
    chip_sum = chip_sum.reshape(GROUP, rows, -1)
    masks = masks_of(GROUP_BITS)
    return reduce_bits(
        links,
        lambda mask: chip_sum[masks.index(mask)],
        GROUP_BITS,
        False,
        lambda got, bit: reorder([got], [masks.index(bit)])[0],
    )


def units_kernel(
    share, count, own_ref, other_ref, own_back_ref, other_back_ref, *refs
):
    pieces, (act_ref, d_units_ref, d_in_ref, out_ref, weight_ref, sems) = refs[:count], refs[count:]
    step = pl.program_id(0)

    @pl.when(step == 0)
    def _():
        copies, start = [], 0
        for at, piece in enumerate(pieces):
            rows = piece.shape[0]
            copies.append(
                pltpu.make_async_copy(piece, weight_ref.at[pl.ds(start, rows)], sems.at[at])
            )
            start += rows
        for copy in copies:
            copy.start()
        for copy in copies:
            copy.wait()

    is_own = step < pl.num_programs(0) // 2
    tokens = jnp.where(is_own, own_ref[...], other_ref[...])
    back = jnp.where(is_own, own_back_ref[...], other_back_ref[...])
    gate_cut, up_cut = slice(0, share), slice(share, 2 * share)
    down_cut = slice(2 * share, 3 * share)
    gate = plain_mul(tokens, weight_ref[:, gate_cut])
    upper = plain_mul(tokens, weight_ref[:, up_cut])
    d_act = plain_mul(back, weight_ref[:, down_cut])
    slope = 1.0 / (1.0 + jnp.exp(-gate))
    swished = gate * slope
    act = low(swished * upper)
    act_ref[...] = act
    d_units_ref[:, gate_cut] = low(d_act * upper * (slope + swished * (1.0 - slope)))
    d_units_ref[:, up_cut] = low(d_act * swished)
    d_in_ref[...] = low(mul_trans(d_units_ref[...], weight_ref[:, : 2 * share]))
    out_ref[...] = low(mul_trans(act, weight_ref[:, down_cut]))


def run_units(tokens, back, pieces, share):
    own, other = tokens
    rows, width = own.shape
    steps = 4
    block = 2 * rows // steps
    half = steps // 2
    in_own = pl.BlockSpec((block, width), lambda step: (jnp.minimum(step, half - 1), 0))
    in_other = pl.BlockSpec((block, width), lambda step: (jnp.maximum(step - half, 0), 0))
    many = pl.BlockSpec(memory_space=pl.ANY)

    def out_spec(columns):
        return pl.BlockSpec((block, columns), lambda step: (step, 0))

    columns = (share, 2 * share, width, width)
    return pl.pallas_call(
        partial(units_kernel, share, len(pieces)),
        grid=(steps,),
        in_specs=[in_own, in_other, in_own, in_other] + [many] * len(pieces),
        out_specs=[out_spec(item) for item in columns],
        out_shape=[jax.ShapeDtypeStruct((2 * rows, item), jnp.bfloat16) for item in columns],
        scratch_shapes=[
            pltpu.VMEM((width, 3 * share), jnp.bfloat16),
            pltpu.SemaphoreType.DMA((len(pieces),)),
        ],
        compiler_params=pltpu.CompilerParams(vmem_limit_bytes=56 * 2**20),
        name="run_units",
    )(own, other, *back, *pieces)


def unit_grads_kernel(share, own_ref, other_ref, own_back_ref, other_back_ref, act_ref, d_units_ref, out_ref):
    tokens = jnp.concatenate([own_ref[...], other_ref[...]], axis=0)
    out_ref[:, : 2 * share] = low(trans_mul(tokens, d_units_ref[...]))
    back = jnp.concatenate([own_back_ref[...], other_back_ref[...]], axis=0)
    out_ref[:, 2 * share :] = low(trans_mul(back, act_ref[...]))


def unit_grads(tokens, back, act, d_units, share):
    rows, width = tokens[0].shape
    chunk = width // CHUNKS
    part = pl.BlockSpec((rows, chunk), lambda step: (0, step))
    return pl.pallas_call(
        partial(unit_grads_kernel, share),
        grid=(CHUNKS,),
        in_specs=[part] * 4
        + [pl.BlockSpec(act.shape, lambda step: (0, 0)), pl.BlockSpec(d_units.shape, lambda step: (0, 0))],
        out_specs=pl.BlockSpec((chunk, 3 * share), lambda step: (step, 0)),
        out_shape=jax.ShapeDtypeStruct((width, 3 * share), jnp.bfloat16),
        compiler_params=pltpu.CompilerParams(vmem_limit_bytes=56 * 2**20),
        name="unit_grads",
    )(*tokens, *back, act, d_units)


def pair_tokens(values):
    return jnp.concatenate([values, core_swap(values)], axis=0)


def split_pair(values):
    rows = values.shape[0] // 2
    return values[:rows] + wide(core_swap(low(values[rows:])))


def block_origins(total):
    order = row_order()
    block = total // len(order)
    place = jnp.arange(total, dtype=jnp.int32)
    index = place // block
    mask = jnp.zeros_like(index)
    for at, bit in enumerate(GROUP_BITS + other_bits(GROUP_BITS)):
        mask = mask + ((index >> at) % 2) * bit
    return (lax.axis_index("dp") ^ mask) * block + place % block


def one_hot(origins, size):
    return (jnp.arange(size, dtype=jnp.int32)[:, None] == origins[None, :]).astype(jnp.bfloat16)


def in_parts(values, count):
    parts = []
    for _ in range(count):
        part = low(values)
        parts.append(part)
        values = values - wide(part)
    return parts


def move_columns(values, selector, transpose, count):
    rows = values.shape[0]
    stacked = jnp.concatenate(in_parts(values, count), axis=0)
    moved = mul_trans(stacked, selector) if transpose else plain_mul(stacked, selector)
    return sum(moved[at * rows : (at + 1) * rows] for at in range(count))


def round_up(size, step):
    return -(-size // step) * step


def turn_tables(positions):
    lane = jnp.arange(LANES, dtype=jnp.int32)[None, :]
    half = ROPE // 2
    frequency = THETA ** (-2.0 * ((lane - NOPE) % half).astype(jnp.float32) / ROPE)
    angles = positions.astype(jnp.float32)[:, None] * frequency
    in_first = (lane >= NOPE) & (lane < NOPE + half)
    in_last = (lane >= NOPE + half) & (lane < NOPE + ROPE)
    cosine, sine = jnp.cos(angles), jnp.sin(angles)
    keep = jnp.where(in_first | in_last, cosine, jnp.where(lane < NOPE, 1.0, 0.0))
    return keep, jnp.where(in_first, -sine, 0.0), jnp.where(in_last, sine, 0.0)


def lanes_on(values, step):
    return pltpu.roll(values, (-step) % LANES, 1)


def key_of(tile, k_rotary):
    lane = lax.broadcasted_iota(jnp.int32, tile.shape, 1)
    return jnp.where(lane < NOPE, tile, k_rotary)


def probs_of(query, key, visible, scale):
    scores = jnp.where(visible, mul_trans(query, key) * scale, NEG_FILL)
    exp_scores = jnp.exp(scores - jnp.max(scores, axis=-1, keepdims=True))
    return exp_scores / jnp.sum(exp_scores, axis=-1, keepdims=True)


def attend_kernel(scale, q_ref, kv_ref, rot_ref, seen_ref, keep_ref, up_ref, down_ref, out_ref, query_ref):
    visible = seen_ref[...] > 0.0
    outs = []
    for head in range(2):
        lanes = slice(head * LANES, (head + 1) * LANES)
        raw = q_ref[:, lanes]
        query = (
            raw * keep_ref[...]
            + lanes_on(raw, ROPE // 2) * up_ref[...]
            + lanes_on(raw, -(ROPE // 2)) * down_ref[...]
        ).astype(jnp.bfloat16)
        query_ref[:, lanes] = query
        tile = kv_ref[:, lanes]
        probs = probs_of(query, key_of(tile, rot_ref[...]), visible, scale)
        outs.append(plain_mul(probs.astype(jnp.bfloat16), tile))
    lane = lax.broadcasted_iota(jnp.int32, outs[0].shape, 1)
    out_ref[...] = jnp.where(lane < VD, pltpu.roll(outs[0], VD, 1), outs[1]).astype(jnp.bfloat16)


def attend_back_kernel(
    scale, query_ref, kv_ref, rot_ref, seen_ref, keep_ref, up_ref, down_ref, d_out_ref,
    d_q_ref, d_kv_ref, d_rot_ref,
):
    @pl.when(pl.program_id(0) == 0)
    def _():
        d_rot_ref[...] = jnp.zeros_like(d_rot_ref)

    visible = seen_ref[...] > 0.0
    d_pair = wide(d_out_ref[...])
    lane = lax.broadcasted_iota(jnp.int32, d_pair.shape, 1)
    d_rot = d_rot_ref[...]
    for head in range(2):
        lanes = slice(head * LANES, (head + 1) * LANES)
        query = query_ref[:, lanes]
        tile = kv_ref[:, lanes]
        key = key_of(tile, rot_ref[...])
        probs = probs_of(query, key, visible, scale)
        d_head = d_pair if head else pltpu.roll(d_pair, VD, 1)
        d_head = low(jnp.where(lane < NOPE, 0.0, d_head))
        d_probs = mul_trans(d_head, tile)
        d_values = trans_mul(low(probs), d_head)
        row_dot = jnp.sum(probs * d_probs, axis=-1, keepdims=True)
        d_scores = low(probs * (d_probs - row_dot) * scale)
        d_query = plain_mul(d_scores, key)
        d_key = trans_mul(d_scores, query)
        d_q_ref[:, lanes] = low(
            d_query * keep_ref[...]
            - lanes_on(d_query, ROPE // 2) * up_ref[...]
            - lanes_on(d_query, -(ROPE // 2)) * down_ref[...]
        )
        d_kv_ref[:, lanes] = low(jnp.where(lane < NOPE, d_key, d_values))
        d_rot += d_key
    d_rot_ref[...] = d_rot


def attend_specs(length):
    pair = pl.BlockSpec((length, 2 * LANES), lambda step: (0, step))
    single = pl.BlockSpec((length, LANES), lambda step: (0, step))
    table = pl.BlockSpec((length, LANES), lambda step: (0, 0))
    seen = pl.BlockSpec((length, length), lambda step: (0, 0))
    return pair, single, table, seen


def attend(query, key_value, rot_pad, seen, tables, scale):
    length, columns = query.shape
    pair, single, table, whole = attend_specs(length)
    return pl.pallas_call(
        partial(attend_kernel, scale),
        grid=(columns // (2 * LANES),),
        in_specs=[pair, pair, table, whole, table, table, table],
        out_specs=[single, pair],
        out_shape=[
            jax.ShapeDtypeStruct((length, columns // 2), jnp.bfloat16),
            jax.ShapeDtypeStruct((length, columns), jnp.bfloat16),
        ],
        compiler_params=pltpu.CompilerParams(vmem_limit_bytes=32 * 2**20),
        name="attend",
    )(query, key_value, rot_pad, seen, *tables)


def attend_back(query_full, key_value, rot_pad, seen, tables, d_heads, scale):
    length, columns = query_full.shape
    pair, single, table, whole = attend_specs(length)
    return pl.pallas_call(
        partial(attend_back_kernel, scale),
        grid=(columns // (2 * LANES),),
        in_specs=[pair, pair, table, whole, table, table, table, single],
        out_specs=[pair, pair, table],
        out_shape=[
            jax.ShapeDtypeStruct((length, columns), jnp.bfloat16),
            jax.ShapeDtypeStruct((length, columns), jnp.bfloat16),
            jax.ShapeDtypeStruct((length, LANES), jnp.float32),
        ],
        compiler_params=pltpu.CompilerParams(vmem_limit_bytes=32 * 2**20),
        name="attend_back",
    )(query_full, key_value, rot_pad, seen, *tables, d_heads)


def body(
    hidden_in,
    prefix_len,
    attn_gain,
    q_down,
    q_gain,
    kv_down,
    kv_gain,
    q_up,
    kv_up,
    o_proj,
    mlp_gain,
    w_gate,
    w_up,
    w_down,
    cotangent,
):
    tensor_count = lax.axis_size("tensor")
    tensor_rank = lax.axis_index("tensor")
    dp_count = lax.axis_size("dp")
    own_rows, width = hidden_in.shape
    q_rank = q_down.shape[1]
    rank = q_rank + KR
    down_rows = q_down.shape[0]
    q_share, kv_share = q_gain.shape[0], kv_gain.shape[0]
    q_rows, kv_rows = q_up.shape[0], kv_up.shape[0]
    head_qk = NOPE + ROPE
    heads_local = q_up.shape[1] // head_qk
    scale = head_qk ** (-0.5)
    links = Links()
    heads_width = heads_local * LANES
    q_padded = jnp.pad(
        q_up.reshape(q_rows, heads_local, head_qk), ((0, 0), (0, 0), (0, LANES - head_qk))
    ).reshape(q_rows, heads_width)
    units = w_gate.shape[1]
    share = round_up(units // GROUP, LANES)

    down_columns = rank + ROPE
    packed_columns = round_up(down_columns + 3, LANES)

    def column_of(gain):
        return jnp.pad(gain, (0, down_rows - gain.shape[0]))[:, None]

    packed = jnp.concatenate(
        [
            q_down,
            kv_down,
            column_of(attn_gain),
            column_of(mlp_gain),
            column_of(jnp.concatenate([q_gain, kv_gain])),
            jnp.zeros((down_rows, packed_columns - down_columns - 3), jnp.bfloat16),
        ],
        axis=1,
    )
    down_column = start_gather(links, packed)
    up_column = start_gather(links, jnp.concatenate([q_padded, kv_up], axis=0))
    out_column = start_gather(links, o_proj.T)
    core_packed = end_gather(links, down_column).reshape(dp_count, down_rows, packed_columns)
    unit_column = jnp.stack(
        exchange_group(
            links,
            pick_group(
                jnp.concatenate([cut_units(item, share) for item in (w_gate, w_up, w_down.T)], axis=-1)
            ),
        )
    )
    up_weight = end_gather(links, up_column)
    out_trans = end_gather(links, out_column)
    other_packed = core_swap(core_packed)
    is_first = tensor_rank == 0
    all_packed = jnp.stack(
        [
            jnp.where(is_first, core_packed, other_packed),
            jnp.where(is_first, other_packed, core_packed),
        ],
        axis=1,
    ).reshape(width, packed_columns)

    width_origins = block_origins(width)
    to_order = one_hot(width_origins, width)
    rank_block = q_rows + kv_rows
    place = jnp.arange(rank, dtype=jnp.int32)
    device_of = block_origins(rank) // rank_block
    in_block = place % rank_block
    is_query = in_block < q_rows
    rank_order = one_hot(
        jnp.where(
            is_query,
            device_of * q_rows + in_block,
            q_rank + device_of * kv_rows + in_block - q_rows,
        ),
        rank,
    )
    device_place = width_origins // down_rows
    in_share = width_origins % down_rows
    gain_order = one_hot(
        jnp.where(
            in_share < q_share,
            device_place * q_share + in_share,
            jnp.where(
                in_share < q_share + kv_share,
                q_rank + device_place * kv_share + in_share - q_share,
                -1,
            ),
        ),
        rank,
    )
    gains = all_packed[:, down_columns : down_columns + 3].T
    gain_attn = wide(gains[0])
    gain_mlp = wide(gains[1])
    gain_rank = mul_trans(gains[2:3], gain_order)[0]
    gain_q, gain_kv = gain_rank[:q_rank], gain_rank[q_rank:]

    moved_in = plain_mul(jnp.concatenate([hidden_in, cotangent], axis=0), to_order)
    resid_in, grad_out = moved_in[:own_rows], moved_in[own_rows:]
    mlp_back = gather_tokens(links, (RESID * grad_out).astype(jnp.bfloat16))
    others = other_bits(GROUP_BITS)
    links.tie(NEAR, FAR)
    known_units = gather_bits(links, unit_column, others, True, most=1)
    x_normed = norm_apply(resid_in, gain_attn).astype(jnp.bfloat16)
    latents = plain_mul(x_normed, all_packed)
    q_latent = latents[:, :q_rank]
    kv_latent = latents[:, q_rank:rank]
    rot_latent = latents[:, rank:down_columns]
    q_normed = norm_apply(q_latent, gain_q).astype(jnp.bfloat16)
    kv_normed = norm_apply(kv_latent, gain_kv).astype(jnp.bfloat16)
    own_pos = tensor_rank * own_rows + jnp.arange(own_rows, dtype=jnp.int32)
    other_pos = (1 - tensor_rank) * own_rows + jnp.arange(own_rows, dtype=jnp.int32)
    positions = jnp.concatenate([own_pos, other_pos])
    k_rotary = rotate(rot_latent, own_pos).astype(jnp.bfloat16)
    ranks_normed = low(plain_mul(jnp.concatenate([q_normed, kv_normed], axis=-1), rank_order))
    rot_pad = jnp.pad(k_rotary, ((0, 0), (NOPE, LANES - head_qk)))
    latent_seq = pair_tokens(jnp.concatenate([ranks_normed, rot_pad], axis=-1))
    rank_seq = latent_seq[:, :rank]
    rot_seq = latent_seq[:, rank:]
    zero = jnp.zeros((), jnp.bfloat16)
    q_seq = jnp.where(is_query[None, :], rank_seq, zero)
    kv_seq = jnp.where(is_query[None, :], zero, rank_seq)
    query = plain_mul(q_seq, up_weight)
    key_value = low(plain_mul(kv_seq, up_weight))
    visible = (positions[None, :] <= positions[:, None]) | (positions[None, :] < prefix_len[0])
    seen = visible.astype(jnp.float32)
    tables = turn_tables(positions)
    heads_low, query_full = attend(query, key_value, rot_seq, seen, tables, scale)
    attn_own = split_pair(mul_trans(heads_low, out_trans))
    mid_resid = resid_in + RESID * attn_own
    mlp_normed = norm_apply(mid_resid, gain_mlp).astype(jnp.bfloat16)

    links.tie(FAR, NEAR)
    mlp_seq = gather_tokens(links, mlp_normed)
    links.tie(NEAR, FAR)
    known_units = gather_bits(links, unit_column, others, True, known=known_units)
    unit_pieces = [
        piece.reshape(-1, 3 * share) for mask in masks_of(others) for piece in known_units[mask]
    ]
    act_low, d_units, d_mlp_terms, mlp_terms = run_units(mlp_seq, mlp_back, unit_pieces, share)
    d_mlp_own = return_tokens(links, d_mlp_terms, own_rows)
    unit_grad = unit_grads(mlp_seq, mlp_back, act_low, d_units, share).reshape(
        len(masks_of(others)), GROUP, -1, 3 * share
    )
    links.tie(NEAR, FAR)
    unit_sum = reduce_bits(
        links, lambda mask: unit_grad[masks_of(others).index(mask)], others, True
    )
    mlp_own = return_tokens(links, mlp_terms, own_rows)
    layer_out = low(mul_trans(low(mid_resid + RESID * mlp_own), to_order))
    unit_shards = place_group(exchange_group(links, [low(unit_sum[at]) for at in range(GROUP)]))
    gate_shard = join_units(unit_shards[..., :share], units)
    upper_shard = join_units(unit_shards[..., share : 2 * share], units)
    down_shard = join_units(unit_shards[..., 2 * share :], units).T

    _, mlp_norm_back = jax.vjp(norm_apply, mid_resid, gain_mlp)
    d_mid_norm, _ = mlp_norm_back(d_mlp_own)
    mid_inverse = lax.rsqrt(jnp.mean(mid_resid * mid_resid, axis=-1, keepdims=True) + EPS)
    gain_mlp_terms = d_mlp_own * mid_resid * mid_inverse
    d_mid = grad_out + d_mid_norm
    attn_back = pair_tokens((RESID * d_mid).astype(jnp.bfloat16))
    d_heads = low(plain_mul(attn_back, out_trans))
    out_shard = reduce_dp(links, trans_mul(attn_back, heads_low)).T
    d_query, d_key_value, d_rot = attend_back(
        query_full, key_value, rot_seq, seen, tables, d_heads, scale
    )
    d_rank = jnp.where(
        is_query[None, :], mul_trans(d_query, up_weight), mul_trans(d_key_value, up_weight)
    )
    d_latent_own = split_pair(jnp.concatenate([d_rank, d_rot], axis=-1))
    d_rank_own = move_columns(d_latent_own[:, :rank], rank_order, True, 2)
    d_q_own, d_kv_own = d_rank_own[:, :q_rank], d_rank_own[:, q_rank:]
    d_rot_own = d_latent_own[:, rank + NOPE : rank + head_qk]
    up_shard = reduce_dp(
        links,
        trans_mul(
            jnp.concatenate([q_seq, kv_seq], axis=0),
            jnp.concatenate([d_query, d_key_value], axis=0),
        ),
    )
    qup_shard = up_shard[:q_rows].reshape(q_rows, heads_local, LANES)[..., :head_qk]
    kvup_shard = up_shard[q_rows:]

    _, q_norm_back = jax.vjp(norm_apply, q_latent, gain_q)
    d_q_latent, _ = q_norm_back(d_q_own)
    _, kv_norm_back = jax.vjp(norm_apply, kv_latent, gain_kv)
    d_kv_latent, _ = kv_norm_back(d_kv_own)
    q_inverse = lax.rsqrt(jnp.mean(q_latent * q_latent, axis=-1, keepdims=True) + EPS)
    kv_inverse = lax.rsqrt(jnp.mean(kv_latent * kv_latent, axis=-1, keepdims=True) + EPS)
    gain_rank_terms = low(
        jnp.concatenate(
            [d_q_own * q_latent * q_inverse, d_kv_own * kv_latent * kv_inverse], axis=-1
        )
    )
    d_rot_raw = rotate_back(rot_latent, own_pos, d_rot_own)
    d_latents = low(
        jnp.concatenate(
            [
                d_q_latent,
                d_kv_latent,
                d_rot_raw,
                jnp.zeros((own_rows, packed_columns - down_columns), jnp.float32),
            ],
            axis=-1,
        )
    )
    d_x_normed = mul_trans(d_latents, all_packed)
    _, x_norm_back = jax.vjp(norm_apply, resid_in, gain_attn)
    d_x_norm, _ = x_norm_back(d_x_normed)
    x_inverse = lax.rsqrt(jnp.mean(resid_in * resid_in, axis=-1, keepdims=True) + EPS)
    gain_attn_terms = d_x_normed * resid_in * x_inverse
    grad_input = move_columns(d_mid + d_x_norm, to_order, True, 3)

    kind = jnp.arange(3 * own_rows, dtype=jnp.int32)[:, None] // own_rows + down_columns
    markers = (jnp.arange(packed_columns, dtype=jnp.int32)[None, :] == kind).astype(jnp.bfloat16)
    grad_packed = trans_mul(
        jnp.concatenate(
            [
                x_normed,
                low(gain_attn_terms),
                low(gain_mlp_terms),
                low(plain_mul(gain_rank_terms, gain_order)),
            ],
            axis=0,
        ),
        jnp.concatenate([d_latents, markers], axis=0),
    ).reshape(dp_count, tensor_count, down_rows, packed_columns)
    keep = jnp.where(is_first, grad_packed[:, 0], grad_packed[:, 1])
    give = jnp.where(is_first, grad_packed[:, 1], grad_packed[:, 0])
    keep = keep + wide(core_swap(low(give)))
    packed_shard = reduce_dp(links, keep.reshape(dp_count * down_rows, packed_columns))
    gain_shards = packed_shard[:, down_columns : down_columns + 3].T

    return (
        layer_out,
        grad_input,
        gain_shards[0],
        packed_shard[:, :q_rank],
        gain_shards[2, :q_share],
        packed_shard[:, q_rank:down_columns],
        gain_shards[2, q_share : q_share + kv_share],
        qup_shard.reshape(q_up.shape),
        kvup_shard,
        out_shard,
        gain_shards[1],
        gate_shard,
        upper_shard,
        down_shard,
    )


def solution(mesh):
    return jax.shard_map(
        body,
        mesh=mesh,
        in_specs=(
            P(("dp", "tensor"), None),
            P("dp"),
            P(("dp", "tensor")),
            P(("dp", "tensor"), None),
            P(("dp", "tensor")),
            P(("dp", "tensor"), None),
            P(("dp", "tensor")),
            P("dp", "tensor"),
            P("dp", "tensor"),
            P("tensor", "dp"),
            P(("dp", "tensor")),
            P("dp", "tensor"),
            P("dp", "tensor"),
            P("tensor", "dp"),
            P(("dp", "tensor"), None),
        ),
        out_specs=(
            P(("dp", "tensor"), None),
            P(("dp", "tensor"), None),
            P(("dp", "tensor")),
            P(("dp", "tensor"), None),
            P(("dp", "tensor")),
            P(("dp", "tensor"), None),
            P(("dp", "tensor")),
            P("dp", "tensor"),
            P("dp", "tensor"),
            P("tensor", "dp"),
            P(("dp", "tensor")),
            P("dp", "tensor"),
            P("dp", "tensor"),
            P("tensor", "dp"),
        ),
        check_vma=False,
    )
```

```python
from functools import partial
import math

import jax
import jax.numpy as jnp
from jax import lax
from jax.experimental import pallas as pl
from jax.experimental.pallas import tpu as pltpu
from jax.sharding import PartitionSpec as P

NOPE = 64
ROPE = 32
VD = 64
KR = 256
LANES = 128
GROUP_BITS = (2, 8)
LAST_BITS = (1, 2)
NEAR, FAR = 4, 8
GROUP = 4


EPS = 1e-05
RESID = 1.4 / math.sqrt(62.0)
THETA = 10000.0
NEG_FILL = -1e30


def norm_apply(values, gain):
    inverse = lax.rsqrt(jnp.mean(values * values, axis=-1, keepdims=True) + EPS)
    return values * inverse * gain


def rotate(values, positions):
    width_half = values.shape[-1] // 2
    frequency = THETA ** (-2.0 * jnp.arange(width_half, dtype=jnp.float32) / values.shape[-1])
    angles = positions.astype(jnp.float32)[:, None] * frequency[None, :]
    extra_dims = (1,) * (values.ndim - 2)
    cosine = jnp.cos(angles).reshape(angles.shape[:1] + extra_dims + angles.shape[1:])
    sine = jnp.sin(angles).reshape(angles.shape[:1] + extra_dims + angles.shape[1:])
    lower_part = values[..., :width_half]
    upper_part = values[..., width_half:]
    return jnp.concatenate(
        [lower_part * cosine - upper_part * sine, upper_part * cosine + lower_part * sine], axis=-1
    )


def rotate_back(values, positions, grads):
    _, pullback = jax.vjp(partial(rotate, positions=positions), values)
    return pullback(grads)[0]


def plain_mul(left, right):
    return jnp.dot(left, right, preferred_element_type=jnp.float32)


def mul_trans(left, right):
    return lax.dot_general(
        left, right, (((1,), (1,)), ((), ())), preferred_element_type=jnp.float32
    )


def trans_mul(left, right):
    return lax.dot_general(
        left, right, (((0,), (0,)), ((), ())), preferred_element_type=jnp.float32
    )


def low(values):
    return values.astype(jnp.bfloat16)


def wide(values):
    return values.astype(jnp.float32)


def core_swap(values):
    return lax.ppermute(values, "tensor", [(0, 1), (1, 0)])


def all_bits():
    count = lax.axis_size("dp")
    return tuple(1 << at for at in range(count.bit_length() - 1))


def other_bits(bits):
    return tuple(bit for bit in all_bits() if bit not in bits)


def masks_of(bits):
    masks = [0]
    for bit in bits:
        masks += [mask | bit for mask in masks]
    return masks


def by_count(bits):
    return sorted(masks_of(bits)[1:], key=lambda mask: bin(mask).count("1"))


def group_place():
    place = lax.axis_index("dp")
    return sum(((place // bit) % 2) << at for at, bit in enumerate(GROUP_BITS))


def tied(values, others):
    return lax.optimization_barrier((values, others))[0] if others else values


AFTER = {
    "A1": ("B0", "B1"),
    "C1": ("B0",),
    "U0": ("B2", "C0", "C1"),
    "B3": ("C0", "C1"),
    "B4": ("C2",),
    "B5": ("latents", "V1"),
    "B6": ("latents",),
    "G1": ("B4",),
    "G2": ("B5", "B6"),
    "C5": ("G1", "V2"),
    "C6": ("G1", "V2"),
    "M0": ("G2",),
    "M1": ("G2",),
    "M2": ("W1", "W0"),
    "W2": ("M1",),
    "W3": ("M1",),
    "R1": ("D1",),
    "R2": ("D2", "D1"),
    "R3": ("D2", "D1"),
    "P0": ("D2", "D1"),
    "P1": ("R0",),
    "P2": ("R1",),
    "O0": ("R1",),
    "Q0": ("P2", "R2"),
    "Q1": ("R2",),
    "T0": ("Q3",),
}


class Flow:
    def __init__(self, links, name, routine):
        self.links, self.name, self.routine = links, name, routine
        self.count, self.result, self.given = 0, None, None
        self.wanted = self.resume(None)

    def resume(self, given):
        try:
            return self.routine.send(given)
        except StopIteration as end:
            self.result = end.value
            return None

    def step(self, hold=()):
        if self.wanted is None:
            return self
        name = self.name + str(self.count)
        got = self.links.send(*self.wanted, AFTER.get(name, ()))
        self.links.done[name] = got
        self.count += 1
        self.wanted = self.resume(tied(got, self.links.named(hold)))
        return self

    def end(self):
        while self.wanted is not None:
            self.step()
        return self.result


class Links:
    def __init__(self):
        self.last = {}
        self.done = {}

    def named(self, names):
        return [self.done[name] for name in names if name in self.done]

    def send(self, values, mask, after=()):
        masks = mask if isinstance(mask, list) else [mask]
        bits = sorted({bit for item in masks for bit in all_bits() if bit & item})
        before = self.named(after) + [self.last[bit] for bit in bits if bit in self.last]
        values = tied(values, before)
        count = lax.axis_size("dp")
        got = [
            lax.ppermute(item, "dp", [(place, place ^ to) for place in range(count)])
            for item, to in zip(values if mask is masks else [values], masks)
        ]
        got = got if mask is masks else got[0]
        self.last.update({bit: got for bit in bits})
        return got

    def flow(self, name, routine):
        return Flow(self, name, routine)


def routes(mask, bits, split):
    ordered = [bit for bit in bits if bit & mask]
    if len(ordered) > 1 and split == "both":
        return [(ordered[0], 0), (ordered[-1], 1)]
    return [(ordered[-1 if split == "last" else 0], None)]


def halves(values):
    half = values.shape[0] // 2
    return values[:half], values[half:]


def gather_bits(values, bits, split):
    known = {0: [values]}
    for mask in by_count(bits):
        pieces = []
        for bit, part in routes(mask, bits, split):
            source = known[mask ^ bit]
            if part is None:
                moving = source[0] if len(source) == 1 else jnp.concatenate(source)
            else:
                moving = halves(source[0])[part] if len(source) == 1 else source[part]
            pieces.append((yield moving, bit))
        known[mask] = pieces
    return known


def reduce_bits(block_of, bits, split, arrive=lambda values, bit: values):
    added = {mask: [] for mask in masks_of(bits)}

    def summed(mask, part):
        values = block_of(mask)
        if part is not None:
            values = halves(values)[part]
        if added[mask]:
            values = wide(values)
        for held, extra in added[mask]:
            if part is None or part == held:
                values = values + wide(extra)
            elif held is None:
                values = values + wide(halves(extra)[part])
        return values

    def whole(mask):
        if any(held is not None for held, _ in added[mask]):
            return [summed(mask, 0), summed(mask, 1)]
        return [summed(mask, None)]

    for mask in reversed(by_count(bits)):
        for bit, part in routes(mask, bits, split):
            if part is None:
                parts = [low(item) for item in whole(mask)]
                moving = parts[0] if len(parts) == 1 else jnp.concatenate(parts)
            else:
                moving = low(summed(mask, part))
            got = yield moving, bit
            added[mask ^ bit].append((part, arrive(got, bit)))
    parts = whole(0)
    return parts[0] if len(parts) == 1 else jnp.concatenate(parts)


def row_order():
    return [
        other | group for other in masks_of(other_bits(GROUP_BITS)) for group in masks_of(GROUP_BITS)
    ]


def first_bits():
    return other_bits(LAST_BITS)


def gather_dp(values):
    first = masks_of(first_bits())
    known = yield from gather_bits(values, first_bits(), "first")
    column = jnp.stack([known[mask][0] for mask in first])
    known = yield from gather_bits(column, LAST_BITS, "both")
    half = len(first) // 2

    def block(mask):
        at = first.index(mask & ~sum(LAST_BITS))
        pieces = known[mask & sum(LAST_BITS)]
        return pieces[0][at] if len(pieces) == 1 else pieces[at // half][at % half]

    return jnp.concatenate([block(mask) for mask in row_order()], axis=0)


def gather_dp_direct(values):
    first, last = masks_of(first_bits()), masks_of(LAST_BITS)
    got = yield [values] * (len(first) - 1), first[1:]
    column = jnp.stack([values] + got)
    got = yield [column] * (len(last) - 1), last[1:]
    known = dict(zip(last, [column] + got))
    return jnp.concatenate(
        [known[mask & sum(LAST_BITS)][first.index(mask & ~sum(LAST_BITS))] for mask in row_order()],
        axis=0,
    )


def reduce_dp_direct(grad):
    order, first, last = row_order(), masks_of(first_bits()), masks_of(LAST_BITS)
    blocks = grad.reshape(len(order), -1, grad.shape[1])
    columns = [jnp.stack([blocks[order.index(mask | item)] for item in first]) for mask in last]
    got = yield [low(column) for column in columns[1:]], last[1:]
    column = columns[0] + sum(wide(item) for item in got)
    got = yield [low(column[at]) for at in range(1, len(first))], first[1:]
    return column[0] + sum(wide(item) for item in got)


def reduce_dp(grad):
    order = row_order()
    blocks = grad.reshape(len(order), -1, grad.shape[1])
    first = masks_of(first_bits())

    def column(last):
        return jnp.stack([blocks[order.index(last | mask)] for mask in first])

    partial_sum = yield from reduce_bits(column, LAST_BITS, "both")
    return (
        yield from reduce_bits(lambda mask: partial_sum[first.index(mask)], first_bits(), "first")
    )


def place_kernel(place_ref, *refs):
    out_ref = refs[-1]
    for step, ref in enumerate(refs[:-1]):

        @pl.when(pl.program_id(0) == step)
        def _():
            out_ref[0] = ref[...]


def pick_kernel(place_ref, values_ref, *out_refs):
    for step, ref in enumerate(out_refs):

        @pl.when(pl.program_id(0) == step)
        def _():
            ref[...] = values_ref[0]


def place_index():
    return group_place().reshape(1).astype(jnp.int32)


def place_group(blocks):
    rows, width = blocks[0].shape
    return pl.pallas_call(
        place_kernel,
        grid_spec=pltpu.PrefetchScalarGridSpec(
            num_scalar_prefetch=1,
            grid=(GROUP,),
            in_specs=[pl.BlockSpec((rows, width), lambda step, place: (0, 0))] * GROUP,
            out_specs=pl.BlockSpec(
                (1, rows, width), lambda step, place: (lax.bitwise_xor(place[0], step), 0, 0)
            ),
        ),
        out_shape=jax.ShapeDtypeStruct((GROUP, rows, width), blocks[0].dtype),
        compiler_params=pltpu.CompilerParams(vmem_limit_bytes=32 * 2**20),
        name="place_group",
    )(place_index(), *blocks)


def pick_group(values):
    _, rows, width = values.shape
    blocks = pl.pallas_call(
        pick_kernel,
        grid_spec=pltpu.PrefetchScalarGridSpec(
            num_scalar_prefetch=1,
            grid=(GROUP,),
            in_specs=[
                pl.BlockSpec(
                    (1, rows, width), lambda step, place: (lax.bitwise_xor(place[0], step), 0, 0)
                )
            ],
            out_specs=[pl.BlockSpec((rows, width), lambda step, place: (0, 0))] * GROUP,
        ),
        out_shape=[jax.ShapeDtypeStruct((rows, width), values.dtype)] * GROUP,
        compiler_params=pltpu.CompilerParams(vmem_limit_bytes=32 * 2**20),
        name="pick_group",
    )(place_index(), values)
    return list(blocks)


def exchange_group(blocks, arrived):
    near, far = GROUP_BITS
    there = yield jnp.stack([blocks[1], blocks[3]]), near
    arrived.append(jnp.stack([blocks[0], there[0]]))
    across = yield blocks[2], far
    relayed = yield there[1], far
    arrived.append(jnp.stack([across, relayed]))


def cut_units(weight, share):
    rows, units = weight.shape
    cut = jnp.moveaxis(weight.reshape(rows, GROUP, units // GROUP), 1, 0)
    return jnp.pad(cut, ((0, 0), (0, 0), (0, share - units // GROUP)))


def join_units(pieces, units):
    rows = pieces.shape[1]
    return wide(jnp.moveaxis(pieces[..., : units // GROUP], 0, 1)).reshape(rows, units)


CHUNKS = 4


def reorder_kernel(steps, block, *refs):
    width = refs[0].shape[-1]
    chunk = width // CHUNKS
    for at, step in enumerate(steps):
        source, target = refs[at], refs[-1].at[at]
        if not step:
            target[...] = source[...]
            continue
        row = lax.broadcasted_iota(jnp.int32, (chunk, chunk), 0)
        column = lax.broadcasted_iota(jnp.int32, (chunk, chunk), 1)
        index = lax.rem(lax.div(column, block), GROUP)
        origin = column + (lax.bitwise_xor(index, step) - index) * block
        moved = jnp.where(row == origin, 1.0, 0.0).astype(jnp.bfloat16)
        for part in range(CHUNKS):
            columns = slice(part * chunk, (part + 1) * chunk)
            target[:, columns] = low(plain_mul(source[:, columns], moved))


def reorder(arrays, steps):
    rows, width = arrays[0].shape
    return pl.pallas_call(
        partial(reorder_kernel, tuple(steps), width // lax.axis_size("dp")),
        out_shape=jax.ShapeDtypeStruct((len(steps), rows, width), arrays[0].dtype),
        compiler_params=pltpu.CompilerParams(vmem_limit_bytes=32 * 2**20),
        name="reorder",
    )(*arrays)


def gather_tokens(values):
    known = yield from gather_bits(values, GROUP_BITS, "first")
    own = reorder([known[mask][0] for mask in masks_of(GROUP_BITS)], range(GROUP))
    own = own.reshape(-1, values.shape[1])
    return own, core_swap(own)


def gather_whole_tokens(values, to_order):
    known = yield from gather_bits(values, GROUP_BITS, "last")
    own = jnp.concatenate([known[mask][0] for mask in masks_of(GROUP_BITS)], axis=0)
    own = low(plain_mul(own, to_order))
    return own, core_swap(own)


def return_tokens(mine, others, rows):
    chip_sum = (wide(mine) + wide(others)).reshape(GROUP, rows, -1)
    masks = masks_of(GROUP_BITS)
    return reduce_bits(
        lambda mask: chip_sum[masks.index(mask)],
        GROUP_BITS,
        "first",
        lambda got, bit: reorder([got], [masks.index(bit)])[0],
    )


def units_kernel(
    share, count, own_ref, other_ref, own_back_ref, other_back_ref, *refs
):
    pieces, (act_ref, d_units_ref, d_in_ref, out_ref, weight_ref, sems) = refs[:count], refs[count:]
    step = pl.program_id(0)

    @pl.when(step == 0)
    def _():
        copies, start = [], 0
        for at, piece in enumerate(pieces):
            rows = piece.shape[0]
            copies.append(
                pltpu.make_async_copy(piece, weight_ref.at[pl.ds(start, rows)], sems.at[at])
            )
            start += rows
        for copy in copies:
            copy.start()
        for copy in copies:
            copy.wait()

    is_own = step < pl.num_programs(0) // 2
    tokens = jnp.where(is_own, own_ref[...], other_ref[...])
    back = jnp.where(is_own, own_back_ref[...], other_back_ref[...])
    gate_cut, up_cut = slice(0, share), slice(share, 2 * share)
    down_cut = slice(2 * share, 3 * share)
    gate = plain_mul(tokens, weight_ref[:, gate_cut])
    upper = plain_mul(tokens, weight_ref[:, up_cut])
    d_act = plain_mul(back, weight_ref[:, down_cut])
    slope = 1.0 / (1.0 + jnp.exp(-gate))
    swished = gate * slope
    act = low(swished * upper)
    act_ref[...] = act
    d_units_ref[:, gate_cut] = low(d_act * upper * (slope + swished * (1.0 - slope)))
    d_units_ref[:, up_cut] = low(d_act * swished)
    d_in_ref[...] = low(mul_trans(d_units_ref[...], weight_ref[:, : 2 * share]))
    out_ref[...] = low(mul_trans(act, weight_ref[:, down_cut]))


def run_units(tokens, back, pieces, share):
    own, other = tokens
    rows, width = own.shape
    steps = 4
    block = 2 * rows // steps
    half = steps // 2
    in_own = pl.BlockSpec((block, width), lambda step: (jnp.minimum(step, half - 1), 0))
    in_other = pl.BlockSpec((block, width), lambda step: (jnp.maximum(step - half, 0), 0))
    many = pl.BlockSpec(memory_space=pl.ANY)

    def out_spec(columns):
        return pl.BlockSpec((block, columns), lambda step: (step, 0))

    columns = (share, 2 * share, width, width)
    return pl.pallas_call(
        partial(units_kernel, share, len(pieces)),
        grid=(steps,),
        in_specs=[in_own, in_other, in_own, in_other] + [many] * len(pieces),
        out_specs=[out_spec(item) for item in columns],
        out_shape=[jax.ShapeDtypeStruct((2 * rows, item), jnp.bfloat16) for item in columns],
        scratch_shapes=[
            pltpu.VMEM((width, 3 * share), jnp.bfloat16),
            pltpu.SemaphoreType.DMA((len(pieces),)),
        ],
        compiler_params=pltpu.CompilerParams(vmem_limit_bytes=56 * 2**20),
        name="run_units",
    )(own, other, *back, *pieces)


def unit_grads_kernel(share, own_ref, other_ref, own_back_ref, other_back_ref, act_ref, d_units_ref, out_ref):
    tokens = jnp.concatenate([own_ref[...], other_ref[...]], axis=0)
    out_ref[:, : 2 * share] = low(trans_mul(tokens, d_units_ref[...]))
    back = jnp.concatenate([own_back_ref[...], other_back_ref[...]], axis=0)
    out_ref[:, 2 * share :] = low(trans_mul(back, act_ref[...]))


def unit_grads(tokens, back, act, d_units, share):
    rows, width = tokens[0].shape
    chunk = width // CHUNKS
    part = pl.BlockSpec((rows, chunk), lambda step: (0, step))
    return pl.pallas_call(
        partial(unit_grads_kernel, share),
        grid=(CHUNKS,),
        in_specs=[part] * 4
        + [pl.BlockSpec(act.shape, lambda step: (0, 0)), pl.BlockSpec(d_units.shape, lambda step: (0, 0))],
        out_specs=pl.BlockSpec((chunk, 3 * share), lambda step: (step, 0)),
        out_shape=jax.ShapeDtypeStruct((width, 3 * share), jnp.bfloat16),
        compiler_params=pltpu.CompilerParams(vmem_limit_bytes=56 * 2**20),
        name="unit_grads",
    )(*tokens, *back, act, d_units)


def pair_tokens(values):
    return jnp.concatenate([values, core_swap(values)], axis=0)


def split_pair(values):
    rows = values.shape[0] // 2
    return values[:rows] + wide(core_swap(low(values[rows:])))


def block_origins(total):
    order = row_order()
    block = total // len(order)
    place = jnp.arange(total, dtype=jnp.int32)
    index = place // block
    mask = jnp.zeros_like(index)
    for at, bit in enumerate(GROUP_BITS + other_bits(GROUP_BITS)):
        mask = mask + ((index >> at) % 2) * bit
    return (lax.axis_index("dp") ^ mask) * block + place % block


def one_hot(origins, size):
    return (jnp.arange(size, dtype=jnp.int32)[:, None] == origins[None, :]).astype(jnp.bfloat16)


def pad_heads(columns, head):
    column = jnp.arange(columns // head * LANES, dtype=jnp.int32)
    within = column % LANES
    return one_hot(jnp.where(within < head, column // LANES * head + within, -1), columns)


def in_parts(values, count):
    parts = []
    for _ in range(count):
        part = low(values)
        parts.append(part)
        values = values - wide(part)
    return parts


def move_columns(values, selector, transpose, count):
    rows = values.shape[0]
    stacked = jnp.concatenate(in_parts(values, count), axis=0)
    moved = mul_trans(stacked, selector) if transpose else plain_mul(stacked, selector)
    return sum(moved[at * rows : (at + 1) * rows] for at in range(count))


def round_up(size, step):
    return -(-size // step) * step


def turn_tables(positions):
    lane = jnp.arange(LANES, dtype=jnp.int32)[None, :]
    half = ROPE // 2
    frequency = THETA ** (-2.0 * ((lane - NOPE) % half).astype(jnp.float32) / ROPE)
    angles = positions.astype(jnp.float32)[:, None] * frequency
    in_first = (lane >= NOPE) & (lane < NOPE + half)
    in_last = (lane >= NOPE + half) & (lane < NOPE + ROPE)
    cosine, sine = jnp.cos(angles), jnp.sin(angles)
    keep = jnp.where(in_first | in_last, cosine, jnp.where(lane < NOPE, 1.0, 0.0))
    return keep, jnp.where(in_first, -sine, 0.0), jnp.where(in_last, sine, 0.0)


def lanes_on(values, step):
    return pltpu.roll(values, (-step) % LANES, 1)


def key_of(tile, k_rotary):
    lane = lax.broadcasted_iota(jnp.int32, tile.shape, 1)
    return jnp.where(lane < NOPE, tile, k_rotary)


def probs_of(query, key, visible, scale):
    scores = jnp.where(visible, mul_trans(query, key) * scale, NEG_FILL)
    exp_scores = jnp.exp(scores - jnp.max(scores, axis=-1, keepdims=True))
    return exp_scores / jnp.sum(exp_scores, axis=-1, keepdims=True)


def attend_kernel(scale, q_ref, kv_ref, rot_ref, seen_ref, keep_ref, up_ref, down_ref, out_ref, query_ref):
    visible = seen_ref[...] > 0.0
    outs = []
    for head in range(2):
        lanes = slice(head * LANES, (head + 1) * LANES)
        raw = q_ref[:, lanes]
        query = (
            raw * keep_ref[...]
            + lanes_on(raw, ROPE // 2) * up_ref[...]
            + lanes_on(raw, -(ROPE // 2)) * down_ref[...]
        ).astype(jnp.bfloat16)
        query_ref[:, lanes] = query
        tile = kv_ref[:, lanes]
        probs = probs_of(query, key_of(tile, rot_ref[...]), visible, scale)
        outs.append(plain_mul(probs.astype(jnp.bfloat16), tile))
    lane = lax.broadcasted_iota(jnp.int32, outs[0].shape, 1)
    out_ref[...] = jnp.where(lane < VD, pltpu.roll(outs[0], VD, 1), outs[1]).astype(jnp.bfloat16)


def attend_back_kernel(
    scale, query_ref, kv_ref, rot_ref, seen_ref, keep_ref, up_ref, down_ref, d_out_ref,
    d_q_ref, d_kv_ref, d_rot_ref,
):
    @pl.when(pl.program_id(0) == 0)
    def _():
        d_rot_ref[...] = jnp.zeros_like(d_rot_ref)

    visible = seen_ref[...] > 0.0
    d_pair = wide(d_out_ref[...])
    lane = lax.broadcasted_iota(jnp.int32, d_pair.shape, 1)
    d_rot = d_rot_ref[...]
    for head in range(2):
        lanes = slice(head * LANES, (head + 1) * LANES)
        query = query_ref[:, lanes]
        tile = kv_ref[:, lanes]
        key = key_of(tile, rot_ref[...])
        probs = probs_of(query, key, visible, scale)
        d_head = d_pair if head else pltpu.roll(d_pair, VD, 1)
        d_head = low(jnp.where(lane < NOPE, 0.0, d_head))
        d_probs = mul_trans(d_head, tile)
        d_values = trans_mul(low(probs), d_head)
        row_dot = jnp.sum(probs * d_probs, axis=-1, keepdims=True)
        d_scores = low(probs * (d_probs - row_dot) * scale)
        d_query = plain_mul(d_scores, key)
        d_key = trans_mul(d_scores, query)
        d_q_ref[:, lanes] = low(
            d_query * keep_ref[...]
            - lanes_on(d_query, ROPE // 2) * up_ref[...]
            - lanes_on(d_query, -(ROPE // 2)) * down_ref[...]
        )
        d_kv_ref[:, lanes] = low(jnp.where(lane < NOPE, d_key, d_values))
        d_rot += d_key
    d_rot_ref[...] = d_rot


def attend_specs(length):
    pair = pl.BlockSpec((length, 2 * LANES), lambda step: (0, step))
    single = pl.BlockSpec((length, LANES), lambda step: (0, step))
    table = pl.BlockSpec((length, LANES), lambda step: (0, 0))
    seen = pl.BlockSpec((length, length), lambda step: (0, 0))
    return pair, single, table, seen


def attend(query, key_value, rot_pad, seen, tables, scale):
    length, columns = query.shape
    pair, single, table, whole = attend_specs(length)
    return pl.pallas_call(
        partial(attend_kernel, scale),
        grid=(columns // (2 * LANES),),
        in_specs=[pair, pair, table, whole, table, table, table],
        out_specs=[single, pair],
        out_shape=[
            jax.ShapeDtypeStruct((length, columns // 2), jnp.bfloat16),
            jax.ShapeDtypeStruct((length, columns), jnp.bfloat16),
        ],
        compiler_params=pltpu.CompilerParams(vmem_limit_bytes=32 * 2**20),
        name="attend",
    )(query, key_value, rot_pad, seen, *tables)


def attend_back(query_full, key_value, rot_pad, seen, tables, d_heads, scale):
    length, columns = query_full.shape
    pair, single, table, whole = attend_specs(length)
    return pl.pallas_call(
        partial(attend_back_kernel, scale),
        grid=(columns // (2 * LANES),),
        in_specs=[pair, pair, table, whole, table, table, table, single],
        out_specs=[pair, pair, table],
        out_shape=[
            jax.ShapeDtypeStruct((length, columns), jnp.bfloat16),
            jax.ShapeDtypeStruct((length, columns), jnp.bfloat16),
            jax.ShapeDtypeStruct((length, LANES), jnp.float32),
        ],
        compiler_params=pltpu.CompilerParams(vmem_limit_bytes=32 * 2**20),
        name="attend_back",
    )(query_full, key_value, rot_pad, seen, *tables, d_heads)


def body(
    hidden_in,
    prefix_len,
    attn_gain,
    q_down,
    q_gain,
    kv_down,
    kv_gain,
    q_up,
    kv_up,
    o_proj,
    mlp_gain,
    w_gate,
    w_up,
    w_down,
    cotangent,
):
    tensor_count = lax.axis_size("tensor")
    tensor_rank = lax.axis_index("tensor")
    dp_count = lax.axis_size("dp")
    own_rows, width = hidden_in.shape
    q_rank = q_down.shape[1]
    rank = q_rank + KR
    down_rows = q_down.shape[0]
    q_share, kv_share = q_gain.shape[0], kv_gain.shape[0]
    q_rows, kv_rows = q_up.shape[0], kv_up.shape[0]
    head_qk = NOPE + ROPE
    heads_local = q_up.shape[1] // head_qk
    scale = head_qk ** (-0.5)
    links = Links()
    width_origins = block_origins(width)
    to_order = one_hot(width_origins, width)
    units = w_gate.shape[1]
    share = round_up(units // GROUP, LANES)

    down_columns = rank + ROPE
    packed_columns = round_up(down_columns + 3, LANES)

    def column_of(gain):
        return jnp.pad(gain, (0, down_rows - gain.shape[0]))[:, None]

    packed = jnp.concatenate(
        [
            q_down,
            kv_down,
            column_of(attn_gain),
            column_of(mlp_gain),
            column_of(jnp.concatenate([q_gain, kv_gain])),
            jnp.zeros((down_rows, packed_columns - down_columns - 3), jnp.bfloat16),
        ],
        axis=1,
    )
    others = other_bits(GROUP_BITS)
    near_first = (NEAR,) + tuple(bit for bit in others if bit != NEAR)
    back_flow = links.flow(
        "G",
        gather_whole_tokens(
            (RESID * cotangent.astype(jnp.float32)).astype(jnp.bfloat16), to_order
        ),
    )
    down_flow = links.flow("A", gather_dp_direct(packed)).step()
    back_flow.step()
    q_padded = low(plain_mul(q_up, pad_heads(q_up.shape[1], head_qk)))
    up_flow = links.flow("B", gather_dp(jnp.concatenate([q_padded, kv_up], axis=0))).step().step()
    down_flow.step()
    up_flow.step()
    out_flow = links.flow("C", gather_dp(o_proj.T)).step().step().step()
    core_packed = down_flow.end().reshape(dp_count, down_rows, packed_columns)
    unit_parts = []
    unit_picks = pick_group(
        jnp.concatenate(
            [
                cut_units(item, share)
                for item in tied((w_gate, w_up, w_down.T), links.named(["B0"]))
            ],
            axis=-1,
        )
    )
    exchange_flow = links.flow("U", exchange_group(unit_picks, unit_parts))
    exchange_flow.step().step().step()
    first_flow = links.flow("V", gather_bits(unit_parts[0], near_first, "first")).step()
    up_flow.step()
    up_flow.step()
    other_packed = core_swap(core_packed)
    is_first = tensor_rank == 0
    all_packed = jnp.stack(
        [
            jnp.where(is_first, core_packed, other_packed),
            jnp.where(is_first, other_packed, core_packed),
        ],
        axis=1,
    ).reshape(width, packed_columns)

    rank_block = q_rows + kv_rows
    place = jnp.arange(rank, dtype=jnp.int32)
    device_of = block_origins(rank) // rank_block
    in_block = place % rank_block
    is_query = in_block < q_rows
    rank_order = one_hot(
        jnp.where(
            is_query,
            device_of * q_rows + in_block,
            q_rank + device_of * kv_rows + in_block - q_rows,
        ),
        rank,
    )
    hidden_low, cotangent_low = tied((hidden_in, cotangent), links.named(["A0"]))
    moved_in = plain_mul(jnp.concatenate([hidden_low, cotangent_low], axis=0), to_order)
    resid_in, grad_out = moved_in[:own_rows], moved_in[own_rows:]
    device_place = width_origins // down_rows
    in_share = width_origins % down_rows
    gain_order = one_hot(
        jnp.where(
            in_share < q_share,
            device_place * q_share + in_share,
            jnp.where(
                in_share < q_share + kv_share,
                q_rank + device_place * kv_share + in_share - q_share,
                -1,
            ),
        ),
        rank,
    )
    gains = all_packed[:, down_columns : down_columns + 3].T
    gain_attn = wide(gains[0])
    gain_mlp = wide(gains[1])
    gain_rank = mul_trans(gains[2:3], gain_order)[0]
    gain_q, gain_kv = gain_rank[:q_rank], gain_rank[q_rank:]

    x_normed = norm_apply(resid_in, gain_attn).astype(jnp.bfloat16)
    latents = plain_mul(x_normed, all_packed)
    q_latent = latents[:, :q_rank]
    kv_latent = latents[:, q_rank:rank]
    rot_latent = latents[:, rank:down_columns]
    q_normed = norm_apply(q_latent, gain_q).astype(jnp.bfloat16)
    kv_normed = norm_apply(kv_latent, gain_kv).astype(jnp.bfloat16)
    own_pos = tensor_rank * own_rows + jnp.arange(own_rows, dtype=jnp.int32)
    other_pos = (1 - tensor_rank) * own_rows + jnp.arange(own_rows, dtype=jnp.int32)
    positions = jnp.concatenate([own_pos, other_pos])
    k_rotary = rotate(rot_latent, own_pos).astype(jnp.bfloat16)
    ranks_normed = low(plain_mul(jnp.concatenate([q_normed, kv_normed], axis=-1), rank_order))
    rot_pad = jnp.pad(k_rotary, ((0, 0), (NOPE, LANES - head_qk)))
    latent_seq = pair_tokens(jnp.concatenate([ranks_normed, rot_pad], axis=-1))
    links.done["latents"] = latent_seq
    first_flow.step()
    up_flow.step().step()
    up_weight = up_flow.end()
    first_flow.step()
    out_flow.step().step()
    last_flow = links.flow("W", gather_bits(unit_parts[1], near_first, "both")).step()
    back_flow.step().step()
    mlp_back = back_flow.end()
    out_flow.step().step()
    out_trans = out_flow.end()
    last_flow.step()
    rank_seq = latent_seq[:, :rank]
    rot_seq = latent_seq[:, rank:]
    zero = jnp.zeros((), jnp.bfloat16)
    q_seq = jnp.where(is_query[None, :], rank_seq, zero)
    kv_seq = jnp.where(is_query[None, :], zero, rank_seq)
    query = plain_mul(q_seq, up_weight)
    key_value = low(plain_mul(kv_seq, up_weight))
    visible = (positions[None, :] <= positions[:, None]) | (positions[None, :] < prefix_len[0])
    seen = visible.astype(jnp.float32)
    tables = turn_tables(positions)
    heads_low, query_full = attend(query, key_value, rot_seq, seen, tables, scale)
    attn_own = split_pair(mul_trans(heads_low, tied(out_trans, links.named(["G2"]))))
    mid_resid = resid_in + RESID * attn_own
    mlp_normed = norm_apply(mid_resid, gain_mlp).astype(jnp.bfloat16)

    mlp_flow = links.flow("M", gather_tokens(mlp_normed)).step().step()
    mlp_seq = mlp_flow.end()
    last_flow.step().step()
    first_units, last_units = first_flow.end(), last_flow.end()
    unit_pieces = [
        piece.reshape(-1, 3 * share)
        for mask in masks_of(others)
        for piece in first_units[mask] + last_units[mask]
    ]
    if any(piece.shape[0] % 16 for piece in unit_pieces):
        unit_pieces = [jnp.concatenate(unit_pieces)]
    act_low, d_units, d_mlp_terms, mlp_terms = run_units(mlp_seq, mlp_back, unit_pieces, share)
    chip_rows = GROUP * own_rows
    d_mlp_other = core_swap(d_mlp_terms[chip_rows:])
    d_mlp_flow = links.flow("D", return_tokens(d_mlp_terms[:chip_rows], d_mlp_other, own_rows))
    d_mlp_flow.step().step().step()
    d_mlp_own = d_mlp_flow.end()
    unit_grad = unit_grads(
        mlp_seq, mlp_back, tied(act_low, [d_mlp_other]), d_units, share
    ).reshape(len(masks_of(others)), GROUP, -1, 3 * share)
    unit_flow = links.flow(
        "R", reduce_bits(lambda mask: unit_grad[masks_of(others).index(mask)], others, "both")
    )
    unit_flow.step(["D1", "D2"]).step()
    mlp_flow = links.flow(
        "O",
        return_tokens(
            mlp_terms[:chip_rows],
            core_swap(tied(mlp_terms, [d_mlp_other])[chip_rows:]),
            own_rows,
        ),
    )

    _, mlp_norm_back = jax.vjp(norm_apply, mid_resid, gain_mlp)
    d_mid_norm, _ = mlp_norm_back(d_mlp_own)
    mid_inverse = lax.rsqrt(jnp.mean(mid_resid * mid_resid, axis=-1, keepdims=True) + EPS)
    gain_mlp_terms = d_mlp_own * mid_resid * mid_inverse
    d_mid = grad_out + d_mid_norm
    attn_back = pair_tokens((RESID * d_mid).astype(jnp.bfloat16))
    d_heads = low(plain_mul(attn_back, out_trans))
    out_grad = trans_mul(attn_back, heads_low)
    out_flow = links.flow("P", reduce_dp(out_grad)).step().step()
    unit_flow.step().step()
    out_flow.step()
    mlp_flow.step().step().step()
    d_query, d_key_value, d_rot = attend_back(
        query_full, key_value, rot_seq, seen, tables, tied(d_heads, links.named(["R0"]) + [out_grad]), scale
    )
    d_query, d_key_value, d_rot = tied((d_query, d_key_value, d_rot), links.named(["R1"]))
    d_rank = jnp.where(
        is_query[None, :], mul_trans(d_query, up_weight), mul_trans(d_key_value, up_weight)
    )
    d_latent_own = split_pair(jnp.concatenate([d_rank, d_rot], axis=-1))
    d_rank_own = move_columns(d_latent_own[:, :rank], rank_order, True, 2)
    d_q_own, d_kv_own = d_rank_own[:, :q_rank], d_rank_own[:, q_rank:]
    d_rot_own = d_latent_own[:, rank + NOPE : rank + head_qk]
    up_flow = links.flow(
        "Q",
        reduce_dp(
            trans_mul(
                jnp.concatenate([q_seq, kv_seq], axis=0),
                jnp.concatenate([d_query, d_key_value], axis=0),
            )
        ),
    )
    unit_sum = unit_flow.end()
    unit_parts = []
    exchange_flow = links.flow(
        "S", exchange_group([low(unit_sum[at]) for at in range(GROUP)], unit_parts)
    )
    exchange_flow.step().step()
    out_flow.step()
    exchange_flow.step()
    up_flow.step().step().step().step()
    out_flow.step().step()
    out_shard = out_flow.end().T

    _, q_norm_back = jax.vjp(norm_apply, q_latent, gain_q)
    d_q_latent, _ = q_norm_back(d_q_own)
    _, kv_norm_back = jax.vjp(norm_apply, kv_latent, gain_kv)
    d_kv_latent, _ = kv_norm_back(d_kv_own)
    q_inverse = lax.rsqrt(jnp.mean(q_latent * q_latent, axis=-1, keepdims=True) + EPS)
    kv_inverse = lax.rsqrt(jnp.mean(kv_latent * kv_latent, axis=-1, keepdims=True) + EPS)
    gain_rank_terms = low(
        jnp.concatenate(
            [d_q_own * q_latent * q_inverse, d_kv_own * kv_latent * kv_inverse], axis=-1
        )
    )
    d_rot_raw = rotate_back(rot_latent, own_pos, d_rot_own)
    d_latents = low(
        jnp.concatenate(
            [
                d_q_latent,
                d_kv_latent,
                d_rot_raw,
                jnp.zeros((own_rows, packed_columns - down_columns), jnp.float32),
            ],
            axis=-1,
        )
    )
    d_x_normed = mul_trans(d_latents, all_packed)
    _, x_norm_back = jax.vjp(norm_apply, resid_in, gain_attn)
    d_x_norm, _ = x_norm_back(d_x_normed)
    x_inverse = lax.rsqrt(jnp.mean(resid_in * resid_in, axis=-1, keepdims=True) + EPS)
    gain_attn_terms = d_x_normed * resid_in * x_inverse
    grad_input = move_columns(d_mid + d_x_norm, to_order, True, 3)

    kind = jnp.arange(3 * own_rows, dtype=jnp.int32)[:, None] // own_rows + down_columns
    markers = (jnp.arange(packed_columns, dtype=jnp.int32)[None, :] == kind).astype(jnp.bfloat16)
    grad_packed = trans_mul(
        jnp.concatenate(
            [
                x_normed,
                low(gain_attn_terms),
                low(gain_mlp_terms),
                low(plain_mul(gain_rank_terms, gain_order)),
            ],
            axis=0,
        ),
        jnp.concatenate([d_latents, markers], axis=0),
    ).reshape(dp_count, tensor_count, down_rows, packed_columns)
    keep = jnp.where(is_first, grad_packed[:, 0], grad_packed[:, 1])
    give = jnp.where(is_first, grad_packed[:, 1], grad_packed[:, 0])
    keep = keep + wide(core_swap(low(give)))
    up_flow.step()
    down_flow = links.flow("T", reduce_dp_direct(keep.reshape(dp_count * down_rows, packed_columns)))
    down_flow.step()
    up_flow.step().step()
    up_shard = up_flow.end()
    packed_shard = down_flow.end()
    qup_shard = up_shard[:q_rows].reshape(q_rows, heads_local, LANES)[..., :head_qk]
    kvup_shard = up_shard[q_rows:]
    exchange_flow.end()
    unit_parts = tied(unit_parts, links.named(["Q3"]))
    unit_shards = place_group([part[at] for part in unit_parts for at in range(GROUP // 2)])
    gate_shard = join_units(unit_shards[..., :share], units)
    upper_shard = join_units(unit_shards[..., share : 2 * share], units)
    down_shard = join_units(unit_shards[..., 2 * share :], units).T
    mlp_own = mlp_flow.end()
    layer_out = low(mul_trans(low(mid_resid + RESID * mlp_own), to_order))
    gain_shards = packed_shard[:, down_columns : down_columns + 3].T

    return (
        layer_out,
        grad_input,
        gain_shards[0],
        packed_shard[:, :q_rank],
        gain_shards[2, :q_share],
        packed_shard[:, q_rank:down_columns],
        gain_shards[2, q_share : q_share + kv_share],
        qup_shard.reshape(q_up.shape),
        kvup_shard,
        out_shard,
        gain_shards[1],
        gate_shard,
        upper_shard,
        down_shard,
    )


def solution(mesh):
    return jax.shard_map(
        body,
        mesh=mesh,
        in_specs=(
            P(("dp", "tensor"), None),
            P("dp"),
            P(("dp", "tensor")),
            P(("dp", "tensor"), None),
            P(("dp", "tensor")),
            P(("dp", "tensor"), None),
            P(("dp", "tensor")),
            P("dp", "tensor"),
            P("dp", "tensor"),
            P("tensor", "dp"),
            P(("dp", "tensor")),
            P("dp", "tensor"),
            P("dp", "tensor"),
            P("tensor", "dp"),
            P(("dp", "tensor"), None),
        ),
        out_specs=(
            P(("dp", "tensor"), None),
            P(("dp", "tensor"), None),
            P(("dp", "tensor")),
            P(("dp", "tensor"), None),
            P(("dp", "tensor")),
            P(("dp", "tensor"), None),
            P(("dp", "tensor")),
            P("dp", "tensor"),
            P("dp", "tensor"),
            P("tensor", "dp"),
            P(("dp", "tensor")),
            P("dp", "tensor"),
            P("dp", "tensor"),
            P("tensor", "dp"),
        ),
        check_vma=False,
    )
```

```python
from functools import partial
import math

import jax
import jax.numpy as jnp
from jax import lax
from jax.experimental import pallas as pl
from jax.experimental.pallas import tpu as pltpu
from jax.sharding import PartitionSpec as P

NOPE = 64
ROPE = 32
VD = 64
KR = 256
LANES = 128
GROUP_BITS = (2, 8)
LAST_BITS = (1, 2)
NEAR, FAR = 4, 8
GROUP = 4


EPS = 1e-05
RESID = 1.4 / math.sqrt(62.0)
THETA = 10000.0
NEG_FILL = -1e30


def norm_apply(values, gain):
    inverse = lax.rsqrt(jnp.mean(values * values, axis=-1, keepdims=True) + EPS)
    return values * inverse * gain


def rotate(values, positions):
    width_half = values.shape[-1] // 2
    frequency = THETA ** (-2.0 * jnp.arange(width_half, dtype=jnp.float32) / values.shape[-1])
    angles = positions.astype(jnp.float32)[:, None] * frequency[None, :]
    extra_dims = (1,) * (values.ndim - 2)
    cosine = jnp.cos(angles).reshape(angles.shape[:1] + extra_dims + angles.shape[1:])
    sine = jnp.sin(angles).reshape(angles.shape[:1] + extra_dims + angles.shape[1:])
    lower_part = values[..., :width_half]
    upper_part = values[..., width_half:]
    return jnp.concatenate(
        [lower_part * cosine - upper_part * sine, upper_part * cosine + lower_part * sine], axis=-1
    )


def rotate_back(values, positions, grads):
    _, pullback = jax.vjp(partial(rotate, positions=positions), values)
    return pullback(grads)[0]


def plain_mul(left, right):
    return jnp.dot(left, right, preferred_element_type=jnp.float32)


def mul_trans(left, right):
    return lax.dot_general(
        left, right, (((1,), (1,)), ((), ())), preferred_element_type=jnp.float32
    )


def trans_mul(left, right):
    return lax.dot_general(
        left, right, (((0,), (0,)), ((), ())), preferred_element_type=jnp.float32
    )


def low(values):
    return values.astype(jnp.bfloat16)


def wide(values):
    return values.astype(jnp.float32)


def core_swap(values):
    return lax.ppermute(values, "tensor", [(0, 1), (1, 0)])


def all_bits():
    count = lax.axis_size("dp")
    return tuple(1 << at for at in range(count.bit_length() - 1))


def other_bits(bits):
    return tuple(bit for bit in all_bits() if bit not in bits)


def masks_of(bits):
    masks = [0]
    for bit in bits:
        masks += [mask | bit for mask in masks]
    return masks


def by_count(bits):
    return sorted(masks_of(bits)[1:], key=lambda mask: bin(mask).count("1"))


def group_place():
    place = lax.axis_index("dp")
    return sum(((place // bit) % 2) << at for at, bit in enumerate(GROUP_BITS))


def tied(values, others):
    return lax.optimization_barrier((values, others))[0] if others else values


AFTER = {
    "A1": ("B0", "B1"),
    "C1": ("B0",),
    "U0": ("B2", "C0", "C1"),
    "B3": ("C0", "C1"),
    "B4": ("C2",),
    "B5": ("latents", "V1"),
    "B6": ("latents",),
    "G1": ("B5", "B6"),
    "C5": ("G1", "V2"),
    "C6": ("G1", "V2"),
    "M0": ("G2",),
    "M1": ("G2",),
    "M2": ("W1",),
    "W2": ("M1",),
    "W3": ("M1",),
    "R1": ("D1",),
    "R2": ("D2", "D1"),
    "R3": ("D2", "D1"),
    "P0": ("D2", "D1"),
    "P1": ("R0",),
    "P2": ("R1",),
    "O0": ("R1",),
    "Q0": ("P2", "R2"),
    "Q1": ("R2",),
    "T0": ("Q3",),
}


FREE = ("T1",)


class Flow:
    def __init__(self, links, name, routine):
        self.links, self.name, self.routine = links, name, routine
        self.count, self.result, self.given = 0, None, None
        self.wanted = self.resume(None)

    def resume(self, given):
        try:
            return self.routine.send(given)
        except StopIteration as end:
            self.result = end.value
            return None

    def step(self, hold=()):
        if self.wanted is None:
            return self
        name = self.name + str(self.count)
        got = self.links.send(*self.wanted, AFTER.get(name, ()), name not in FREE)
        self.links.sent[name] = self.wanted[0]
        self.links.done[name] = got
        self.count += 1
        self.wanted = self.resume(tied(got, self.links.named(hold)))
        return self

    def end(self):
        while self.wanted is not None:
            self.step()
        return self.result


class Links:
    def __init__(self):
        self.last = {}
        self.done = {}
        self.sent = {}

    def named(self, names):
        return [self.done[name] for name in names if name in self.done]

    def send(self, values, mask, after=(), in_line=True):
        masks = mask if isinstance(mask, list) else [mask]
        bits = sorted({bit for item in masks for bit in all_bits() if bit & item})
        before = self.named(after)
        if in_line:
            before += [self.last[bit] for bit in bits if bit in self.last]
        values = tied(values, before)
        count = lax.axis_size("dp")
        got = [
            lax.ppermute(item, "dp", [(place, place ^ to) for place in range(count)])
            for item, to in zip(values if mask is masks else [values], masks)
        ]
        got = got if mask is masks else got[0]
        self.last.update({bit: got for bit in bits})
        return got

    def flow(self, name, routine):
        return Flow(self, name, routine)


def routes(mask, bits, split):
    ordered = [bit for bit in bits if bit & mask]
    if len(ordered) > 1 and split == "both":
        return [(ordered[0], 0), (ordered[-1], 1)]
    return [(ordered[-1 if split == "last" else 0], None)]


def halves(values):
    half = values.shape[0] // 2
    return values[:half], values[half:]


def gather_bits(values, bits, split):
    known = {0: [values]}
    for mask in by_count(bits):
        pieces = []
        for bit, part in routes(mask, bits, split):
            source = known[mask ^ bit]
            if part is None:
                moving = source[0] if len(source) == 1 else jnp.concatenate(source)
            else:
                moving = halves(source[0])[part] if len(source) == 1 else source[part]
            pieces.append((yield moving, bit))
        known[mask] = pieces
    return known


def reduce_bits(block_of, bits, split, arrive=lambda values, bit: values):
    added = {mask: [] for mask in masks_of(bits)}

    def summed(mask, part):
        values = block_of(mask)
        if part is not None:
            values = halves(values)[part]
        if added[mask]:
            values = wide(values)
        for held, extra in added[mask]:
            if part is None or part == held:
                values = values + wide(extra)
            elif held is None:
                values = values + wide(halves(extra)[part])
        return values

    def whole(mask):
        if any(held is not None for held, _ in added[mask]):
            return [summed(mask, 0), summed(mask, 1)]
        return [summed(mask, None)]

    for mask in reversed(by_count(bits)):
        for bit, part in routes(mask, bits, split):
            if part is None:
                parts = [low(item) for item in whole(mask)]
                moving = parts[0] if len(parts) == 1 else jnp.concatenate(parts)
            else:
                moving = low(summed(mask, part))
            got = yield moving, bit
            added[mask ^ bit].append((part, arrive(got, bit)))
    parts = whole(0)
    return parts[0] if len(parts) == 1 else jnp.concatenate(parts)


def row_order():
    return [
        other | group for other in masks_of(other_bits(GROUP_BITS)) for group in masks_of(GROUP_BITS)
    ]


def first_bits():
    return other_bits(LAST_BITS)


def gather_dp(values):
    first = masks_of(first_bits())
    known = yield from gather_bits(values, first_bits(), "first")
    column = jnp.stack([known[mask][0] for mask in first])
    known = yield from gather_bits(column, LAST_BITS, "both")
    half = len(first) // 2

    def block(mask):
        at = first.index(mask & ~sum(LAST_BITS))
        pieces = known[mask & sum(LAST_BITS)]
        return pieces[0][at] if len(pieces) == 1 else pieces[at // half][at % half]

    return jnp.concatenate([block(mask) for mask in row_order()], axis=0)


def gather_dp_direct(values):
    first, last = masks_of(first_bits()), masks_of(LAST_BITS)
    got = yield [values] * (len(first) - 1), first[1:]
    column = jnp.stack([values] + got)
    got = yield [column] * (len(last) - 1), last[1:]
    known = dict(zip(last, [column] + got))
    return jnp.concatenate(
        [known[mask & sum(LAST_BITS)][first.index(mask & ~sum(LAST_BITS))] for mask in row_order()],
        axis=0,
    )


def reduce_dp_direct(grad):
    order, first, last = row_order(), masks_of(first_bits()), masks_of(LAST_BITS)
    blocks = grad.reshape(len(order), -1, grad.shape[1])
    columns = [jnp.stack([blocks[order.index(mask | item)] for item in first]) for mask in last]
    got = yield [low(column) for column in columns[1:]], last[1:]
    column = columns[0] + sum(wide(item) for item in got)
    got = yield [low(column[at]) for at in range(1, len(first))], first[1:]
    return column[0] + sum(wide(item) for item in got)


def reduce_dp(grad):
    order = row_order()
    blocks = grad.reshape(len(order), -1, grad.shape[1])
    first = masks_of(first_bits())

    def column(last):
        return jnp.stack([blocks[order.index(last | mask)] for mask in first])

    partial_sum = yield from reduce_bits(column, LAST_BITS, "both")
    return (
        yield from reduce_bits(lambda mask: partial_sum[first.index(mask)], first_bits(), "first")
    )


def place_kernel(place_ref, *refs):
    out_ref = refs[-1]
    for step, ref in enumerate(refs[:-1]):

        @pl.when(pl.program_id(0) == step)
        def _():
            out_ref[0] = ref[...]


def pick_kernel(place_ref, values_ref, *out_refs):
    for step, ref in enumerate(out_refs):

        @pl.when(pl.program_id(0) == step)
        def _():
            ref[...] = values_ref[0]


def place_index():
    return group_place().reshape(1).astype(jnp.int32)


def place_group(blocks):
    rows, width = blocks[0].shape
    return pl.pallas_call(
        place_kernel,
        grid_spec=pltpu.PrefetchScalarGridSpec(
            num_scalar_prefetch=1,
            grid=(GROUP,),
            in_specs=[pl.BlockSpec((rows, width), lambda step, place: (0, 0))] * GROUP,
            out_specs=pl.BlockSpec(
                (1, rows, width), lambda step, place: (lax.bitwise_xor(place[0], step), 0, 0)
            ),
        ),
        out_shape=jax.ShapeDtypeStruct((GROUP, rows, width), blocks[0].dtype),
        compiler_params=pltpu.CompilerParams(vmem_limit_bytes=32 * 2**20),
        name="place_group",
    )(place_index(), *blocks)


def pick_group(values):
    _, rows, width = values.shape
    blocks = pl.pallas_call(
        pick_kernel,
        grid_spec=pltpu.PrefetchScalarGridSpec(
            num_scalar_prefetch=1,
            grid=(GROUP,),
            in_specs=[
                pl.BlockSpec(
                    (1, rows, width), lambda step, place: (lax.bitwise_xor(place[0], step), 0, 0)
                )
            ],
            out_specs=[pl.BlockSpec((rows, width), lambda step, place: (0, 0))] * GROUP,
        ),
        out_shape=[jax.ShapeDtypeStruct((rows, width), values.dtype)] * GROUP,
        compiler_params=pltpu.CompilerParams(vmem_limit_bytes=32 * 2**20),
        name="pick_group",
    )(place_index(), values)
    return list(blocks)


def exchange_group(blocks, arrived):
    near, far = GROUP_BITS
    there = yield jnp.stack([blocks[1], blocks[3]]), near
    arrived.append(jnp.stack([blocks[0], there[0]]))
    across = yield blocks[2], far
    relayed = yield there[1], far
    arrived.append(jnp.stack([across, relayed]))


def cut_units(weight, share):
    rows, units = weight.shape
    cut = jnp.moveaxis(weight.reshape(rows, GROUP, units // GROUP), 1, 0)
    return jnp.pad(cut, ((0, 0), (0, 0), (0, share - units // GROUP)))


def join_units(pieces, units):
    rows = pieces.shape[1]
    return wide(jnp.moveaxis(pieces[..., : units // GROUP], 0, 1)).reshape(rows, units)


CHUNKS = 4


def reorder_kernel(steps, block, *refs):
    width = refs[0].shape[-1]
    chunk = width // CHUNKS
    for at, step in enumerate(steps):
        source, target = refs[at], refs[-1].at[at]
        if not step:
            target[...] = source[...]
            continue
        row = lax.broadcasted_iota(jnp.int32, (chunk, chunk), 0)
        column = lax.broadcasted_iota(jnp.int32, (chunk, chunk), 1)
        index = lax.rem(lax.div(column, block), GROUP)
        origin = column + (lax.bitwise_xor(index, step) - index) * block
        moved = jnp.where(row == origin, 1.0, 0.0).astype(jnp.bfloat16)
        for part in range(CHUNKS):
            columns = slice(part * chunk, (part + 1) * chunk)
            target[:, columns] = low(plain_mul(source[:, columns], moved))


def reorder(arrays, steps):
    rows, width = arrays[0].shape
    return pl.pallas_call(
        partial(reorder_kernel, tuple(steps), width // lax.axis_size("dp")),
        out_shape=jax.ShapeDtypeStruct((len(steps), rows, width), arrays[0].dtype),
        compiler_params=pltpu.CompilerParams(vmem_limit_bytes=32 * 2**20),
        name="reorder",
    )(*arrays)


def gather_tokens(values, held):
    known = yield from gather_bits(values, GROUP_BITS, "first")
    own = reorder([known[mask][0] for mask in masks_of(GROUP_BITS)], range(GROUP))
    own = tied(own.reshape(-1, values.shape[1]), held)
    return own, core_swap(own)


def gather_whole_tokens(values, to_order):
    known = yield from gather_bits(values, GROUP_BITS, "last")
    own = jnp.concatenate([known[mask][0] for mask in masks_of(GROUP_BITS)], axis=0)
    own = low(plain_mul(own, to_order))
    return own, core_swap(own)


def return_tokens(mine, others, rows):
    chip_sum = (wide(mine) + wide(others)).reshape(GROUP, rows, -1)
    masks = masks_of(GROUP_BITS)
    return reduce_bits(
        lambda mask: chip_sum[masks.index(mask)],
        GROUP_BITS,
        "first",
        lambda got, bit: reorder([got], [masks.index(bit)])[0],
    )


def units_kernel(
    share, count, own_ref, other_ref, own_back_ref, other_back_ref, *refs
):
    pieces, (act_ref, d_units_ref, d_in_ref, out_ref, weight_ref, sems) = refs[:count], refs[count:]
    step = pl.program_id(0)

    @pl.when(step == 0)
    def _():
        copies, start = [], 0
        for at, piece in enumerate(pieces):
            rows = piece.shape[0]
            copies.append(
                pltpu.make_async_copy(piece, weight_ref.at[pl.ds(start, rows)], sems.at[at])
            )
            start += rows
        for copy in copies:
            copy.start()
        for copy in copies:
            copy.wait()

    is_own = step < pl.num_programs(0) // 2
    tokens = jnp.where(is_own, own_ref[...], other_ref[...])
    back = jnp.where(is_own, own_back_ref[...], other_back_ref[...])
    gate_cut, up_cut = slice(0, share), slice(share, 2 * share)
    down_cut = slice(2 * share, 3 * share)
    gate = plain_mul(tokens, weight_ref[:, gate_cut])
    upper = plain_mul(tokens, weight_ref[:, up_cut])
    d_act = plain_mul(back, weight_ref[:, down_cut])
    slope = 1.0 / (1.0 + jnp.exp(-gate))
    swished = gate * slope
    act = low(swished * upper)
    act_ref[...] = act
    d_units_ref[:, gate_cut] = low(d_act * upper * (slope + swished * (1.0 - slope)))
    d_units_ref[:, up_cut] = low(d_act * swished)
    d_in_ref[...] = low(mul_trans(d_units_ref[...], weight_ref[:, : 2 * share]))
    out_ref[...] = low(mul_trans(act, weight_ref[:, down_cut]))


def run_units(tokens, back, pieces, share):
    own, other = tokens
    rows, width = own.shape
    steps = 4
    block = 2 * rows // steps
    half = steps // 2
    in_own = pl.BlockSpec((block, width), lambda step: (jnp.minimum(step, half - 1), 0))
    in_other = pl.BlockSpec((block, width), lambda step: (jnp.maximum(step - half, 0), 0))
    many = pl.BlockSpec(memory_space=pl.ANY)

    def out_spec(columns):
        return pl.BlockSpec((block, columns), lambda step: (step, 0))

    columns = (share, 2 * share, width, width)
    return pl.pallas_call(
        partial(units_kernel, share, len(pieces)),
        grid=(steps,),
        in_specs=[in_own, in_other, in_own, in_other] + [many] * len(pieces),
        out_specs=[out_spec(item) for item in columns],
        out_shape=[jax.ShapeDtypeStruct((2 * rows, item), jnp.bfloat16) for item in columns],
        scratch_shapes=[
            pltpu.VMEM((width, 3 * share), jnp.bfloat16),
            pltpu.SemaphoreType.DMA((len(pieces),)),
        ],
        compiler_params=pltpu.CompilerParams(vmem_limit_bytes=56 * 2**20),
        name="run_units",
    )(own, other, *back, *pieces)


def unit_grads_kernel(share, own_ref, other_ref, own_back_ref, other_back_ref, act_ref, d_units_ref, out_ref):
    tokens = jnp.concatenate([own_ref[...], other_ref[...]], axis=0)
    out_ref[:, : 2 * share] = low(trans_mul(tokens, d_units_ref[...]))
    back = jnp.concatenate([own_back_ref[...], other_back_ref[...]], axis=0)
    out_ref[:, 2 * share :] = low(trans_mul(back, act_ref[...]))


def unit_grads(tokens, back, act, d_units, share):
    rows, width = tokens[0].shape
    chunk = width // CHUNKS
    part = pl.BlockSpec((rows, chunk), lambda step: (0, step))
    return pl.pallas_call(
        partial(unit_grads_kernel, share),
        grid=(CHUNKS,),
        in_specs=[part] * 4
        + [pl.BlockSpec(act.shape, lambda step: (0, 0)), pl.BlockSpec(d_units.shape, lambda step: (0, 0))],
        out_specs=pl.BlockSpec((chunk, 3 * share), lambda step: (step, 0)),
        out_shape=jax.ShapeDtypeStruct((width, 3 * share), jnp.bfloat16),
        compiler_params=pltpu.CompilerParams(vmem_limit_bytes=56 * 2**20),
        name="unit_grads",
    )(*tokens, *back, act, d_units)


def pair_tokens(values):
    return jnp.concatenate([values, core_swap(values)], axis=0)


def split_pair(values):
    rows = values.shape[0] // 2
    return values[:rows] + wide(core_swap(low(values[rows:])))


def block_origins(total):
    order = row_order()
    block = total // len(order)
    place = jnp.arange(total, dtype=jnp.int32)
    index = place // block
    mask = jnp.zeros_like(index)
    for at, bit in enumerate(GROUP_BITS + other_bits(GROUP_BITS)):
        mask = mask + ((index >> at) % 2) * bit
    return (lax.axis_index("dp") ^ mask) * block + place % block


def one_hot(origins, size):
    return (jnp.arange(size, dtype=jnp.int32)[:, None] == origins[None, :]).astype(jnp.bfloat16)


def pad_heads(columns, head):
    column = jnp.arange(columns // head * LANES, dtype=jnp.int32)
    within = column % LANES
    return one_hot(jnp.where(within < head, column // LANES * head + within, -1), columns)


def in_parts(values, count):
    parts = []
    for _ in range(count):
        part = low(values)
        parts.append(part)
        values = values - wide(part)
    return parts


def move_columns(values, selector, transpose, count):
    rows = values.shape[0]
    stacked = jnp.concatenate(in_parts(values, count), axis=0)
    moved = mul_trans(stacked, selector) if transpose else plain_mul(stacked, selector)
    return sum(moved[at * rows : (at + 1) * rows] for at in range(count))


def round_up(size, step):
    return -(-size // step) * step


def turn_tables(positions):
    lane = jnp.arange(LANES, dtype=jnp.int32)[None, :]
    half = ROPE // 2
    frequency = THETA ** (-2.0 * ((lane - NOPE) % half).astype(jnp.float32) / ROPE)
    angles = positions.astype(jnp.float32)[:, None] * frequency
    in_first = (lane >= NOPE) & (lane < NOPE + half)
    in_last = (lane >= NOPE + half) & (lane < NOPE + ROPE)
    cosine, sine = jnp.cos(angles), jnp.sin(angles)
    keep = jnp.where(in_first | in_last, cosine, jnp.where(lane < NOPE, 1.0, 0.0))
    return keep, jnp.where(in_first, -sine, 0.0), jnp.where(in_last, sine, 0.0)


def lanes_on(values, step):
    return pltpu.roll(values, (-step) % LANES, 1)


def key_of(tile, k_rotary):
    lane = lax.broadcasted_iota(jnp.int32, tile.shape, 1)
    return jnp.where(lane < NOPE, tile, k_rotary)


def probs_of(query, key, visible, scale):
    scores = jnp.where(visible, mul_trans(query, key) * scale, NEG_FILL)
    exp_scores = jnp.exp(scores - jnp.max(scores, axis=-1, keepdims=True))
    return exp_scores / jnp.sum(exp_scores, axis=-1, keepdims=True)


def attend_kernel(scale, q_ref, kv_ref, rot_ref, seen_ref, keep_ref, up_ref, down_ref, out_ref, query_ref):
    visible = seen_ref[...] > 0.0
    outs = []
    for head in range(2):
        lanes = slice(head * LANES, (head + 1) * LANES)
        raw = q_ref[:, lanes]
        query = (
            raw * keep_ref[...]
            + lanes_on(raw, ROPE // 2) * up_ref[...]
            + lanes_on(raw, -(ROPE // 2)) * down_ref[...]
        ).astype(jnp.bfloat16)
        query_ref[:, lanes] = query
        tile = kv_ref[:, lanes]
        probs = probs_of(query, key_of(tile, rot_ref[...]), visible, scale)
        outs.append(plain_mul(probs.astype(jnp.bfloat16), tile))
    lane = lax.broadcasted_iota(jnp.int32, outs[0].shape, 1)
    out_ref[...] = jnp.where(lane < VD, pltpu.roll(outs[0], VD, 1), outs[1]).astype(jnp.bfloat16)


def attend_back_kernel(
    scale, query_ref, kv_ref, rot_ref, seen_ref, keep_ref, up_ref, down_ref, d_out_ref,
    d_q_ref, d_kv_ref, d_rot_ref,
):
    @pl.when(pl.program_id(0) == 0)
    def _():
        d_rot_ref[...] = jnp.zeros_like(d_rot_ref)

    visible = seen_ref[...] > 0.0
    d_pair = wide(d_out_ref[...])
    lane = lax.broadcasted_iota(jnp.int32, d_pair.shape, 1)
    d_rot = d_rot_ref[...]
    for head in range(2):
        lanes = slice(head * LANES, (head + 1) * LANES)
        query = query_ref[:, lanes]
        tile = kv_ref[:, lanes]
        key = key_of(tile, rot_ref[...])
        probs = probs_of(query, key, visible, scale)
        d_head = d_pair if head else pltpu.roll(d_pair, VD, 1)
        d_head = low(jnp.where(lane < NOPE, 0.0, d_head))
        d_probs = mul_trans(d_head, tile)
        d_values = trans_mul(low(probs), d_head)
        row_dot = jnp.sum(probs * d_probs, axis=-1, keepdims=True)
        d_scores = low(probs * (d_probs - row_dot) * scale)
        d_query = plain_mul(d_scores, key)
        d_key = trans_mul(d_scores, query)
        d_q_ref[:, lanes] = low(
            d_query * keep_ref[...]
            - lanes_on(d_query, ROPE // 2) * up_ref[...]
            - lanes_on(d_query, -(ROPE // 2)) * down_ref[...]
        )
        d_kv_ref[:, lanes] = low(jnp.where(lane < NOPE, d_key, d_values))
        d_rot += d_key
    d_rot_ref[...] = d_rot


def attend_specs(length):
    pair = pl.BlockSpec((length, 2 * LANES), lambda step: (0, step))
    single = pl.BlockSpec((length, LANES), lambda step: (0, step))
    table = pl.BlockSpec((length, LANES), lambda step: (0, 0))
    seen = pl.BlockSpec((length, length), lambda step: (0, 0))
    return pair, single, table, seen


def attend(query, key_value, rot_pad, seen, tables, scale):
    length, columns = query.shape
    pair, single, table, whole = attend_specs(length)
    return pl.pallas_call(
        partial(attend_kernel, scale),
        grid=(columns // (2 * LANES),),
        in_specs=[pair, pair, table, whole, table, table, table],
        out_specs=[single, pair],
        out_shape=[
            jax.ShapeDtypeStruct((length, columns // 2), jnp.bfloat16),
            jax.ShapeDtypeStruct((length, columns), jnp.bfloat16),
        ],
        compiler_params=pltpu.CompilerParams(vmem_limit_bytes=32 * 2**20),
        name="attend",
    )(query, key_value, rot_pad, seen, *tables)


def attend_back(query_full, key_value, rot_pad, seen, tables, d_heads, scale):
    length, columns = query_full.shape
    pair, single, table, whole = attend_specs(length)
    return pl.pallas_call(
        partial(attend_back_kernel, scale),
        grid=(columns // (2 * LANES),),
        in_specs=[pair, pair, table, whole, table, table, table, single],
        out_specs=[pair, pair, table],
        out_shape=[
            jax.ShapeDtypeStruct((length, columns), jnp.bfloat16),
            jax.ShapeDtypeStruct((length, columns), jnp.bfloat16),
            jax.ShapeDtypeStruct((length, LANES), jnp.float32),
        ],
        compiler_params=pltpu.CompilerParams(vmem_limit_bytes=32 * 2**20),
        name="attend_back",
    )(query_full, key_value, rot_pad, seen, *tables, d_heads)


def body(
    hidden_in,
    prefix_len,
    attn_gain,
    q_down,
    q_gain,
    kv_down,
    kv_gain,
    q_up,
    kv_up,
    o_proj,
    mlp_gain,
    w_gate,
    w_up,
    w_down,
    cotangent,
):
    tensor_count = lax.axis_size("tensor")
    tensor_rank = lax.axis_index("tensor")
    dp_count = lax.axis_size("dp")
    own_rows, width = hidden_in.shape
    q_rank = q_down.shape[1]
    rank = q_rank + KR
    down_rows = q_down.shape[0]
    q_share, kv_share = q_gain.shape[0], kv_gain.shape[0]
    q_rows, kv_rows = q_up.shape[0], kv_up.shape[0]
    head_qk = NOPE + ROPE
    heads_local = q_up.shape[1] // head_qk
    scale = head_qk ** (-0.5)
    links = Links()
    width_origins = block_origins(width)
    to_order = one_hot(width_origins, width)
    units = w_gate.shape[1]
    share = round_up(units // GROUP, LANES)

    down_columns = rank + ROPE
    packed_columns = round_up(down_columns + 3, LANES)

    def column_of(gain):
        return jnp.pad(gain, (0, down_rows - gain.shape[0]))[:, None]

    packed = jnp.concatenate(
        [
            q_down,
            kv_down,
            column_of(attn_gain),
            column_of(mlp_gain),
            column_of(jnp.concatenate([q_gain, kv_gain])),
            jnp.zeros((down_rows, packed_columns - down_columns - 3), jnp.bfloat16),
        ],
        axis=1,
    )
    others = other_bits(GROUP_BITS)
    near_first = (NEAR,) + tuple(bit for bit in others if bit != NEAR)
    back_flow = links.flow(
        "G",
        gather_whole_tokens(
            (RESID * cotangent.astype(jnp.float32)).astype(jnp.bfloat16), to_order
        ),
    )
    down_flow = links.flow("A", gather_dp_direct(packed)).step()
    back_flow.step()
    q_padded = low(plain_mul(q_up, pad_heads(q_up.shape[1], head_qk)))
    up_flow = links.flow("B", gather_dp(jnp.concatenate([q_padded, kv_up], axis=0))).step().step()
    down_flow.step()
    up_flow.step()
    out_flow = links.flow("C", gather_dp(o_proj.T)).step().step().step()
    core_packed = down_flow.end().reshape(dp_count, down_rows, packed_columns)
    unit_parts = []
    unit_picks = pick_group(
        jnp.concatenate(
            [
                cut_units(item, share)
                for item in tied((w_gate, w_up, w_down.T), links.named(["B0"]))
            ],
            axis=-1,
        )
    )
    exchange_flow = links.flow("U", exchange_group(unit_picks, unit_parts))
    exchange_flow.step().step().step()
    first_flow = links.flow("V", gather_bits(unit_parts[0], near_first, "first")).step()
    up_flow.step()
    up_flow.step()
    other_packed = core_swap(core_packed)
    is_first = tensor_rank == 0
    all_packed = jnp.stack(
        [
            jnp.where(is_first, core_packed, other_packed),
            jnp.where(is_first, other_packed, core_packed),
        ],
        axis=1,
    ).reshape(width, packed_columns)

    rank_block = q_rows + kv_rows
    place = jnp.arange(rank, dtype=jnp.int32)
    device_of = block_origins(rank) // rank_block
    in_block = place % rank_block
    is_query = in_block < q_rows
    rank_order = one_hot(
        jnp.where(
            is_query,
            device_of * q_rows + in_block,
            q_rank + device_of * kv_rows + in_block - q_rows,
        ),
        rank,
    )
    hidden_low, cotangent_low = tied((hidden_in, cotangent), links.named(["A0"]))
    moved_in = plain_mul(jnp.concatenate([hidden_low, cotangent_low], axis=0), to_order)
    resid_in, grad_out = moved_in[:own_rows], moved_in[own_rows:]
    device_place = width_origins // down_rows
    in_share = width_origins % down_rows
    gain_order = one_hot(
        jnp.where(
            in_share < q_share,
            device_place * q_share + in_share,
            jnp.where(
                in_share < q_share + kv_share,
                q_rank + device_place * kv_share + in_share - q_share,
                -1,
            ),
        ),
        rank,
    )
    gains = all_packed[:, down_columns : down_columns + 3].T
    gain_attn = wide(gains[0])
    gain_mlp = wide(gains[1])
    gain_rank = mul_trans(gains[2:3], gain_order)[0]
    gain_q, gain_kv = gain_rank[:q_rank], gain_rank[q_rank:]

    x_normed = norm_apply(resid_in, gain_attn).astype(jnp.bfloat16)
    latents = plain_mul(x_normed, all_packed)
    q_latent = latents[:, :q_rank]
    kv_latent = latents[:, q_rank:rank]
    rot_latent = latents[:, rank:down_columns]
    q_normed = norm_apply(q_latent, gain_q).astype(jnp.bfloat16)
    kv_normed = norm_apply(kv_latent, gain_kv).astype(jnp.bfloat16)
    own_pos = tensor_rank * own_rows + jnp.arange(own_rows, dtype=jnp.int32)
    other_pos = (1 - tensor_rank) * own_rows + jnp.arange(own_rows, dtype=jnp.int32)
    positions = jnp.concatenate([own_pos, other_pos])
    k_rotary = rotate(rot_latent, own_pos).astype(jnp.bfloat16)
    ranks_normed = low(plain_mul(jnp.concatenate([q_normed, kv_normed], axis=-1), rank_order))
    rot_pad = jnp.pad(k_rotary, ((0, 0), (NOPE, LANES - head_qk)))
    latent_seq = pair_tokens(jnp.concatenate([ranks_normed, rot_pad], axis=-1))
    links.done["latents"] = latent_seq
    first_flow.step()
    up_flow.step().step()
    up_weight = up_flow.end()
    first_flow.step()
    out_flow.step().step()
    last_flow = links.flow("W", gather_bits(unit_parts[1], near_first, "both")).step()
    back_flow.step().step()
    mlp_back = back_flow.end()
    out_flow.step().step()
    out_trans = out_flow.end()
    last_flow.step()
    rank_seq = latent_seq[:, :rank]
    rot_seq = latent_seq[:, rank:]
    zero = jnp.zeros((), jnp.bfloat16)
    q_seq = jnp.where(is_query[None, :], rank_seq, zero)
    kv_seq = jnp.where(is_query[None, :], zero, rank_seq)
    query = plain_mul(q_seq, up_weight)
    key_value = low(plain_mul(kv_seq, up_weight))
    visible = (positions[None, :] <= positions[:, None]) | (positions[None, :] < prefix_len[0])
    seen = visible.astype(jnp.float32)
    tables = turn_tables(positions)
    heads_low, query_full = attend(query, key_value, rot_seq, seen, tables, scale)
    attn_own = split_pair(mul_trans(heads_low, tied(out_trans, links.named(["G2"]))))
    mid_resid = resid_in + RESID * attn_own
    mlp_normed = norm_apply(mid_resid, gain_mlp).astype(jnp.bfloat16)

    mlp_flow = links.flow("M", gather_tokens(mlp_normed, links.named(["W0"]))).step().step()
    mlp_seq = mlp_flow.end()
    last_flow.step().step()
    first_units, last_units = first_flow.end(), last_flow.end()
    unit_pieces = [
        piece.reshape(-1, 3 * share)
        for mask in masks_of(others)
        for piece in first_units[mask] + last_units[mask]
    ]
    if any(piece.shape[0] % 16 for piece in unit_pieces):
        unit_pieces = [jnp.concatenate(unit_pieces)]
    act_low, d_units, d_mlp_terms, mlp_terms = run_units(mlp_seq, mlp_back, unit_pieces, share)
    chip_rows = GROUP * own_rows
    d_mlp_other = core_swap(d_mlp_terms[chip_rows:])
    d_mlp_flow = links.flow("D", return_tokens(d_mlp_terms[:chip_rows], d_mlp_other, own_rows))
    d_mlp_flow.step().step().step()
    d_mlp_own = d_mlp_flow.end()
    unit_grad = unit_grads(
        mlp_seq, mlp_back, tied(act_low, [d_mlp_other]), d_units, share
    ).reshape(len(masks_of(others)), GROUP, -1, 3 * share)
    unit_flow = links.flow(
        "R", reduce_bits(lambda mask: unit_grad[masks_of(others).index(mask)], others, "both")
    )
    unit_flow.step(["D1", "D2"]).step()
    mlp_flow = links.flow(
        "O",
        return_tokens(
            mlp_terms[:chip_rows],
            core_swap(tied(mlp_terms, [d_mlp_other])[chip_rows:]),
            own_rows,
        ),
    )

    _, mlp_norm_back = jax.vjp(norm_apply, mid_resid, gain_mlp)
    d_mid_norm, _ = mlp_norm_back(d_mlp_own)
    mid_inverse = lax.rsqrt(jnp.mean(mid_resid * mid_resid, axis=-1, keepdims=True) + EPS)
    gain_mlp_terms = d_mlp_own * mid_resid * mid_inverse
    d_mid = grad_out + d_mid_norm
    attn_back = pair_tokens((RESID * d_mid).astype(jnp.bfloat16))
    d_heads = low(plain_mul(attn_back, out_trans))
    out_grad = trans_mul(attn_back, heads_low)
    out_flow = links.flow("P", reduce_dp(out_grad)).step().step()
    unit_flow.step().step()
    out_flow.step()
    mlp_flow.step().step(["R3"]).step(["R3"])
    d_query, d_key_value, d_rot = attend_back(
        query_full, key_value, rot_seq, seen, tables, tied(d_heads, [links.sent["R0"], out_grad]), scale
    )
    d_query, d_key_value, d_rot = tied(
        (d_query, d_key_value, d_rot), links.named(["R1"]) + [links.sent["R3"]]
    )
    d_rank = jnp.where(
        is_query[None, :], mul_trans(d_query, up_weight), mul_trans(d_key_value, up_weight)
    )
    d_latent_own = split_pair(jnp.concatenate([d_rank, d_rot], axis=-1))
    d_rank_own = move_columns(d_latent_own[:, :rank], rank_order, True, 2)
    d_q_own, d_kv_own = d_rank_own[:, :q_rank], d_rank_own[:, q_rank:]
    d_rot_own = d_latent_own[:, rank + NOPE : rank + head_qk]
    up_flow = links.flow(
        "Q",
        reduce_dp(
            trans_mul(
                jnp.concatenate([q_seq, kv_seq], axis=0),
                jnp.concatenate([d_query, d_key_value], axis=0),
            )
        ),
    )
    unit_sum = unit_flow.end()
    unit_parts = []
    exchange_flow = links.flow(
        "S", exchange_group([low(unit_sum[at]) for at in range(GROUP)], unit_parts)
    )
    exchange_flow.step().step()
    out_flow.step()
    exchange_flow.step()
    up_flow.step().step().step().step()
    out_flow.step().step()
    out_shard = out_flow.end().T

    _, q_norm_back = jax.vjp(norm_apply, q_latent, gain_q)
    d_q_latent, _ = q_norm_back(d_q_own)
    _, kv_norm_back = jax.vjp(norm_apply, kv_latent, gain_kv)
    d_kv_latent, _ = kv_norm_back(d_kv_own)
    q_inverse = lax.rsqrt(jnp.mean(q_latent * q_latent, axis=-1, keepdims=True) + EPS)
    kv_inverse = lax.rsqrt(jnp.mean(kv_latent * kv_latent, axis=-1, keepdims=True) + EPS)
    gain_rank_terms = low(
        jnp.concatenate(
            [d_q_own * q_latent * q_inverse, d_kv_own * kv_latent * kv_inverse], axis=-1
        )
    )
    d_rot_raw = rotate_back(rot_latent, own_pos, d_rot_own)
    d_latents = low(
        jnp.concatenate(
            [
                d_q_latent,
                d_kv_latent,
                d_rot_raw,
                jnp.zeros((own_rows, packed_columns - down_columns), jnp.float32),
            ],
            axis=-1,
        )
    )
    d_x_normed = mul_trans(d_latents, all_packed)
    _, x_norm_back = jax.vjp(norm_apply, resid_in, gain_attn)
    d_x_norm, _ = x_norm_back(d_x_normed)
    x_inverse = lax.rsqrt(jnp.mean(resid_in * resid_in, axis=-1, keepdims=True) + EPS)
    gain_attn_terms = d_x_normed * resid_in * x_inverse
    grad_input = move_columns(d_mid + d_x_norm, to_order, True, 3)

    kind = jnp.arange(3 * own_rows, dtype=jnp.int32)[:, None] // own_rows + down_columns
    markers = (jnp.arange(packed_columns, dtype=jnp.int32)[None, :] == kind).astype(jnp.bfloat16)
    grad_packed = trans_mul(
        jnp.concatenate(
            [
                tied(x_normed, links.named(["R3"])),
                low(gain_attn_terms),
                low(gain_mlp_terms),
                low(plain_mul(gain_rank_terms, gain_order)),
            ],
            axis=0,
        ),
        jnp.concatenate([d_latents, markers], axis=0),
    ).reshape(dp_count, tensor_count, down_rows, packed_columns)
    keep = jnp.where(is_first, grad_packed[:, 0], grad_packed[:, 1])
    give = jnp.where(is_first, grad_packed[:, 1], grad_packed[:, 0])
    keep = keep + wide(core_swap(low(give)))
    up_flow.step()
    down_flow = links.flow("T", reduce_dp_direct(keep.reshape(dp_count * down_rows, packed_columns)))
    down_flow.step()
    up_flow.step().step()
    up_shard = up_flow.end()
    packed_shard = down_flow.end()
    qup_shard = up_shard[:q_rows].reshape(q_rows, heads_local, LANES)[..., :head_qk]
    kvup_shard = up_shard[q_rows:]
    exchange_flow.end()
    unit_parts = tied(unit_parts, links.named(["Q4"]))
    unit_shards = place_group([part[at] for part in unit_parts for at in range(GROUP // 2)])
    gate_shard = join_units(unit_shards[..., :share], units)
    upper_shard = join_units(unit_shards[..., share : 2 * share], units)
    down_shard = join_units(unit_shards[..., 2 * share :], units).T
    mlp_own = mlp_flow.end()
    layer_out = low(mul_trans(low(mid_resid + RESID * mlp_own), to_order))
    gain_shards = packed_shard[:, down_columns : down_columns + 3].T

    return (
        layer_out,
        grad_input,
        gain_shards[0],
        packed_shard[:, :q_rank],
        gain_shards[2, :q_share],
        packed_shard[:, q_rank:down_columns],
        gain_shards[2, q_share : q_share + kv_share],
        qup_shard.reshape(q_up.shape),
        kvup_shard,
        out_shard,
        gain_shards[1],
        gate_shard,
        upper_shard,
        down_shard,
    )


def solution(mesh):
    return jax.shard_map(
        body,
        mesh=mesh,
        in_specs=(
            P(("dp", "tensor"), None),
            P("dp"),
            P(("dp", "tensor")),
            P(("dp", "tensor"), None),
            P(("dp", "tensor")),
            P(("dp", "tensor"), None),
            P(("dp", "tensor")),
            P("dp", "tensor"),
            P("dp", "tensor"),
            P("tensor", "dp"),
            P(("dp", "tensor")),
            P("dp", "tensor"),
            P("dp", "tensor"),
            P("tensor", "dp"),
            P(("dp", "tensor"), None),
        ),
        out_specs=(
            P(("dp", "tensor"), None),
            P(("dp", "tensor"), None),
            P(("dp", "tensor")),
            P(("dp", "tensor"), None),
            P(("dp", "tensor")),
            P(("dp", "tensor"), None),
            P(("dp", "tensor")),
            P("dp", "tensor"),
            P("dp", "tensor"),
            P("tensor", "dp"),
            P(("dp", "tensor")),
            P("dp", "tensor"),
            P("dp", "tensor"),
            P("tensor", "dp"),
        ),
        check_vma=False,
    )
```

```python
from functools import partial
import math

import jax
import jax.numpy as jnp
from jax import lax
from jax.experimental import pallas as pl
from jax.experimental.pallas import tpu as pltpu
from jax.sharding import PartitionSpec as P

NOPE = 64
ROPE = 32
VD = 64
KR = 256
LANES = 128
GROUP_BITS = (2, 8)
LAST_BITS = (1, 2)
NEAR, FAR = 4, 8
GROUP = 4


EPS = 1e-05
RESID = 1.4 / math.sqrt(62.0)
THETA = 10000.0
NEG_FILL = -1e30


def norm_apply(values, gain):
    inverse = lax.rsqrt(jnp.mean(values * values, axis=-1, keepdims=True) + EPS)
    return values * inverse * gain


def rotate(values, positions):
    width_half = values.shape[-1] // 2
    frequency = THETA ** (-2.0 * jnp.arange(width_half, dtype=jnp.float32) / values.shape[-1])
    angles = positions.astype(jnp.float32)[:, None] * frequency[None, :]
    extra_dims = (1,) * (values.ndim - 2)
    cosine = jnp.cos(angles).reshape(angles.shape[:1] + extra_dims + angles.shape[1:])
    sine = jnp.sin(angles).reshape(angles.shape[:1] + extra_dims + angles.shape[1:])
    lower_part = values[..., :width_half]
    upper_part = values[..., width_half:]
    return jnp.concatenate(
        [lower_part * cosine - upper_part * sine, upper_part * cosine + lower_part * sine], axis=-1
    )


def rotate_back(values, positions, grads):
    _, pullback = jax.vjp(partial(rotate, positions=positions), values)
    return pullback(grads)[0]


def plain_mul(left, right):
    return jnp.dot(left, right, preferred_element_type=jnp.float32)


def mul_trans(left, right):
    return lax.dot_general(
        left, right, (((1,), (1,)), ((), ())), preferred_element_type=jnp.float32
    )


def trans_mul(left, right):
    return lax.dot_general(
        left, right, (((0,), (0,)), ((), ())), preferred_element_type=jnp.float32
    )


def low(values):
    return values.astype(jnp.bfloat16)


def wide(values):
    return values.astype(jnp.float32)


def core_swap(values):
    return lax.ppermute(values, "tensor", [(0, 1), (1, 0)])


def all_bits():
    count = lax.axis_size("dp")
    return tuple(1 << at for at in range(count.bit_length() - 1))


def other_bits(bits):
    return tuple(bit for bit in all_bits() if bit not in bits)


def masks_of(bits):
    masks = [0]
    for bit in bits:
        masks += [mask | bit for mask in masks]
    return masks


def by_count(bits):
    return sorted(masks_of(bits)[1:], key=lambda mask: bin(mask).count("1"))


def group_place():
    place = lax.axis_index("dp")
    return sum(((place // bit) % 2) << at for at, bit in enumerate(GROUP_BITS))


def tied(values, others):
    return lax.optimization_barrier((values, others))[0] if others else values


AFTER = {
    "A1": ("B0", "B1"),
    "C1": ("B0",),
    "U0": ("B2", "C0", "C1"),
    "B3": ("C0", "C1"),
    "B4": ("C2",),
    "B5": ("latents", "V1"),
    "B6": ("latents",),
    "G1": ("B5", "B6"),
    "C5": ("G1", "V2"),
    "C6": ("G1", "V2"),
    "M0": ("G2",),
    "M1": ("G2",),
    "M2": ("W1",),
    "W2": ("M1",),
    "W3": ("M1",),
    "R1": ("D1",),
    "R2": ("D2", "D1"),
    "R3": ("D2", "D1"),
    "P0": ("D2", "D1"),
    "P1": ("R0",),
    "P2": ("R1",),
    "O0": ("R1",),
    "Q0": ("P2", "R2"),
    "Q1": ("R2",),
    "T0": ("Q3",),
}


FREE = ("T1",)


class Flow:
    def __init__(self, links, name, routine):
        self.links, self.name, self.routine = links, name, routine
        self.count, self.result, self.given = 0, None, None
        self.wanted = self.resume(None)

    def resume(self, given):
        try:
            return self.routine.send(given)
        except StopIteration as end:
            self.result = end.value
            return None

    def step(self, hold=()):
        if self.wanted is None:
            return self
        name = self.name + str(self.count)
        got = self.links.send(*self.wanted, AFTER.get(name, ()), name not in FREE)
        self.links.sent[name] = self.wanted[0]
        self.links.done[name] = got
        self.count += 1
        self.wanted = self.resume(tied(got, self.links.named(hold)))
        return self

    def end(self):
        while self.wanted is not None:
            self.step()
        return self.result


class Links:
    def __init__(self):
        self.last = {}
        self.done = {}
        self.sent = {}

    def named(self, names):
        return [self.done[name] for name in names if name in self.done]

    def send(self, values, mask, after=(), in_line=True):
        masks = mask if isinstance(mask, list) else [mask]
        bits = sorted({bit for item in masks for bit in all_bits() if bit & item})
        before = self.named(after)
        if in_line:
            before += [self.last[bit] for bit in bits if bit in self.last]
        values = tied(values, before)
        count = lax.axis_size("dp")
        got = [
            lax.ppermute(item, "dp", [(place, place ^ to) for place in range(count)])
            for item, to in zip(values if mask is masks else [values], masks)
        ]
        got = got if mask is masks else got[0]
        self.last.update({bit: got for bit in bits})
        return got

    def flow(self, name, routine):
        return Flow(self, name, routine)


def routes(mask, bits, split):
    ordered = [bit for bit in bits if bit & mask]
    if len(ordered) > 1 and split == "both":
        return [(ordered[0], 0), (ordered[-1], 1)]
    return [(ordered[-1 if split == "last" else 0], None)]


def halves(values):
    half = values.shape[0] // 2
    return values[:half], values[half:]


def gather_bits(values, bits, split):
    known = {0: [values]}
    for mask in by_count(bits):
        pieces = []
        for bit, part in routes(mask, bits, split):
            source = known[mask ^ bit]
            if part is None:
                moving = source[0] if len(source) == 1 else jnp.concatenate(source)
            else:
                moving = halves(source[0])[part] if len(source) == 1 else source[part]
            pieces.append((yield moving, bit))
        known[mask] = pieces
    return known


def reduce_bits(block_of, bits, split, arrive=lambda values, bit: values):
    added = {mask: [] for mask in masks_of(bits)}

    def summed(mask, part):
        values = block_of(mask)
        if part is not None:
            values = halves(values)[part]
        if added[mask]:
            values = wide(values)
        for held, extra in added[mask]:
            if part is None or part == held:
                values = values + wide(extra)
            elif held is None:
                values = values + wide(halves(extra)[part])
        return values

    def whole(mask):
        if any(held is not None for held, _ in added[mask]):
            return [summed(mask, 0), summed(mask, 1)]
        return [summed(mask, None)]

    for mask in reversed(by_count(bits)):
        for bit, part in routes(mask, bits, split):
            if part is None:
                parts = [low(item) for item in whole(mask)]
                moving = parts[0] if len(parts) == 1 else jnp.concatenate(parts)
            else:
                moving = low(summed(mask, part))
            got = yield moving, bit
            added[mask ^ bit].append((part, arrive(got, bit)))
    parts = whole(0)
    return parts[0] if len(parts) == 1 else jnp.concatenate(parts)


def row_order():
    return [
        other | group for other in masks_of(other_bits(GROUP_BITS)) for group in masks_of(GROUP_BITS)
    ]


def first_bits():
    return other_bits(LAST_BITS)


def gather_dp(values):
    first = masks_of(first_bits())
    known = yield from gather_bits(values, first_bits(), "first")
    column = jnp.stack([known[mask][0] for mask in first])
    known = yield from gather_bits(column, LAST_BITS, "both")
    half = len(first) // 2

    def block(mask):
        at = first.index(mask & ~sum(LAST_BITS))
        pieces = known[mask & sum(LAST_BITS)]
        return pieces[0][at] if len(pieces) == 1 else pieces[at // half][at % half]

    return jnp.concatenate([block(mask) for mask in row_order()], axis=0)


def gather_dp_direct(values):
    first, last = masks_of(first_bits()), masks_of(LAST_BITS)
    got = yield [values] * (len(first) - 1), first[1:]
    column = jnp.stack([values] + got)
    got = yield [column] * (len(last) - 1), last[1:]
    known = dict(zip(last, [column] + got))
    return jnp.concatenate(
        [known[mask & sum(LAST_BITS)][first.index(mask & ~sum(LAST_BITS))] for mask in row_order()],
        axis=0,
    )


def reduce_dp_direct(grad):
    order, first, last = row_order(), masks_of(first_bits()), masks_of(LAST_BITS)
    blocks = grad.reshape(len(order), -1, grad.shape[1])
    columns = [jnp.stack([blocks[order.index(mask | item)] for item in first]) for mask in last]
    got = yield [low(column) for column in columns[1:]], last[1:]
    column = columns[0] + sum(wide(item) for item in got)
    got = yield [low(column[at]) for at in range(1, len(first))], first[1:]
    return column[0] + sum(wide(item) for item in got)


def reduce_dp(grad):
    order = row_order()
    blocks = grad.reshape(len(order), -1, grad.shape[1])
    first = masks_of(first_bits())

    def column(last):
        return jnp.stack([blocks[order.index(last | mask)] for mask in first])

    partial_sum = yield from reduce_bits(column, LAST_BITS, "both")
    return (
        yield from reduce_bits(lambda mask: partial_sum[first.index(mask)], first_bits(), "first")
    )


def place_kernel(place_ref, *refs):
    out_ref = refs[-1]
    for step, ref in enumerate(refs[:-1]):

        @pl.when(pl.program_id(0) == step)
        def _():
            out_ref[0] = ref[...]


def pick_kernel(place_ref, values_ref, *out_refs):
    for step, ref in enumerate(out_refs):

        @pl.when(pl.program_id(0) == step)
        def _():
            ref[...] = values_ref[0]


def place_index():
    return group_place().reshape(1).astype(jnp.int32)


def place_group(blocks):
    rows, width = blocks[0].shape
    return pl.pallas_call(
        place_kernel,
        grid_spec=pltpu.PrefetchScalarGridSpec(
            num_scalar_prefetch=1,
            grid=(GROUP,),
            in_specs=[pl.BlockSpec((rows, width), lambda step, place: (0, 0))] * GROUP,
            out_specs=pl.BlockSpec(
                (1, rows, width), lambda step, place: (lax.bitwise_xor(place[0], step), 0, 0)
            ),
        ),
        out_shape=jax.ShapeDtypeStruct((GROUP, rows, width), blocks[0].dtype),
        compiler_params=pltpu.CompilerParams(vmem_limit_bytes=32 * 2**20),
        name="place_group",
    )(place_index(), *blocks)


def pick_group(values):
    _, rows, width = values.shape
    blocks = pl.pallas_call(
        pick_kernel,
        grid_spec=pltpu.PrefetchScalarGridSpec(
            num_scalar_prefetch=1,
            grid=(GROUP,),
            in_specs=[
                pl.BlockSpec(
                    (1, rows, width), lambda step, place: (lax.bitwise_xor(place[0], step), 0, 0)
                )
            ],
            out_specs=[pl.BlockSpec((rows, width), lambda step, place: (0, 0))] * GROUP,
        ),
        out_shape=[jax.ShapeDtypeStruct((rows, width), values.dtype)] * GROUP,
        compiler_params=pltpu.CompilerParams(vmem_limit_bytes=32 * 2**20),
        name="pick_group",
    )(place_index(), values)
    return list(blocks)


def exchange_group(blocks, arrived):
    near, far = GROUP_BITS
    there = yield jnp.stack([blocks[1], blocks[3]]), near
    arrived.append(jnp.stack([blocks[0], there[0]]))
    across = yield blocks[2], far
    relayed = yield there[1], far
    arrived.append(jnp.stack([across, relayed]))


def cut_units(weight, share):
    rows, units = weight.shape
    cut = jnp.moveaxis(weight.reshape(rows, GROUP, units // GROUP), 1, 0)
    return jnp.pad(cut, ((0, 0), (0, 0), (0, share - units // GROUP)))


def join_units(pieces, units):
    rows = pieces.shape[1]
    return wide(jnp.moveaxis(pieces[..., : units // GROUP], 0, 1)).reshape(rows, units)


CHUNKS = 4


def reorder_kernel(steps, block, *refs):
    width = refs[0].shape[-1]
    chunk = width // CHUNKS
    for at, step in enumerate(steps):
        source, target = refs[at], refs[-1].at[at]
        if not step:
            target[...] = source[...]
            continue
        row = lax.broadcasted_iota(jnp.int32, (chunk, chunk), 0)
        column = lax.broadcasted_iota(jnp.int32, (chunk, chunk), 1)
        index = lax.rem(lax.div(column, block), GROUP)
        origin = column + (lax.bitwise_xor(index, step) - index) * block
        moved = jnp.where(row == origin, 1.0, 0.0).astype(jnp.bfloat16)
        for part in range(CHUNKS):
            columns = slice(part * chunk, (part + 1) * chunk)
            target[:, columns] = low(plain_mul(source[:, columns], moved))


def reorder(arrays, steps):
    rows, width = arrays[0].shape
    return pl.pallas_call(
        partial(reorder_kernel, tuple(steps), width // lax.axis_size("dp")),
        out_shape=jax.ShapeDtypeStruct((len(steps), rows, width), arrays[0].dtype),
        compiler_params=pltpu.CompilerParams(vmem_limit_bytes=32 * 2**20),
        name="reorder",
    )(*arrays)


def gather_tokens(values, held):
    known = yield from gather_bits(values, GROUP_BITS, "first")
    own = reorder([known[mask][0] for mask in masks_of(GROUP_BITS)], range(GROUP))
    own = tied(own.reshape(-1, values.shape[1]), held)
    return own, core_swap(own)


def gather_whole_tokens(values, to_order):
    known = yield from gather_bits(values, GROUP_BITS, "last")
    own = jnp.concatenate([known[mask][0] for mask in masks_of(GROUP_BITS)], axis=0)
    own = low(plain_mul(own, to_order))
    return own, core_swap(own)


def return_tokens(mine, others, rows):
    chip_sum = (wide(mine) + wide(others)).reshape(GROUP, rows, -1)
    masks = masks_of(GROUP_BITS)
    return reduce_bits(
        lambda mask: chip_sum[masks.index(mask)],
        GROUP_BITS,
        "first",
        lambda got, bit: reorder([got], [masks.index(bit)])[0],
    )


def bring(pieces, weight_ref, sems, column):
    copies, start = [], 0
    for at, piece in enumerate(pieces):
        rows = piece.shape[0]
        copies.append(
            pltpu.make_async_copy(
                piece.at[:, pl.ds(column, weight_ref.shape[1])],
                weight_ref.at[pl.ds(start, rows)],
                sems.at[at],
            )
        )
        start += rows
    for copy in copies:
        copy.start()
    for copy in copies:
        copy.wait()


def units_out_kernel(share, count, act_ref, *refs):
    pieces, (out_ref, weight_ref, sems) = refs[:count], refs[count:]

    @pl.when(pl.program_id(0) == 0)
    def _():
        bring(pieces, weight_ref, sems, 2 * share)

    out_ref[...] = low(mul_trans(act_ref[...], weight_ref[...]))


def units_out(act, pieces, share):
    rows, width = act.shape[0], sum(piece.shape[0] for piece in pieces)
    block = rows // 4
    return pl.pallas_call(
        partial(units_out_kernel, share, len(pieces)),
        grid=(4,),
        in_specs=[pl.BlockSpec((block, share), lambda step: (step, 0))]
        + [pl.BlockSpec(memory_space=pl.ANY)] * len(pieces),
        out_specs=pl.BlockSpec((block, width), lambda step: (step, 0)),
        out_shape=jax.ShapeDtypeStruct((rows, width), jnp.bfloat16),
        scratch_shapes=[
            pltpu.VMEM((width, share), jnp.bfloat16),
            pltpu.SemaphoreType.DMA((len(pieces),)),
        ],
        compiler_params=pltpu.CompilerParams(vmem_limit_bytes=32 * 2**20),
        name="units_out",
    )(act, *pieces)


def units_kernel(
    share, count, own_ref, other_ref, own_back_ref, other_back_ref, *refs
):
    pieces, (act_ref, d_units_ref, d_in_ref, weight_ref, sems) = refs[:count], refs[count:]
    step = pl.program_id(0)

    @pl.when(step == 0)
    def _():
        bring(pieces, weight_ref, sems, 0)

    is_own = step < pl.num_programs(0) // 2
    tokens = jnp.where(is_own, own_ref[...], other_ref[...])
    back = jnp.where(is_own, own_back_ref[...], other_back_ref[...])
    gate_cut, up_cut = slice(0, share), slice(share, 2 * share)
    down_cut = slice(2 * share, 3 * share)
    gate = plain_mul(tokens, weight_ref[:, gate_cut])
    upper = plain_mul(tokens, weight_ref[:, up_cut])
    d_act = plain_mul(back, weight_ref[:, down_cut])
    slope = 1.0 / (1.0 + jnp.exp(-gate))
    swished = gate * slope
    act = low(swished * upper)
    act_ref[...] = act
    d_units_ref[:, gate_cut] = low(d_act * upper * (slope + swished * (1.0 - slope)))
    d_units_ref[:, up_cut] = low(d_act * swished)
    d_in_ref[...] = low(mul_trans(d_units_ref[...], weight_ref[:, : 2 * share]))


def run_units(tokens, back, pieces, share):
    own, other = tokens
    rows, width = own.shape
    steps = 4
    block = 2 * rows // steps
    half = steps // 2
    in_own = pl.BlockSpec((block, width), lambda step: (jnp.minimum(step, half - 1), 0))
    in_other = pl.BlockSpec((block, width), lambda step: (jnp.maximum(step - half, 0), 0))
    many = pl.BlockSpec(memory_space=pl.ANY)

    def out_spec(columns):
        return pl.BlockSpec((block, columns), lambda step: (step, 0))

    columns = (share, 2 * share, width)
    return pl.pallas_call(
        partial(units_kernel, share, len(pieces)),
        grid=(steps,),
        in_specs=[in_own, in_other, in_own, in_other] + [many] * len(pieces),
        out_specs=[out_spec(item) for item in columns],
        out_shape=[jax.ShapeDtypeStruct((2 * rows, item), jnp.bfloat16) for item in columns],
        scratch_shapes=[
            pltpu.VMEM((width, 3 * share), jnp.bfloat16),
            pltpu.SemaphoreType.DMA((len(pieces),)),
        ],
        compiler_params=pltpu.CompilerParams(vmem_limit_bytes=56 * 2**20),
        name="run_units",
    )(own, other, *back, *pieces)


def unit_grads_kernel(share, own_ref, other_ref, own_back_ref, other_back_ref, act_ref, d_units_ref, out_ref):
    tokens = jnp.concatenate([own_ref[...], other_ref[...]], axis=0)
    out_ref[:, : 2 * share] = low(trans_mul(tokens, d_units_ref[...]))
    back = jnp.concatenate([own_back_ref[...], other_back_ref[...]], axis=0)
    out_ref[:, 2 * share :] = low(trans_mul(back, act_ref[...]))


def unit_grads(tokens, back, act, d_units, share):
    rows, width = tokens[0].shape
    chunk = width // CHUNKS
    part = pl.BlockSpec((rows, chunk), lambda step: (0, step))
    return pl.pallas_call(
        partial(unit_grads_kernel, share),
        grid=(CHUNKS,),
        in_specs=[part] * 4
        + [pl.BlockSpec(act.shape, lambda step: (0, 0)), pl.BlockSpec(d_units.shape, lambda step: (0, 0))],
        out_specs=pl.BlockSpec((chunk, 3 * share), lambda step: (step, 0)),
        out_shape=jax.ShapeDtypeStruct((width, 3 * share), jnp.bfloat16),
        compiler_params=pltpu.CompilerParams(vmem_limit_bytes=56 * 2**20),
        name="unit_grads",
    )(*tokens, *back, act, d_units)


def pair_tokens(values):
    return jnp.concatenate([values, core_swap(values)], axis=0)


def split_pair(values):
    rows = values.shape[0] // 2
    return values[:rows] + wide(core_swap(low(values[rows:])))


def block_origins(total):
    order = row_order()
    block = total // len(order)
    place = jnp.arange(total, dtype=jnp.int32)
    index = place // block
    mask = jnp.zeros_like(index)
    for at, bit in enumerate(GROUP_BITS + other_bits(GROUP_BITS)):
        mask = mask + ((index >> at) % 2) * bit
    return (lax.axis_index("dp") ^ mask) * block + place % block


def one_hot(origins, size):
    return (jnp.arange(size, dtype=jnp.int32)[:, None] == origins[None, :]).astype(jnp.bfloat16)


def pad_heads(columns, head):
    column = jnp.arange(columns // head * LANES, dtype=jnp.int32)
    within = column % LANES
    return one_hot(jnp.where(within < head, column // LANES * head + within, -1), columns)


def in_parts(values, count):
    parts = []
    for _ in range(count):
        part = low(values)
        parts.append(part)
        values = values - wide(part)
    return parts


def move_columns(values, selector, transpose, count):
    rows = values.shape[0]
    stacked = jnp.concatenate(in_parts(values, count), axis=0)
    moved = mul_trans(stacked, selector) if transpose else plain_mul(stacked, selector)
    return sum(moved[at * rows : (at + 1) * rows] for at in range(count))


def round_up(size, step):
    return -(-size // step) * step


def turn_tables(positions):
    lane = jnp.arange(LANES, dtype=jnp.int32)[None, :]
    half = ROPE // 2
    frequency = THETA ** (-2.0 * ((lane - NOPE) % half).astype(jnp.float32) / ROPE)
    angles = positions.astype(jnp.float32)[:, None] * frequency
    in_first = (lane >= NOPE) & (lane < NOPE + half)
    in_last = (lane >= NOPE + half) & (lane < NOPE + ROPE)
    cosine, sine = jnp.cos(angles), jnp.sin(angles)
    keep = jnp.where(in_first | in_last, cosine, jnp.where(lane < NOPE, 1.0, 0.0))
    return keep, jnp.where(in_first, -sine, 0.0), jnp.where(in_last, sine, 0.0)


def lanes_on(values, step):
    return pltpu.roll(values, (-step) % LANES, 1)


def key_of(tile, k_rotary):
    lane = lax.broadcasted_iota(jnp.int32, tile.shape, 1)
    return jnp.where(lane < NOPE, tile, k_rotary)


def probs_of(query, key, visible, scale):
    scores = jnp.where(visible, mul_trans(query, key) * scale, NEG_FILL)
    exp_scores = jnp.exp(scores - jnp.max(scores, axis=-1, keepdims=True))
    return exp_scores / jnp.sum(exp_scores, axis=-1, keepdims=True)


def attend_kernel(scale, q_ref, kv_ref, rot_ref, seen_ref, keep_ref, up_ref, down_ref, out_ref, query_ref):
    visible = seen_ref[...] > 0.0
    outs = []
    for head in range(2):
        lanes = slice(head * LANES, (head + 1) * LANES)
        raw = q_ref[:, lanes]
        query = (
            raw * keep_ref[...]
            + lanes_on(raw, ROPE // 2) * up_ref[...]
            + lanes_on(raw, -(ROPE // 2)) * down_ref[...]
        ).astype(jnp.bfloat16)
        query_ref[:, lanes] = query
        tile = kv_ref[:, lanes]
        probs = probs_of(query, key_of(tile, rot_ref[...]), visible, scale)
        outs.append(plain_mul(probs.astype(jnp.bfloat16), tile))
    lane = lax.broadcasted_iota(jnp.int32, outs[0].shape, 1)
    out_ref[...] = jnp.where(lane < VD, pltpu.roll(outs[0], VD, 1), outs[1]).astype(jnp.bfloat16)


def attend_back_kernel(
    scale, query_ref, kv_ref, rot_ref, seen_ref, keep_ref, up_ref, down_ref, d_out_ref,
    d_q_ref, d_kv_ref, d_rot_ref,
):
    @pl.when(pl.program_id(0) == 0)
    def _():
        d_rot_ref[...] = jnp.zeros_like(d_rot_ref)

    visible = seen_ref[...] > 0.0
    d_pair = wide(d_out_ref[...])
    lane = lax.broadcasted_iota(jnp.int32, d_pair.shape, 1)
    d_rot = d_rot_ref[...]
    for head in range(2):
        lanes = slice(head * LANES, (head + 1) * LANES)
        query = query_ref[:, lanes]
        tile = kv_ref[:, lanes]
        key = key_of(tile, rot_ref[...])
        probs = probs_of(query, key, visible, scale)
        d_head = d_pair if head else pltpu.roll(d_pair, VD, 1)
        d_head = low(jnp.where(lane < NOPE, 0.0, d_head))
        d_probs = mul_trans(d_head, tile)
        d_values = trans_mul(low(probs), d_head)
        row_dot = jnp.sum(probs * d_probs, axis=-1, keepdims=True)
        d_scores = low(probs * (d_probs - row_dot) * scale)
        d_query = plain_mul(d_scores, key)
        d_key = trans_mul(d_scores, query)
        d_q_ref[:, lanes] = low(
            d_query * keep_ref[...]
            - lanes_on(d_query, ROPE // 2) * up_ref[...]
            - lanes_on(d_query, -(ROPE // 2)) * down_ref[...]
        )
        d_kv_ref[:, lanes] = low(jnp.where(lane < NOPE, d_key, d_values))
        d_rot += d_key
    d_rot_ref[...] = d_rot


def attend_specs(length):
    pair = pl.BlockSpec((length, 2 * LANES), lambda step: (0, step))
    single = pl.BlockSpec((length, LANES), lambda step: (0, step))
    table = pl.BlockSpec((length, LANES), lambda step: (0, 0))
    seen = pl.BlockSpec((length, length), lambda step: (0, 0))
    return pair, single, table, seen


def attend(query, key_value, rot_pad, seen, tables, scale):
    length, columns = query.shape
    pair, single, table, whole = attend_specs(length)
    return pl.pallas_call(
        partial(attend_kernel, scale),
        grid=(columns // (2 * LANES),),
        in_specs=[pair, pair, table, whole, table, table, table],
        out_specs=[single, pair],
        out_shape=[
            jax.ShapeDtypeStruct((length, columns // 2), jnp.bfloat16),
            jax.ShapeDtypeStruct((length, columns), jnp.bfloat16),
        ],
        compiler_params=pltpu.CompilerParams(vmem_limit_bytes=32 * 2**20),
        name="attend",
    )(query, key_value, rot_pad, seen, *tables)


def attend_back(query_full, key_value, rot_pad, seen, tables, d_heads, scale):
    length, columns = query_full.shape
    pair, single, table, whole = attend_specs(length)
    return pl.pallas_call(
        partial(attend_back_kernel, scale),
        grid=(columns // (2 * LANES),),
        in_specs=[pair, pair, table, whole, table, table, table, single],
        out_specs=[pair, pair, table],
        out_shape=[
            jax.ShapeDtypeStruct((length, columns), jnp.bfloat16),
            jax.ShapeDtypeStruct((length, columns), jnp.bfloat16),
            jax.ShapeDtypeStruct((length, LANES), jnp.float32),
        ],
        compiler_params=pltpu.CompilerParams(vmem_limit_bytes=32 * 2**20),
        name="attend_back",
    )(query_full, key_value, rot_pad, seen, *tables, d_heads)


def body(
    hidden_in,
    prefix_len,
    attn_gain,
    q_down,
    q_gain,
    kv_down,
    kv_gain,
    q_up,
    kv_up,
    o_proj,
    mlp_gain,
    w_gate,
    w_up,
    w_down,
    cotangent,
):
    tensor_count = lax.axis_size("tensor")
    tensor_rank = lax.axis_index("tensor")
    dp_count = lax.axis_size("dp")
    own_rows, width = hidden_in.shape
    q_rank = q_down.shape[1]
    rank = q_rank + KR
    down_rows = q_down.shape[0]
    q_share, kv_share = q_gain.shape[0], kv_gain.shape[0]
    q_rows, kv_rows = q_up.shape[0], kv_up.shape[0]
    head_qk = NOPE + ROPE
    heads_local = q_up.shape[1] // head_qk
    scale = head_qk ** (-0.5)
    links = Links()
    width_origins = block_origins(width)
    to_order = one_hot(width_origins, width)
    units = w_gate.shape[1]
    share = round_up(units // GROUP, LANES)

    down_columns = rank + ROPE
    packed_columns = round_up(down_columns + 3, LANES)

    def column_of(gain):
        return jnp.pad(gain, (0, down_rows - gain.shape[0]))[:, None]

    packed = jnp.concatenate(
        [
            q_down,
            kv_down,
            column_of(attn_gain),
            column_of(mlp_gain),
            column_of(jnp.concatenate([q_gain, kv_gain])),
            jnp.zeros((down_rows, packed_columns - down_columns - 3), jnp.bfloat16),
        ],
        axis=1,
    )
    others = other_bits(GROUP_BITS)
    near_first = (NEAR,) + tuple(bit for bit in others if bit != NEAR)
    back_flow = links.flow(
        "G",
        gather_whole_tokens(
            (RESID * cotangent.astype(jnp.float32)).astype(jnp.bfloat16), to_order
        ),
    )
    down_flow = links.flow("A", gather_dp_direct(packed)).step()
    back_flow.step()
    q_padded = low(plain_mul(q_up, pad_heads(q_up.shape[1], head_qk)))
    up_flow = links.flow("B", gather_dp(jnp.concatenate([q_padded, kv_up], axis=0))).step().step()
    down_flow.step()
    up_flow.step()
    out_flow = links.flow("C", gather_dp(o_proj.T)).step().step().step()
    core_packed = down_flow.end().reshape(dp_count, down_rows, packed_columns)
    unit_parts = []
    unit_picks = pick_group(
        jnp.concatenate(
            [
                cut_units(item, share)
                for item in tied((w_gate, w_up, w_down.T), links.named(["B0"]))
            ],
            axis=-1,
        )
    )
    exchange_flow = links.flow("U", exchange_group(unit_picks, unit_parts))
    exchange_flow.step().step().step()
    first_flow = links.flow("V", gather_bits(unit_parts[0], near_first, "first")).step()
    up_flow.step()
    up_flow.step()
    other_packed = core_swap(core_packed)
    is_first = tensor_rank == 0
    all_packed = jnp.stack(
        [
            jnp.where(is_first, core_packed, other_packed),
            jnp.where(is_first, other_packed, core_packed),
        ],
        axis=1,
    ).reshape(width, packed_columns)

    rank_block = q_rows + kv_rows
    place = jnp.arange(rank, dtype=jnp.int32)
    device_of = block_origins(rank) // rank_block
    in_block = place % rank_block
    is_query = in_block < q_rows
    rank_order = one_hot(
        jnp.where(
            is_query,
            device_of * q_rows + in_block,
            q_rank + device_of * kv_rows + in_block - q_rows,
        ),
        rank,
    )
    hidden_low, cotangent_low = tied((hidden_in, cotangent), links.named(["A0"]))
    moved_in = plain_mul(jnp.concatenate([hidden_low, cotangent_low], axis=0), to_order)
    resid_in, grad_out = moved_in[:own_rows], moved_in[own_rows:]
    device_place = width_origins // down_rows
    in_share = width_origins % down_rows
    gain_order = one_hot(
        jnp.where(
            in_share < q_share,
            device_place * q_share + in_share,
            jnp.where(
                in_share < q_share + kv_share,
                q_rank + device_place * kv_share + in_share - q_share,
                -1,
            ),
        ),
        rank,
    )
    gains = all_packed[:, down_columns : down_columns + 3].T
    gain_attn = wide(gains[0])
    gain_mlp = wide(gains[1])
    gain_rank = mul_trans(gains[2:3], gain_order)[0]
    gain_q, gain_kv = gain_rank[:q_rank], gain_rank[q_rank:]

    x_normed = norm_apply(resid_in, gain_attn).astype(jnp.bfloat16)
    latents = plain_mul(x_normed, all_packed)
    q_latent = latents[:, :q_rank]
    kv_latent = latents[:, q_rank:rank]
    rot_latent = latents[:, rank:down_columns]
    q_normed = norm_apply(q_latent, gain_q).astype(jnp.bfloat16)
    kv_normed = norm_apply(kv_latent, gain_kv).astype(jnp.bfloat16)
    own_pos = tensor_rank * own_rows + jnp.arange(own_rows, dtype=jnp.int32)
    other_pos = (1 - tensor_rank) * own_rows + jnp.arange(own_rows, dtype=jnp.int32)
    positions = jnp.concatenate([own_pos, other_pos])
    k_rotary = rotate(rot_latent, own_pos).astype(jnp.bfloat16)
    ranks_normed = low(plain_mul(jnp.concatenate([q_normed, kv_normed], axis=-1), rank_order))
    rot_pad = jnp.pad(k_rotary, ((0, 0), (NOPE, LANES - head_qk)))
    latent_seq = pair_tokens(jnp.concatenate([ranks_normed, rot_pad], axis=-1))
    links.done["latents"] = latent_seq
    first_flow.step()
    up_flow.step().step()
    up_weight = up_flow.end()
    first_flow.step()
    out_flow.step().step()
    last_flow = links.flow("W", gather_bits(unit_parts[1], near_first, "both")).step()
    back_flow.step().step()
    mlp_back = back_flow.end()
    out_flow.step().step()
    out_trans = out_flow.end()
    last_flow.step()
    rank_seq = latent_seq[:, :rank]
    rot_seq = latent_seq[:, rank:]
    zero = jnp.zeros((), jnp.bfloat16)
    q_seq = jnp.where(is_query[None, :], rank_seq, zero)
    kv_seq = jnp.where(is_query[None, :], zero, rank_seq)
    query = plain_mul(q_seq, up_weight)
    key_value = low(plain_mul(kv_seq, up_weight))
    visible = (positions[None, :] <= positions[:, None]) | (positions[None, :] < prefix_len[0])
    seen = visible.astype(jnp.float32)
    tables = turn_tables(positions)
    heads_low, query_full = attend(query, key_value, rot_seq, seen, tables, scale)
    attn_own = split_pair(mul_trans(heads_low, tied(out_trans, links.named(["G2"]))))
    mid_resid = resid_in + RESID * attn_own
    mlp_normed = norm_apply(mid_resid, gain_mlp).astype(jnp.bfloat16)

    mlp_flow = links.flow("M", gather_tokens(mlp_normed, links.named(["W0"]))).step().step()
    mlp_seq = mlp_flow.end()
    last_flow.step().step()
    first_units, last_units = first_flow.end(), last_flow.end()
    unit_pieces = [
        piece.reshape(-1, 3 * share)
        for mask in masks_of(others)
        for piece in first_units[mask] + last_units[mask]
    ]
    if any(piece.shape[0] % 16 for piece in unit_pieces):
        unit_pieces = [jnp.concatenate(unit_pieces)]
    act_low, d_units, d_mlp_terms = run_units(mlp_seq, mlp_back, unit_pieces, share)
    chip_rows = GROUP * own_rows
    d_mlp_other = core_swap(d_mlp_terms[chip_rows:])
    d_mlp_flow = links.flow("D", return_tokens(d_mlp_terms[:chip_rows], d_mlp_other, own_rows))
    d_mlp_flow.step().step().step()
    d_mlp_own = d_mlp_flow.end()
    unit_grad = unit_grads(
        mlp_seq, mlp_back, tied(act_low, [d_mlp_other]), d_units, share
    ).reshape(len(masks_of(others)), GROUP, -1, 3 * share)
    unit_flow = links.flow(
        "R", reduce_bits(lambda mask: unit_grad[masks_of(others).index(mask)], others, "both")
    )
    unit_flow.step(["D1", "D2"]).step()
    mlp_terms = units_out(tied(act_low, links.named(["D0"])), unit_pieces, share)
    mlp_flow = links.flow(
        "O",
        return_tokens(
            mlp_terms[:chip_rows],
            core_swap(mlp_terms[chip_rows:]),
            own_rows,
        ),
    )

    _, mlp_norm_back = jax.vjp(norm_apply, mid_resid, gain_mlp)
    d_mid_norm, _ = mlp_norm_back(d_mlp_own)
    mid_inverse = lax.rsqrt(jnp.mean(mid_resid * mid_resid, axis=-1, keepdims=True) + EPS)
    gain_mlp_terms = d_mlp_own * mid_resid * mid_inverse
    d_mid = grad_out + d_mid_norm
    attn_back = pair_tokens((RESID * d_mid).astype(jnp.bfloat16))
    d_heads = low(plain_mul(attn_back, out_trans))
    out_grad = trans_mul(attn_back, heads_low)
    out_flow = links.flow("P", reduce_dp(out_grad)).step().step()
    unit_flow.step().step()
    out_flow.step()
    mlp_flow.step().step(["R3"]).step(["R3"])
    d_query, d_key_value, d_rot = attend_back(
        query_full, key_value, rot_seq, seen, tables, tied(d_heads, [links.sent["R0"], out_grad]), scale
    )
    d_query, d_key_value, d_rot = tied(
        (d_query, d_key_value, d_rot), links.named(["R1"]) + [links.sent["R3"]]
    )
    d_rank = jnp.where(
        is_query[None, :], mul_trans(d_query, up_weight), mul_trans(d_key_value, up_weight)
    )
    d_latent_own = split_pair(jnp.concatenate([d_rank, d_rot], axis=-1))
    d_rank_own = move_columns(d_latent_own[:, :rank], rank_order, True, 2)
    d_q_own, d_kv_own = d_rank_own[:, :q_rank], d_rank_own[:, q_rank:]
    d_rot_own = d_latent_own[:, rank + NOPE : rank + head_qk]
    up_flow = links.flow(
        "Q",
        reduce_dp(
            trans_mul(
                jnp.concatenate([q_seq, kv_seq], axis=0),
                jnp.concatenate([d_query, d_key_value], axis=0),
            )
        ),
    )
    unit_sum = unit_flow.end()
    unit_parts = []
    exchange_flow = links.flow(
        "S", exchange_group([low(unit_sum[at]) for at in range(GROUP)], unit_parts)
    )
    exchange_flow.step().step()
    out_flow.step()
    exchange_flow.step()
    up_flow.step().step().step().step()
    out_flow.step().step()
    out_shard = out_flow.end().T

    _, q_norm_back = jax.vjp(norm_apply, q_latent, gain_q)
    d_q_latent, _ = q_norm_back(d_q_own)
    _, kv_norm_back = jax.vjp(norm_apply, kv_latent, gain_kv)
    d_kv_latent, _ = kv_norm_back(d_kv_own)
    q_inverse = lax.rsqrt(jnp.mean(q_latent * q_latent, axis=-1, keepdims=True) + EPS)
    kv_inverse = lax.rsqrt(jnp.mean(kv_latent * kv_latent, axis=-1, keepdims=True) + EPS)
    gain_rank_terms = low(
        jnp.concatenate(
            [d_q_own * q_latent * q_inverse, d_kv_own * kv_latent * kv_inverse], axis=-1
        )
    )
    d_rot_raw = rotate_back(rot_latent, own_pos, d_rot_own)
    d_latents = low(
        jnp.concatenate(
            [
                d_q_latent,
                d_kv_latent,
                d_rot_raw,
                jnp.zeros((own_rows, packed_columns - down_columns), jnp.float32),
            ],
            axis=-1,
        )
    )
    d_x_normed = mul_trans(d_latents, all_packed)
    _, x_norm_back = jax.vjp(norm_apply, resid_in, gain_attn)
    d_x_norm, _ = x_norm_back(d_x_normed)
    x_inverse = lax.rsqrt(jnp.mean(resid_in * resid_in, axis=-1, keepdims=True) + EPS)
    gain_attn_terms = d_x_normed * resid_in * x_inverse
    grad_input = move_columns(d_mid + d_x_norm, to_order, True, 3)

    kind = jnp.arange(3 * own_rows, dtype=jnp.int32)[:, None] // own_rows + down_columns
    markers = (jnp.arange(packed_columns, dtype=jnp.int32)[None, :] == kind).astype(jnp.bfloat16)
    grad_packed = trans_mul(
        jnp.concatenate(
            [
                tied(x_normed, links.named(["R3"])),
                low(gain_attn_terms),
                low(gain_mlp_terms),
                low(plain_mul(gain_rank_terms, gain_order)),
            ],
            axis=0,
        ),
        jnp.concatenate([d_latents, markers], axis=0),
    ).reshape(dp_count, tensor_count, down_rows, packed_columns)
    keep = jnp.where(is_first, grad_packed[:, 0], grad_packed[:, 1])
    give = jnp.where(is_first, grad_packed[:, 1], grad_packed[:, 0])
    keep = keep + wide(core_swap(low(give)))
    up_flow.step()
    down_flow = links.flow("T", reduce_dp_direct(keep.reshape(dp_count * down_rows, packed_columns)))
    down_flow.step()
    up_flow.step().step()
    up_shard = up_flow.end()
    packed_shard = down_flow.end()
    qup_shard = up_shard[:q_rows].reshape(q_rows, heads_local, LANES)[..., :head_qk]
    kvup_shard = up_shard[q_rows:]
    exchange_flow.end()
    unit_parts = tied(unit_parts, links.named(["Q4"]))
    unit_shards = place_group([part[at] for part in unit_parts for at in range(GROUP // 2)])
    gate_shard = join_units(unit_shards[..., :share], units)
    upper_shard = join_units(unit_shards[..., share : 2 * share], units)
    down_shard = join_units(unit_shards[..., 2 * share :], units).T
    mlp_own = mlp_flow.end()
    layer_out = low(mul_trans(low(mid_resid + RESID * mlp_own), to_order))
    gain_shards = packed_shard[:, down_columns : down_columns + 3].T

    return (
        layer_out,
        grad_input,
        gain_shards[0],
        packed_shard[:, :q_rank],
        gain_shards[2, :q_share],
        packed_shard[:, q_rank:down_columns],
        gain_shards[2, q_share : q_share + kv_share],
        qup_shard.reshape(q_up.shape),
        kvup_shard,
        out_shard,
        gain_shards[1],
        gate_shard,
        upper_shard,
        down_shard,
    )


def solution(mesh):
    return jax.shard_map(
        body,
        mesh=mesh,
        in_specs=(
            P(("dp", "tensor"), None),
            P("dp"),
            P(("dp", "tensor")),
            P(("dp", "tensor"), None),
            P(("dp", "tensor")),
            P(("dp", "tensor"), None),
            P(("dp", "tensor")),
            P("dp", "tensor"),
            P("dp", "tensor"),
            P("tensor", "dp"),
            P(("dp", "tensor")),
            P("dp", "tensor"),
            P("dp", "tensor"),
            P("tensor", "dp"),
            P(("dp", "tensor"), None),
        ),
        out_specs=(
            P(("dp", "tensor"), None),
            P(("dp", "tensor"), None),
            P(("dp", "tensor")),
            P(("dp", "tensor"), None),
            P(("dp", "tensor")),
            P(("dp", "tensor"), None),
            P(("dp", "tensor")),
            P("dp", "tensor"),
            P("dp", "tensor"),
            P("tensor", "dp"),
            P(("dp", "tensor")),
            P("dp", "tensor"),
            P("dp", "tensor"),
            P("tensor", "dp"),
        ),
        check_vma=False,
    )
```

```python
from functools import partial
import math

import jax
import jax.numpy as jnp
from jax import lax
from jax.experimental import pallas as pl
from jax.experimental.pallas import tpu as pltpu
from jax.sharding import PartitionSpec as P

NOPE = 64
ROPE = 32
VD = 64
KR = 256
LANES = 128
GROUP_BITS = (2, 8)
LAST_BITS = (1, 2)
NEAR, FAR = 4, 8
GROUP = 4


EPS = 1e-05
RESID = 1.4 / math.sqrt(62.0)
THETA = 10000.0
NEG_FILL = -1e30


def norm_apply(values, gain):
    inverse = lax.rsqrt(jnp.mean(values * values, axis=-1, keepdims=True) + EPS)
    return values * inverse * gain


def rotate(values, positions):
    width_half = values.shape[-1] // 2
    frequency = THETA ** (-2.0 * jnp.arange(width_half, dtype=jnp.float32) / values.shape[-1])
    angles = positions.astype(jnp.float32)[:, None] * frequency[None, :]
    extra_dims = (1,) * (values.ndim - 2)
    cosine = jnp.cos(angles).reshape(angles.shape[:1] + extra_dims + angles.shape[1:])
    sine = jnp.sin(angles).reshape(angles.shape[:1] + extra_dims + angles.shape[1:])
    lower_part = values[..., :width_half]
    upper_part = values[..., width_half:]
    return jnp.concatenate(
        [lower_part * cosine - upper_part * sine, upper_part * cosine + lower_part * sine], axis=-1
    )


def rotate_back(values, positions, grads):
    _, pullback = jax.vjp(partial(rotate, positions=positions), values)
    return pullback(grads)[0]


def plain_mul(left, right):
    return jnp.dot(left, right, preferred_element_type=jnp.float32)


def mul_trans(left, right):
    return lax.dot_general(
        left, right, (((1,), (1,)), ((), ())), preferred_element_type=jnp.float32
    )


def trans_mul(left, right):
    return lax.dot_general(
        left, right, (((0,), (0,)), ((), ())), preferred_element_type=jnp.float32
    )


def low(values):
    return values.astype(jnp.bfloat16)


def wide(values):
    return values.astype(jnp.float32)


def core_swap(values):
    return lax.ppermute(values, "tensor", [(0, 1), (1, 0)])


def all_bits():
    count = lax.axis_size("dp")
    return tuple(1 << at for at in range(count.bit_length() - 1))


def other_bits(bits):
    return tuple(bit for bit in all_bits() if bit not in bits)


def masks_of(bits):
    masks = [0]
    for bit in bits:
        masks += [mask | bit for mask in masks]
    return masks


def by_count(bits):
    return sorted(masks_of(bits)[1:], key=lambda mask: bin(mask).count("1"))


def group_place():
    place = lax.axis_index("dp")
    return sum(((place // bit) % 2) << at for at, bit in enumerate(GROUP_BITS))


def tied(values, others):
    return lax.optimization_barrier((values, others))[0] if others else values


AFTER = {
    "A1": ("B0", "B1"),
    "C1": ("B0",),
    "U0": ("B2", "C0", "C1"),
    "B3": ("C0", "C1"),
    "B4": ("C2",),
    "B5": ("latents", "V1"),
    "B6": ("latents",),
    "G1": ("B5", "B6"),
    "C5": ("G1", "V2"),
    "C6": ("G1", "V2"),
    "M0": ("G2",),
    "M1": ("G2",),
    "M2": ("W1",),
    "W2": ("M1",),
    "W3": ("M1",),
    "R1": ("D1",),
    "R2": ("D2", "D1"),
    "R3": ("D2", "D1"),
    "P0": ("D2", "D1"),
    "P1": ("R0",),
    "P2": ("R1",),
    "O0": ("R1",),
    "Q0": ("P2", "R2"),
    "Q1": ("R2",),
    "T0": ("Q3",),
}


FREE = ("T1",)


class Flow:
    def __init__(self, links, name, routine):
        self.links, self.name, self.routine = links, name, routine
        self.count, self.result, self.given = 0, None, None
        self.wanted = self.resume(None)

    def resume(self, given):
        try:
            return self.routine.send(given)
        except StopIteration as end:
            self.result = end.value
            return None

    def step(self, hold=()):
        if self.wanted is None:
            return self
        name = self.name + str(self.count)
        got = self.links.send(*self.wanted, AFTER.get(name, ()), name not in FREE)
        self.links.sent[name] = self.wanted[0]
        self.links.done[name] = got
        self.count += 1
        self.wanted = self.resume(tied(got, self.links.named(hold)))
        return self

    def end(self):
        while self.wanted is not None:
            self.step()
        return self.result


class Links:
    def __init__(self):
        self.last = {}
        self.done = {}
        self.sent = {}

    def named(self, names):
        return [self.done[name] for name in names if name in self.done]

    def send(self, values, mask, after=(), in_line=True):
        masks = mask if isinstance(mask, list) else [mask]
        bits = sorted({bit for item in masks for bit in all_bits() if bit & item})
        before = self.named(after)
        if in_line:
            before += [self.last[bit] for bit in bits if bit in self.last]
        values = tied(values, before)
        count = lax.axis_size("dp")
        got = [
            lax.ppermute(item, "dp", [(place, place ^ to) for place in range(count)])
            for item, to in zip(values if mask is masks else [values], masks)
        ]
        got = got if mask is masks else got[0]
        self.last.update({bit: got for bit in bits})
        return got

    def flow(self, name, routine):
        return Flow(self, name, routine)


def routes(mask, bits, split):
    ordered = [bit for bit in bits if bit & mask]
    if len(ordered) > 1 and split == "both":
        return [(ordered[0], 0), (ordered[-1], 1)]
    return [(ordered[-1 if split == "last" else 0], None)]


def halves(values):
    half = values.shape[0] // 2
    return values[:half], values[half:]


def gather_bits(values, bits, split):
    known = {0: [values]}
    for mask in by_count(bits):
        pieces = []
        for bit, part in routes(mask, bits, split):
            source = known[mask ^ bit]
            if part is None:
                moving = source[0] if len(source) == 1 else jnp.concatenate(source)
            else:
                moving = halves(source[0])[part] if len(source) == 1 else source[part]
            pieces.append((yield moving, bit))
        known[mask] = pieces
    return known


def reduce_bits(block_of, bits, split, arrive=lambda values, bit: values):
    added = {mask: [] for mask in masks_of(bits)}

    def summed(mask, part):
        values = block_of(mask)
        if part is not None:
            values = halves(values)[part]
        if added[mask]:
            values = wide(values)
        for held, extra in added[mask]:
            if part is None or part == held:
                values = values + wide(extra)
            elif held is None:
                values = values + wide(halves(extra)[part])
        return values

    def whole(mask):
        if any(held is not None for held, _ in added[mask]):
            return [summed(mask, 0), summed(mask, 1)]
        return [summed(mask, None)]

    for mask in reversed(by_count(bits)):
        for bit, part in routes(mask, bits, split):
            if part is None:
                parts = [low(item) for item in whole(mask)]
                moving = parts[0] if len(parts) == 1 else jnp.concatenate(parts)
            else:
                moving = low(summed(mask, part))
            got = yield moving, bit
            added[mask ^ bit].append((part, arrive(got, bit)))
    parts = whole(0)
    return parts[0] if len(parts) == 1 else jnp.concatenate(parts)


def row_order():
    return [
        other | group for other in masks_of(other_bits(GROUP_BITS)) for group in masks_of(GROUP_BITS)
    ]


def first_bits():
    return other_bits(LAST_BITS)


def gather_dp(values):
    first = masks_of(first_bits())
    known = yield from gather_bits(values, first_bits(), "first")
    column = jnp.stack([known[mask][0] for mask in first])
    known = yield from gather_bits(column, LAST_BITS, "both")
    half = len(first) // 2

    def block(mask):
        at = first.index(mask & ~sum(LAST_BITS))
        pieces = known[mask & sum(LAST_BITS)]
        return pieces[0][at] if len(pieces) == 1 else pieces[at // half][at % half]

    return jnp.concatenate([block(mask) for mask in row_order()], axis=0)


def gather_dp_direct(values):
    first, last = masks_of(first_bits()), masks_of(LAST_BITS)
    got = yield [values] * (len(first) - 1), first[1:]
    column = jnp.stack([values] + got)
    got = yield [column] * (len(last) - 1), last[1:]
    known = dict(zip(last, [column] + got))
    return jnp.concatenate(
        [known[mask & sum(LAST_BITS)][first.index(mask & ~sum(LAST_BITS))] for mask in row_order()],
        axis=0,
    )


def reduce_dp_direct(grad):
    order, first, last = row_order(), masks_of(first_bits()), masks_of(LAST_BITS)
    blocks = grad.reshape(len(order), -1, grad.shape[1])
    columns = [jnp.stack([blocks[order.index(mask | item)] for item in first]) for mask in last]
    got = yield [low(column) for column in columns[1:]], last[1:]
    column = columns[0] + sum(wide(item) for item in got)
    got = yield [low(column[at]) for at in range(1, len(first))], first[1:]
    return column[0] + sum(wide(item) for item in got)


def reduce_dp(grad):
    order = row_order()
    blocks = grad.reshape(len(order), -1, grad.shape[1])
    first = masks_of(first_bits())

    def column(last):
        return jnp.stack([blocks[order.index(last | mask)] for mask in first])

    partial_sum = yield from reduce_bits(column, LAST_BITS, "both")
    return (
        yield from reduce_bits(lambda mask: partial_sum[first.index(mask)], first_bits(), "first")
    )


def place_kernel(place_ref, *refs):
    out_ref = refs[-1]
    for step, ref in enumerate(refs[:-1]):

        @pl.when(pl.program_id(0) == step)
        def _():
            out_ref[0] = ref[...]


def pick_kernel(place_ref, values_ref, *out_refs):
    for step, ref in enumerate(out_refs):

        @pl.when(pl.program_id(0) == step)
        def _():
            ref[...] = values_ref[0]


def place_index():
    return group_place().reshape(1).astype(jnp.int32)


def place_group(blocks):
    rows, width = blocks[0].shape
    return pl.pallas_call(
        place_kernel,
        grid_spec=pltpu.PrefetchScalarGridSpec(
            num_scalar_prefetch=1,
            grid=(GROUP,),
            in_specs=[pl.BlockSpec((rows, width), lambda step, place: (0, 0))] * GROUP,
            out_specs=pl.BlockSpec(
                (1, rows, width), lambda step, place: (lax.bitwise_xor(place[0], step), 0, 0)
            ),
        ),
        out_shape=jax.ShapeDtypeStruct((GROUP, rows, width), blocks[0].dtype),
        compiler_params=pltpu.CompilerParams(vmem_limit_bytes=32 * 2**20),
        name="place_group",
    )(place_index(), *blocks)


def pick_group(values):
    _, rows, width = values.shape
    blocks = pl.pallas_call(
        pick_kernel,
        grid_spec=pltpu.PrefetchScalarGridSpec(
            num_scalar_prefetch=1,
            grid=(GROUP,),
            in_specs=[
                pl.BlockSpec(
                    (1, rows, width), lambda step, place: (lax.bitwise_xor(place[0], step), 0, 0)
                )
            ],
            out_specs=[pl.BlockSpec((rows, width), lambda step, place: (0, 0))] * GROUP,
        ),
        out_shape=[jax.ShapeDtypeStruct((rows, width), values.dtype)] * GROUP,
        compiler_params=pltpu.CompilerParams(vmem_limit_bytes=32 * 2**20),
        name="pick_group",
    )(place_index(), values)
    return list(blocks)


def exchange_group(blocks, arrived):
    near, far = GROUP_BITS
    there = yield jnp.stack([blocks[1], blocks[3]]), near
    arrived.append(jnp.stack([blocks[0], there[0]]))
    across = yield blocks[2], far
    relayed = yield there[1], far
    arrived.append(jnp.stack([across, relayed]))


def cut_units(weight, share):
    rows, units = weight.shape
    cut = jnp.moveaxis(weight.reshape(rows, GROUP, units // GROUP), 1, 0)
    return jnp.pad(cut, ((0, 0), (0, 0), (0, share - units // GROUP)))


def join_units(pieces, units):
    rows = pieces.shape[1]
    return wide(jnp.moveaxis(pieces[..., : units // GROUP], 0, 1)).reshape(rows, units)


CHUNKS = 4


def reorder_kernel(steps, block, *refs):
    width = refs[0].shape[-1]
    chunk = width // CHUNKS
    for at, step in enumerate(steps):
        source, target = refs[at], refs[-1].at[at]
        if not step:
            target[...] = source[...]
            continue
        row = lax.broadcasted_iota(jnp.int32, (chunk, chunk), 0)
        column = lax.broadcasted_iota(jnp.int32, (chunk, chunk), 1)
        index = lax.rem(lax.div(column, block), GROUP)
        origin = column + (lax.bitwise_xor(index, step) - index) * block
        moved = jnp.where(row == origin, 1.0, 0.0).astype(jnp.bfloat16)
        for part in range(CHUNKS):
            columns = slice(part * chunk, (part + 1) * chunk)
            target[:, columns] = low(plain_mul(source[:, columns], moved))


def reorder(arrays, steps):
    rows, width = arrays[0].shape
    return pl.pallas_call(
        partial(reorder_kernel, tuple(steps), width // lax.axis_size("dp")),
        out_shape=jax.ShapeDtypeStruct((len(steps), rows, width), arrays[0].dtype),
        compiler_params=pltpu.CompilerParams(vmem_limit_bytes=32 * 2**20),
        name="reorder",
    )(*arrays)


def gather_tokens(values, held):
    known = yield from gather_bits(values, GROUP_BITS, "first")
    own = reorder([known[mask][0] for mask in masks_of(GROUP_BITS)], range(GROUP))
    own = tied(own.reshape(-1, values.shape[1]), held)
    return own, core_swap(own)


def gather_whole_tokens(values, to_order):
    known = yield from gather_bits(values, GROUP_BITS, "last")
    own = jnp.concatenate([known[mask][0] for mask in masks_of(GROUP_BITS)], axis=0)
    own = low(plain_mul(own, to_order))
    return own, core_swap(own)


def return_tokens(mine, others, rows):
    chip_sum = (wide(mine) + wide(others)).reshape(GROUP, rows, -1)
    masks = masks_of(GROUP_BITS)
    return reduce_bits(
        lambda mask: chip_sum[masks.index(mask)],
        GROUP_BITS,
        "first",
        lambda got, bit: reorder([got], [masks.index(bit)])[0],
    )


def bring(pieces, weight_ref, sems, column):
    copies, start = [], 0
    for at, piece in enumerate(pieces):
        rows = piece.shape[0]
        copies.append(
            pltpu.make_async_copy(
                piece.at[:, pl.ds(column, weight_ref.shape[1])],
                weight_ref.at[pl.ds(start, rows)],
                sems.at[at],
            )
        )
        start += rows
    for copy in copies:
        copy.start()
    for copy in copies:
        copy.wait()


def units_out_kernel(share, count, act_ref, *refs):
    pieces, (out_ref, weight_ref, sems) = refs[:count], refs[count:]

    @pl.when(pl.program_id(0) == 0)
    def _():
        bring(pieces, weight_ref, sems, 2 * share)

    out_ref[...] = low(mul_trans(act_ref[...], weight_ref[...]))


def units_out(act, pieces, share):
    rows, width = act.shape[0], sum(piece.shape[0] for piece in pieces)
    block = rows // 4
    return pl.pallas_call(
        partial(units_out_kernel, share, len(pieces)),
        grid=(4,),
        in_specs=[pl.BlockSpec((block, share), lambda step: (step, 0))]
        + [pl.BlockSpec(memory_space=pl.ANY)] * len(pieces),
        out_specs=pl.BlockSpec((block, width), lambda step: (step, 0)),
        out_shape=jax.ShapeDtypeStruct((rows, width), jnp.bfloat16),
        scratch_shapes=[
            pltpu.VMEM((width, share), jnp.bfloat16),
            pltpu.SemaphoreType.DMA((len(pieces),)),
        ],
        compiler_params=pltpu.CompilerParams(vmem_limit_bytes=32 * 2**20),
        name="units_out",
    )(act, *pieces)


def units_kernel(
    share, count, own_ref, other_ref, own_back_ref, other_back_ref, *refs
):
    pieces, (act_ref, d_units_ref, d_in_ref, weight_ref, sems) = refs[:count], refs[count:]
    step = pl.program_id(0)

    @pl.when(step == 0)
    def _():
        bring(pieces, weight_ref, sems, 0)

    is_own = step < pl.num_programs(0) // 2
    tokens = jnp.where(is_own, own_ref[...], other_ref[...])
    back = jnp.where(is_own, own_back_ref[...], other_back_ref[...])
    gate_cut, up_cut = slice(0, share), slice(share, 2 * share)
    down_cut = slice(2 * share, 3 * share)
    gate = plain_mul(tokens, weight_ref[:, gate_cut])
    upper = plain_mul(tokens, weight_ref[:, up_cut])
    d_act = plain_mul(back, weight_ref[:, down_cut])
    slope = 1.0 / (1.0 + jnp.exp(-gate))
    swished = gate * slope
    act = low(swished * upper)
    act_ref[...] = act
    d_units_ref[:, gate_cut] = low(d_act * upper * (slope + swished * (1.0 - slope)))
    d_units_ref[:, up_cut] = low(d_act * swished)
    d_in_ref[...] = low(mul_trans(d_units_ref[...], weight_ref[:, : 2 * share]))


def run_units(tokens, back, pieces, share):
    own, other = tokens
    rows, width = own.shape
    steps = 4
    block = 2 * rows // steps
    half = steps // 2
    in_own = pl.BlockSpec((block, width), lambda step: (jnp.minimum(step, half - 1), 0))
    in_other = pl.BlockSpec((block, width), lambda step: (jnp.maximum(step - half, 0), 0))
    many = pl.BlockSpec(memory_space=pl.ANY)

    def out_spec(columns):
        return pl.BlockSpec((block, columns), lambda step: (step, 0))

    columns = (share, 2 * share, width)
    return pl.pallas_call(
        partial(units_kernel, share, len(pieces)),
        grid=(steps,),
        in_specs=[in_own, in_other, in_own, in_other] + [many] * len(pieces),
        out_specs=[out_spec(item) for item in columns],
        out_shape=[jax.ShapeDtypeStruct((2 * rows, item), jnp.bfloat16) for item in columns],
        scratch_shapes=[
            pltpu.VMEM((width, 3 * share), jnp.bfloat16),
            pltpu.SemaphoreType.DMA((len(pieces),)),
        ],
        compiler_params=pltpu.CompilerParams(vmem_limit_bytes=56 * 2**20),
        name="run_units",
    )(own, other, *back, *pieces)


def unit_grads_kernel(share, own_ref, other_ref, own_back_ref, other_back_ref, act_ref, d_units_ref, out_ref):
    tokens = jnp.concatenate([own_ref[...], other_ref[...]], axis=0)
    out_ref[:, : 2 * share] = low(trans_mul(tokens, d_units_ref[...]))
    back = jnp.concatenate([own_back_ref[...], other_back_ref[...]], axis=0)
    out_ref[:, 2 * share :] = low(trans_mul(back, act_ref[...]))


def unit_grads(tokens, back, act, d_units, share, first, count):
    rows, width = tokens[0].shape
    chunk = width // CHUNKS
    part = pl.BlockSpec((rows, chunk), lambda step: (0, first + step))
    return pl.pallas_call(
        partial(unit_grads_kernel, share),
        grid=(count,),
        in_specs=[part] * 4
        + [pl.BlockSpec(act.shape, lambda step: (0, 0)), pl.BlockSpec(d_units.shape, lambda step: (0, 0))],
        out_specs=pl.BlockSpec((chunk, 3 * share), lambda step: (step, 0)),
        out_shape=jax.ShapeDtypeStruct((count * chunk, 3 * share), jnp.bfloat16),
        compiler_params=pltpu.CompilerParams(vmem_limit_bytes=56 * 2**20),
        name="unit_grads",
    )(*tokens, *back, act, d_units)


def pair_tokens(values):
    return jnp.concatenate([values, core_swap(values)], axis=0)


def split_pair(values):
    rows = values.shape[0] // 2
    return values[:rows] + wide(core_swap(low(values[rows:])))


def block_origins(total):
    order = row_order()
    block = total // len(order)
    place = jnp.arange(total, dtype=jnp.int32)
    index = place // block
    mask = jnp.zeros_like(index)
    for at, bit in enumerate(GROUP_BITS + other_bits(GROUP_BITS)):
        mask = mask + ((index >> at) % 2) * bit
    return (lax.axis_index("dp") ^ mask) * block + place % block


def one_hot(origins, size):
    return (jnp.arange(size, dtype=jnp.int32)[:, None] == origins[None, :]).astype(jnp.bfloat16)


def pad_heads(columns, head):
    column = jnp.arange(columns // head * LANES, dtype=jnp.int32)
    within = column % LANES
    return one_hot(jnp.where(within < head, column // LANES * head + within, -1), columns)


def in_parts(values, count):
    parts = []
    for _ in range(count):
        part = low(values)
        parts.append(part)
        values = values - wide(part)
    return parts


def move_columns(values, selector, transpose, count):
    rows = values.shape[0]
    stacked = jnp.concatenate(in_parts(values, count), axis=0)
    moved = mul_trans(stacked, selector) if transpose else plain_mul(stacked, selector)
    return sum(moved[at * rows : (at + 1) * rows] for at in range(count))


def round_up(size, step):
    return -(-size // step) * step


def turn_tables(positions):
    lane = jnp.arange(LANES, dtype=jnp.int32)[None, :]
    half = ROPE // 2
    frequency = THETA ** (-2.0 * ((lane - NOPE) % half).astype(jnp.float32) / ROPE)
    angles = positions.astype(jnp.float32)[:, None] * frequency
    in_first = (lane >= NOPE) & (lane < NOPE + half)
    in_last = (lane >= NOPE + half) & (lane < NOPE + ROPE)
    cosine, sine = jnp.cos(angles), jnp.sin(angles)
    keep = jnp.where(in_first | in_last, cosine, jnp.where(lane < NOPE, 1.0, 0.0))
    return keep, jnp.where(in_first, -sine, 0.0), jnp.where(in_last, sine, 0.0)


def lanes_on(values, step):
    return pltpu.roll(values, (-step) % LANES, 1)


def key_of(tile, k_rotary):
    lane = lax.broadcasted_iota(jnp.int32, tile.shape, 1)
    return jnp.where(lane < NOPE, tile, k_rotary)


def probs_of(query, key, visible, scale):
    scores = jnp.where(visible, mul_trans(query, key) * scale, NEG_FILL)
    exp_scores = jnp.exp(scores - jnp.max(scores, axis=-1, keepdims=True))
    return exp_scores / jnp.sum(exp_scores, axis=-1, keepdims=True)


def attend_kernel(scale, q_ref, kv_ref, rot_ref, seen_ref, keep_ref, up_ref, down_ref, out_ref, query_ref):
    visible = seen_ref[...] > 0.0
    outs = []
    for head in range(2):
        lanes = slice(head * LANES, (head + 1) * LANES)
        raw = q_ref[:, lanes]
        query = (
            raw * keep_ref[...]
            + lanes_on(raw, ROPE // 2) * up_ref[...]
            + lanes_on(raw, -(ROPE // 2)) * down_ref[...]
        ).astype(jnp.bfloat16)
        query_ref[:, lanes] = query
        tile = kv_ref[:, lanes]
        probs = probs_of(query, key_of(tile, rot_ref[...]), visible, scale)
        outs.append(plain_mul(probs.astype(jnp.bfloat16), tile))
    lane = lax.broadcasted_iota(jnp.int32, outs[0].shape, 1)
    out_ref[...] = jnp.where(lane < VD, pltpu.roll(outs[0], VD, 1), outs[1]).astype(jnp.bfloat16)


def attend_back_kernel(
    scale, query_ref, kv_ref, rot_ref, seen_ref, keep_ref, up_ref, down_ref, d_out_ref,
    d_q_ref, d_kv_ref, d_rot_ref,
):
    @pl.when(pl.program_id(0) == 0)
    def _():
        d_rot_ref[...] = jnp.zeros_like(d_rot_ref)

    visible = seen_ref[...] > 0.0
    d_pair = wide(d_out_ref[...])
    lane = lax.broadcasted_iota(jnp.int32, d_pair.shape, 1)
    d_rot = d_rot_ref[...]
    for head in range(2):
        lanes = slice(head * LANES, (head + 1) * LANES)
        query = query_ref[:, lanes]
        tile = kv_ref[:, lanes]
        key = key_of(tile, rot_ref[...])
        probs = probs_of(query, key, visible, scale)
        d_head = d_pair if head else pltpu.roll(d_pair, VD, 1)
        d_head = low(jnp.where(lane < NOPE, 0.0, d_head))
        d_probs = mul_trans(d_head, tile)
        d_values = trans_mul(low(probs), d_head)
        row_dot = jnp.sum(probs * d_probs, axis=-1, keepdims=True)
        d_scores = low(probs * (d_probs - row_dot) * scale)
        d_query = plain_mul(d_scores, key)
        d_key = trans_mul(d_scores, query)
        d_q_ref[:, lanes] = low(
            d_query * keep_ref[...]
            - lanes_on(d_query, ROPE // 2) * up_ref[...]
            - lanes_on(d_query, -(ROPE // 2)) * down_ref[...]
        )
        d_kv_ref[:, lanes] = low(jnp.where(lane < NOPE, d_key, d_values))
        d_rot += d_key
    d_rot_ref[...] = d_rot


def attend_specs(length):
    pair = pl.BlockSpec((length, 2 * LANES), lambda step: (0, step))
    single = pl.BlockSpec((length, LANES), lambda step: (0, step))
    table = pl.BlockSpec((length, LANES), lambda step: (0, 0))
    seen = pl.BlockSpec((length, length), lambda step: (0, 0))
    return pair, single, table, seen


def attend(query, key_value, rot_pad, seen, tables, scale):
    length, columns = query.shape
    pair, single, table, whole = attend_specs(length)
    return pl.pallas_call(
        partial(attend_kernel, scale),
        grid=(columns // (2 * LANES),),
        in_specs=[pair, pair, table, whole, table, table, table],
        out_specs=[single, pair],
        out_shape=[
            jax.ShapeDtypeStruct((length, columns // 2), jnp.bfloat16),
            jax.ShapeDtypeStruct((length, columns), jnp.bfloat16),
        ],
        compiler_params=pltpu.CompilerParams(vmem_limit_bytes=32 * 2**20),
        name="attend",
    )(query, key_value, rot_pad, seen, *tables)


def attend_back(query_full, key_value, rot_pad, seen, tables, d_heads, scale):
    length, columns = query_full.shape
    pair, single, table, whole = attend_specs(length)
    return pl.pallas_call(
        partial(attend_back_kernel, scale),
        grid=(columns // (2 * LANES),),
        in_specs=[pair, pair, table, whole, table, table, table, single],
        out_specs=[pair, pair, table],
        out_shape=[
            jax.ShapeDtypeStruct((length, columns), jnp.bfloat16),
            jax.ShapeDtypeStruct((length, columns), jnp.bfloat16),
            jax.ShapeDtypeStruct((length, LANES), jnp.float32),
        ],
        compiler_params=pltpu.CompilerParams(vmem_limit_bytes=32 * 2**20),
        name="attend_back",
    )(query_full, key_value, rot_pad, seen, *tables, d_heads)


def body(
    hidden_in,
    prefix_len,
    attn_gain,
    q_down,
    q_gain,
    kv_down,
    kv_gain,
    q_up,
    kv_up,
    o_proj,
    mlp_gain,
    w_gate,
    w_up,
    w_down,
    cotangent,
):
    tensor_count = lax.axis_size("tensor")
    tensor_rank = lax.axis_index("tensor")
    dp_count = lax.axis_size("dp")
    own_rows, width = hidden_in.shape
    q_rank = q_down.shape[1]
    rank = q_rank + KR
    down_rows = q_down.shape[0]
    q_share, kv_share = q_gain.shape[0], kv_gain.shape[0]
    q_rows, kv_rows = q_up.shape[0], kv_up.shape[0]
    head_qk = NOPE + ROPE
    heads_local = q_up.shape[1] // head_qk
    scale = head_qk ** (-0.5)
    links = Links()
    width_origins = block_origins(width)
    to_order = one_hot(width_origins, width)
    units = w_gate.shape[1]
    share = round_up(units // GROUP, LANES)

    down_columns = rank + ROPE
    packed_columns = round_up(down_columns + 3, LANES)

    def column_of(gain):
        return jnp.pad(gain, (0, down_rows - gain.shape[0]))[:, None]

    packed = jnp.concatenate(
        [
            q_down,
            kv_down,
            column_of(attn_gain),
            column_of(mlp_gain),
            column_of(jnp.concatenate([q_gain, kv_gain])),
            jnp.zeros((down_rows, packed_columns - down_columns - 3), jnp.bfloat16),
        ],
        axis=1,
    )
    others = other_bits(GROUP_BITS)
    near_first = (NEAR,) + tuple(bit for bit in others if bit != NEAR)
    back_flow = links.flow(
        "G",
        gather_whole_tokens(
            (RESID * cotangent.astype(jnp.float32)).astype(jnp.bfloat16), to_order
        ),
    )
    down_flow = links.flow("A", gather_dp_direct(packed)).step()
    back_flow.step()
    q_padded = low(plain_mul(q_up, pad_heads(q_up.shape[1], head_qk)))
    up_flow = links.flow("B", gather_dp(jnp.concatenate([q_padded, kv_up], axis=0))).step().step()
    down_flow.step()
    up_flow.step()
    out_flow = links.flow("C", gather_dp(o_proj.T)).step().step().step()
    core_packed = down_flow.end().reshape(dp_count, down_rows, packed_columns)
    unit_parts = []
    unit_picks = pick_group(
        jnp.concatenate(
            [
                cut_units(item, share)
                for item in tied((w_gate, w_up, w_down.T), links.named(["B0"]))
            ],
            axis=-1,
        )
    )
    exchange_flow = links.flow("U", exchange_group(unit_picks, unit_parts))
    exchange_flow.step().step().step()
    first_flow = links.flow("V", gather_bits(unit_parts[0], near_first, "first")).step()
    up_flow.step()
    up_flow.step()
    other_packed = core_swap(core_packed)
    is_first = tensor_rank == 0
    all_packed = jnp.stack(
        [
            jnp.where(is_first, core_packed, other_packed),
            jnp.where(is_first, other_packed, core_packed),
        ],
        axis=1,
    ).reshape(width, packed_columns)

    rank_block = q_rows + kv_rows
    place = jnp.arange(rank, dtype=jnp.int32)
    device_of = block_origins(rank) // rank_block
    in_block = place % rank_block
    is_query = in_block < q_rows
    rank_order = one_hot(
        jnp.where(
            is_query,
            device_of * q_rows + in_block,
            q_rank + device_of * kv_rows + in_block - q_rows,
        ),
        rank,
    )
    hidden_low, cotangent_low = tied((hidden_in, cotangent), links.named(["A0"]))
    moved_in = plain_mul(jnp.concatenate([hidden_low, cotangent_low], axis=0), to_order)
    resid_in, grad_out = moved_in[:own_rows], moved_in[own_rows:]
    device_place = width_origins // down_rows
    in_share = width_origins % down_rows
    gain_order = one_hot(
        jnp.where(
            in_share < q_share,
            device_place * q_share + in_share,
            jnp.where(
                in_share < q_share + kv_share,
                q_rank + device_place * kv_share + in_share - q_share,
                -1,
            ),
        ),
        rank,
    )
    gains = all_packed[:, down_columns : down_columns + 3].T
    gain_attn = wide(gains[0])
    gain_mlp = wide(gains[1])
    gain_rank = mul_trans(gains[2:3], gain_order)[0]
    gain_q, gain_kv = gain_rank[:q_rank], gain_rank[q_rank:]

    x_normed = norm_apply(resid_in, gain_attn).astype(jnp.bfloat16)
    latents = plain_mul(x_normed, all_packed)
    q_latent = latents[:, :q_rank]
    kv_latent = latents[:, q_rank:rank]
    rot_latent = latents[:, rank:down_columns]
    q_normed = norm_apply(q_latent, gain_q).astype(jnp.bfloat16)
    kv_normed = norm_apply(kv_latent, gain_kv).astype(jnp.bfloat16)
    own_pos = tensor_rank * own_rows + jnp.arange(own_rows, dtype=jnp.int32)
    other_pos = (1 - tensor_rank) * own_rows + jnp.arange(own_rows, dtype=jnp.int32)
    positions = jnp.concatenate([own_pos, other_pos])
    k_rotary = rotate(rot_latent, own_pos).astype(jnp.bfloat16)
    ranks_normed = low(plain_mul(jnp.concatenate([q_normed, kv_normed], axis=-1), rank_order))
    rot_pad = jnp.pad(k_rotary, ((0, 0), (NOPE, LANES - head_qk)))
    latent_seq = pair_tokens(jnp.concatenate([ranks_normed, rot_pad], axis=-1))
    links.done["latents"] = latent_seq
    first_flow.step()
    up_flow.step().step()
    up_weight = up_flow.end()
    first_flow.step()
    out_flow.step().step()
    last_flow = links.flow("W", gather_bits(unit_parts[1], near_first, "both")).step()
    back_flow.step().step()
    mlp_back = back_flow.end()
    out_flow.step().step()
    out_trans = out_flow.end()
    last_flow.step()
    rank_seq = latent_seq[:, :rank]
    rot_seq = latent_seq[:, rank:]
    zero = jnp.zeros((), jnp.bfloat16)
    q_seq = jnp.where(is_query[None, :], rank_seq, zero)
    kv_seq = jnp.where(is_query[None, :], zero, rank_seq)
    query = plain_mul(q_seq, up_weight)
    key_value = low(plain_mul(kv_seq, up_weight))
    visible = (positions[None, :] <= positions[:, None]) | (positions[None, :] < prefix_len[0])
    seen = visible.astype(jnp.float32)
    tables = turn_tables(positions)
    heads_low, query_full = attend(query, key_value, rot_seq, seen, tables, scale)
    attn_own = split_pair(mul_trans(heads_low, tied(out_trans, links.named(["G2"]))))
    mid_resid = resid_in + RESID * attn_own
    mlp_normed = norm_apply(mid_resid, gain_mlp).astype(jnp.bfloat16)

    mlp_flow = links.flow("M", gather_tokens(mlp_normed, links.named(["W0"]))).step().step()
    mlp_seq = mlp_flow.end()
    last_flow.step().step()
    first_units, last_units = first_flow.end(), last_flow.end()
    unit_pieces = [
        piece.reshape(-1, 3 * share)
        for mask in masks_of(others)
        for piece in first_units[mask] + last_units[mask]
    ]
    if any(piece.shape[0] % 16 for piece in unit_pieces):
        unit_pieces = [jnp.concatenate(unit_pieces)]
    act_low, d_units, d_mlp_terms = run_units(mlp_seq, mlp_back, unit_pieces, share)
    chip_rows = GROUP * own_rows
    d_mlp_other = core_swap(d_mlp_terms[chip_rows:])
    d_mlp_flow = links.flow("D", return_tokens(d_mlp_terms[:chip_rows], d_mlp_other, own_rows))
    d_mlp_flow.step().step().step()
    d_mlp_own = d_mlp_flow.end()
    other_masks = masks_of(others)

    def some_grads(act, first, count):
        grads = unit_grads(mlp_seq, mlp_back, act, d_units, share, first, count)
        return grads.reshape(count * len(other_masks) // CHUNKS, GROUP, -1, 3 * share)

    late_grads = some_grads(tied(act_low, [d_mlp_other]), CHUNKS // 2, CHUNKS // 2)
    early_grads = some_grads(tied(act_low, links.named(["D0"])), 0, CHUNKS // 2)

    def unit_block(mask):
        at = other_masks.index(mask)
        return early_grads[at] if at < early_grads.shape[0] else late_grads[at - early_grads.shape[0]]

    unit_flow = links.flow(
        "R", reduce_bits(unit_block, others, "both")
    )
    unit_flow.step(["D1", "D2"]).step()
    mlp_terms = units_out(tied(act_low, links.named(["D0"])), unit_pieces, share)
    mlp_flow = links.flow(
        "O",
        return_tokens(
            mlp_terms[:chip_rows],
            core_swap(mlp_terms[chip_rows:]),
            own_rows,
        ),
    )

    _, mlp_norm_back = jax.vjp(norm_apply, mid_resid, gain_mlp)
    d_mid_norm, _ = mlp_norm_back(d_mlp_own)
    mid_inverse = lax.rsqrt(jnp.mean(mid_resid * mid_resid, axis=-1, keepdims=True) + EPS)
    gain_mlp_terms = d_mlp_own * mid_resid * mid_inverse
    d_mid = grad_out + d_mid_norm
    attn_back = pair_tokens((RESID * d_mid).astype(jnp.bfloat16))
    d_heads = low(plain_mul(attn_back, out_trans))
    out_grad = trans_mul(attn_back, heads_low)
    out_flow = links.flow("P", reduce_dp(out_grad)).step().step()
    unit_flow.step().step()
    out_flow.step()
    mlp_flow.step().step(["R3"]).step(["R3"])
    d_query, d_key_value, d_rot = attend_back(
        query_full, key_value, rot_seq, seen, tables, tied(d_heads, [links.sent["R0"], out_grad]), scale
    )
    d_query, d_key_value, d_rot = tied(
        (d_query, d_key_value, d_rot), links.named(["R1"]) + [links.sent["R3"]]
    )
    d_rank = jnp.where(
        is_query[None, :], mul_trans(d_query, up_weight), mul_trans(d_key_value, up_weight)
    )
    d_latent_own = split_pair(jnp.concatenate([d_rank, d_rot], axis=-1))
    d_rank_own = move_columns(d_latent_own[:, :rank], rank_order, True, 2)
    d_q_own, d_kv_own = d_rank_own[:, :q_rank], d_rank_own[:, q_rank:]
    d_rot_own = d_latent_own[:, rank + NOPE : rank + head_qk]
    up_flow = links.flow(
        "Q",
        reduce_dp(
            trans_mul(
                jnp.concatenate([q_seq, kv_seq], axis=0),
                jnp.concatenate([d_query, d_key_value], axis=0),
            )
        ),
    )
    unit_sum = unit_flow.end()
    unit_parts = []
    exchange_flow = links.flow(
        "S", exchange_group([low(unit_sum[at]) for at in range(GROUP)], unit_parts)
    )
    exchange_flow.step().step()
    out_flow.step()
    exchange_flow.step()
    up_flow.step().step().step().step()
    out_flow.step().step()
    out_shard = out_flow.end().T

    _, q_norm_back = jax.vjp(norm_apply, q_latent, gain_q)
    d_q_latent, _ = q_norm_back(d_q_own)
    _, kv_norm_back = jax.vjp(norm_apply, kv_latent, gain_kv)
    d_kv_latent, _ = kv_norm_back(d_kv_own)
    q_inverse = lax.rsqrt(jnp.mean(q_latent * q_latent, axis=-1, keepdims=True) + EPS)
    kv_inverse = lax.rsqrt(jnp.mean(kv_latent * kv_latent, axis=-1, keepdims=True) + EPS)
    gain_rank_terms = low(
        jnp.concatenate(
            [d_q_own * q_latent * q_inverse, d_kv_own * kv_latent * kv_inverse], axis=-1
        )
    )
    d_rot_raw = rotate_back(rot_latent, own_pos, d_rot_own)
    d_latents = low(
        jnp.concatenate(
            [
                d_q_latent,
                d_kv_latent,
                d_rot_raw,
                jnp.zeros((own_rows, packed_columns - down_columns), jnp.float32),
            ],
            axis=-1,
        )
    )
    d_x_normed = mul_trans(d_latents, all_packed)
    _, x_norm_back = jax.vjp(norm_apply, resid_in, gain_attn)
    d_x_norm, _ = x_norm_back(d_x_normed)
    x_inverse = lax.rsqrt(jnp.mean(resid_in * resid_in, axis=-1, keepdims=True) + EPS)
    gain_attn_terms = d_x_normed * resid_in * x_inverse
    grad_input = move_columns(d_mid + d_x_norm, to_order, True, 3)

    kind = jnp.arange(3 * own_rows, dtype=jnp.int32)[:, None] // own_rows + down_columns
    markers = (jnp.arange(packed_columns, dtype=jnp.int32)[None, :] == kind).astype(jnp.bfloat16)
    grad_packed = trans_mul(
        jnp.concatenate(
            [
                tied(x_normed, links.named(["R3"])),
                low(gain_attn_terms),
                low(gain_mlp_terms),
                low(plain_mul(gain_rank_terms, gain_order)),
            ],
            axis=0,
        ),
        jnp.concatenate([d_latents, markers], axis=0),
    ).reshape(dp_count, tensor_count, down_rows, packed_columns)
    keep = jnp.where(is_first, grad_packed[:, 0], grad_packed[:, 1])
    give = jnp.where(is_first, grad_packed[:, 1], grad_packed[:, 0])
    keep = keep + wide(core_swap(low(give)))
    up_flow.step()
    down_flow = links.flow("T", reduce_dp_direct(keep.reshape(dp_count * down_rows, packed_columns)))
    down_flow.step()
    up_flow.step().step()
    up_shard = up_flow.end()
    packed_shard = down_flow.end()
    qup_shard = up_shard[:q_rows].reshape(q_rows, heads_local, LANES)[..., :head_qk]
    kvup_shard = up_shard[q_rows:]
    exchange_flow.end()
    unit_parts = tied(unit_parts, links.named(["Q4"]))
    unit_shards = place_group([part[at] for part in unit_parts for at in range(GROUP // 2)])
    gate_shard = join_units(unit_shards[..., :share], units)
    upper_shard = join_units(unit_shards[..., share : 2 * share], units)
    down_shard = join_units(unit_shards[..., 2 * share :], units).T
    mlp_own = mlp_flow.end()
    layer_out = low(mul_trans(low(mid_resid + RESID * mlp_own), to_order))
    gain_shards = packed_shard[:, down_columns : down_columns + 3].T

    return (
        layer_out,
        grad_input,
        gain_shards[0],
        packed_shard[:, :q_rank],
        gain_shards[2, :q_share],
        packed_shard[:, q_rank:down_columns],
        gain_shards[2, q_share : q_share + kv_share],
        qup_shard.reshape(q_up.shape),
        kvup_shard,
        out_shard,
        gain_shards[1],
        gate_shard,
        upper_shard,
        down_shard,
    )


def solution(mesh):
    return jax.shard_map(
        body,
        mesh=mesh,
        in_specs=(
            P(("dp", "tensor"), None),
            P("dp"),
            P(("dp", "tensor")),
            P(("dp", "tensor"), None),
            P(("dp", "tensor")),
            P(("dp", "tensor"), None),
            P(("dp", "tensor")),
            P("dp", "tensor"),
            P("dp", "tensor"),
            P("tensor", "dp"),
            P(("dp", "tensor")),
            P("dp", "tensor"),
            P("dp", "tensor"),
            P("tensor", "dp"),
            P(("dp", "tensor"), None),
        ),
        out_specs=(
            P(("dp", "tensor"), None),
            P(("dp", "tensor"), None),
            P(("dp", "tensor")),
            P(("dp", "tensor"), None),
            P(("dp", "tensor")),
            P(("dp", "tensor"), None),
            P(("dp", "tensor")),
            P("dp", "tensor"),
            P("dp", "tensor"),
            P("tensor", "dp"),
            P(("dp", "tensor")),
            P("dp", "tensor"),
            P("dp", "tensor"),
            P("tensor", "dp"),
        ),
        check_vma=False,
    )
```
